32 devices in a mesh: dp: 2 (over x), seq: 4 (over z), tensor: 4 (over y, core).
Axes of the slice: x: 2, y: 2, z: 4, core: 2. Of those that a mesh axis runs over, the one named last changes fastest.
Arguments:
- x_in: bfloat16 [2, 2048, 768], P('dp', 'seq'), may hold values from -6 to 6
- cotangent: bfloat16 [2, 2048, 768], P('dp', 'seq'), may hold values from -6 to 6
- segment_ids: int32 [2, 2048], P('dp'), may hold values from 0 to 31, never falling along the last dimension, each value on 1 to 1600 neighbouring positions
- random_blocks: int32 [2, 12, 32, 3], P('dp', 'tensor'), may hold values from 1 to 30, as said below
- query_key_value_weight: float32 [2, 768, 3, 768], P(None, ('dp', 'seq'), None, 'tensor'), may hold values from -0.21875 to 0.21875
- mixer_exit_projection_matrix: float32 [2, 768, 768], P(None, 'tensor', ('dp', 'seq')), may hold values from -2.5 to 2.5
- ffn_input_weight: float32 [2, 768, 3072], P(None, ('dp', 'seq'), 'tensor'), may hold values from -0.21875 to 0.21875
- perceptron_exit_matrix: float32 [2, 3072, 768], P(None, 'tensor', ('dp', 'seq')), may hold values from -0.15625 to 0.15625
- qv_bias: float32 [2, 2, 4, 192], P(None, None, 'tensor', ('dp', 'seq')), may hold values from -4 to 4
- mid_bias: float32 [2, 4, 768], P(None, 'tensor', ('dp', 'seq')), may hold values from -4 to 4
- shifts: float32 [2, 4, 768], P(None, None, ('dp', 'seq')), may hold values from -4 to 4
- gains: float32 [2, 2, 768], P(None, None, ('dp', 'seq')), may hold values from 0.5 to 1.5
Outputs:
- activations: bfloat16 [2, 2048, 768], P('dp', 'seq')
- input_grad: float32 [2, 2048, 768], P('dp', 'seq')
- derivative_joint_projection: float32 [2, 768, 3, 768], P(None, ('dp', 'seq'), None, 'tensor')
- attention_output_weight_gradient: float32 [2, 768, 768], P(None, 'tensor', ('dp', 'seq'))
- ffn_input_weight_gradient: float32 [2, 768, 3072], P(None, ('dp', 'seq'), 'tensor')
- grad_w_back: float32 [2, 3072, 768], P(None, 'tensor', ('dp', 'seq'))
- grad_qv_bias: float32 [2, 2, 4, 192], P(None, None, 'tensor', ('dp', 'seq'))
- grad_mid_bias: float32 [2, 4, 768], P(None, 'tensor', ('dp', 'seq'))
- grad_shifts: float32 [2, 4, 768], P(None, None, ('dp', 'seq'))
- grad_gains: float32 [2, 2, 768], P(None, None, ('dp', 'seq'))
The draws below stay inside these ranges and needn't reach their ends.
Inputs may be any that keep to these rules, and one draw needn't show every extreme that they name: `segment_ids`: ids never fall along a sequence, every id of the range occurs, and each sequence has one document of exactly 1600 tokens. `random_blocks`: for each sequence, head and query block the 3 blocks differ from one another, from the first and last block and from the query block and its two neighbours.
All inputs are finite; a program needn't handle non-finite values.
Results may differ from the reference program's by a relative error of at most 0.035.
Values may be sent and summed in bfloat16 or wider, within the bound.
A program may use at most 128 MiB of HBM per device.

```python
import math
import jax
import jax.numpy as jnp
import numpy as np
from jax import lax

D = 768
HEADS = 12
HD = 64
FF = 3072
BLK = 64
NRAND = 3
LAYERS = 2
LENGTH = 2048
SEQS = 2
N_TENSOR = 4


def draw_random_blocks(key, part):
    key = jax.random.fold_in(key, 11)
    block_count = LENGTH // BLK
    ranks = jax.random.randint(key, (SEQS, HEADS, block_count, block_count), 0, 1 << 20, dtype=jnp.int32)
    column = jnp.arange(block_count, dtype=jnp.int32)
    scores = ranks * block_count + column
    query_block = column[:, None]
    banned = (jnp.abs(column[None, :] - query_block) <= 1) | (column[None, :] == 0) | (column[None, :] == block_count - 1)
    scores = jnp.where(banned, jnp.int32(1 << 30), scores)
    _, chosen = lax.top_k(-scores, NRAND)
    return chosen.astype(jnp.int32)


def with_spikes(drawn, own_key, source, target, parts, factor):
    owner, partner = [(jnp.arange(drawn.shape[axis_at]) // (drawn.shape[axis_at] // parts)).reshape([-1 if axis == axis_at else 1 for axis in range(drawn.ndim)]) for axis_at in (source, target)]
    chosen = jax.random.permutation(own_key, parts)[partner]
    strong = (owner == chosen) | (owner == (partner + parts // 2) % parts)
    return jnp.where(strong, factor * drawn, drawn)


def level_of(own_key, extent, shards, low, high):
    def one(axis_at, parts):
        draws = jax.random.uniform(jax.random.fold_in(jax.random.fold_in(own_key, 6), axis_at), (parts,), jnp.float32, low / len(shards), high / len(shards))
        return jnp.repeat(jnp.exp(draws), extent[axis_at] // parts).reshape((-1,) + (1,) * (len(extent) - axis_at - 1))

    factor_of = one(*shards[0])
    for cut in shards[1:]:
        factor_of = factor_of * one(*cut)
    return factor_of


def length_profile(number_of, total, most, lean):
    portions = [(1 << 20) // math.isqrt(standing ** lean) + 1 for standing in range(2, number_of + 1)]
    surplus, counts = total - most - (number_of - 1), [1] * (number_of - 1)
    while surplus > 0:
        movable = [i for i in range(number_of - 1) if counts[i] < most]
        whole, budget = sum([portions[i] for i in movable]), surplus
        for i in movable:
            addition = min(most - counts[i], max(1, budget * portions[i] // whole), surplus)
            counts[i] = counts[i] + addition
            surplus = surplus - addition
    return np.array([most] + counts)


def uneven(key, count, total, limit, skew):
    if count == 2:
        one = jax.random.randint(key, (), max(1, total - limit), min(limit, total - 1) + 1)
        return jnp.stack([one, total - one])
    lengths = jnp.asarray(length_profile(count, total, limit, skew), jnp.int32)
    twos = (count - 1) // 2
    source_of, receiver = lengths[1:1 + 2 * twos:2], lengths[2:2 + 2 * twos:2]
    slack = jnp.minimum(source_of - 1, limit - receiver)
    shifted = jax.random.randint(jax.random.fold_in(key, 1), (twos,), 0, 1 << 20) % (slack + 1)
    lengths = lengths.at[1:1 + 2 * twos:2].set(source_of - shifted).at[2:2 + 2 * twos:2].set(receiver + shifted)
    return lengths[jax.random.permutation(jax.random.fold_in(key, 2), count)]


def bell_draw(key, shape, scale, limit, cuts=(), kind=jnp.bfloat16):
    level = level_of(key, shape, cuts, -0.22, 0.18) if cuts else 1.0
    drawn = jax.random.normal(key, shape, jnp.float32) * scale * level
    return jnp.minimum(jnp.maximum(drawn, -limit), limit).astype(kind)


def heavy_noise(stream_key, dims, width, limit, shards, heavy, kind=jnp.bfloat16):
    values = width * jax.random.normal(stream_key, dims, jnp.float32)
    if shards:
        values = values * level_of(stream_key, dims, shards, -0.22, 0.18)
    return jnp.clip(with_spikes(values, jax.random.fold_in(stream_key, 3), *heavy), -limit, limit).astype(kind)


def setup_inputs(seed: int = 0) -> dict:
    key_of = jax.random.split(jax.random.key(seed), 13)
    return {
        "x_in": bell_draw(key_of[0], (SEQS, LENGTH, D), 1.0, 6.0, ((0, 2), (1, 4))),
        "cotangent": heavy_noise(key_of[1], (SEQS, LENGTH, D), 1.0, 6.0, ((0, 2), (1, 4)), (0, 2, 2, 2.0)),
        "segment_ids": jax.vmap(lambda own: jnp.searchsorted(jnp.cumsum(uneven(own, LENGTH // BLK, LENGTH, 3 * LENGTH // 4 + BLK, 2)), jnp.arange(LENGTH), side="right"))(jax.random.split(key_of[2], SEQS)).reshape((SEQS, LENGTH)).astype(jnp.int32),
        "random_blocks": draw_random_blocks(jax.random.fold_in(key_of[12], 71), 0),
        "query_key_value_weight": bell_draw(key_of[4], (LAYERS, D, 3, D), D ** -0.5, 0.21875, ((1, 8), (3, 4)), jnp.float32),
        "mixer_exit_projection_matrix": bell_draw(key_of[5], (LAYERS, D, D), (D // 128) ** -0.5, 2.5, ((1, 4), (2, 8)), jnp.float32),
        "ffn_input_weight": bell_draw(key_of[6], (LAYERS, D, FF), D ** -0.5, 0.21875, ((1, 8), (2, 4)), jnp.float32),
        "perceptron_exit_matrix": bell_draw(key_of[7], (LAYERS, FF, D), (FF // 2) ** -0.5, 0.15625, ((1, 4), (2, 8)), jnp.float32),
        "qv_bias": bell_draw(key_of[8], (LAYERS, 2, N_TENSOR, D // N_TENSOR), 0.3, 4.0, ((2, 4), (3, 8)), jnp.float32),
        "mid_bias": bell_draw(key_of[9], (LAYERS, N_TENSOR, FF // N_TENSOR), 0.5, 4.0, ((1, 4), (2, 8)), jnp.float32),
        "shifts": bell_draw(key_of[10], (LAYERS, 4, D), 0.5, 4.0, ((2, 8),), jnp.float32),
        "gains": jnp.clip(1.0 + 0.1 * jax.random.normal(key_of[11], (LAYERS, 2, D), jnp.float32), 0.5, 1.5),
    }


@jax.custom_vjp
def low(v):
    return lax.optimization_barrier(v.astype(jnp.bfloat16)).astype(jnp.float32)

@jax.custom_vjp
def low_back(v):
    return v

def low_keep(v):
    return (low(v), None)

def low_pass(kept, grad):
    return (grad,)

def back_keep(v):
    return (v, None)

def back_low(kept, grad):
    return (low(grad),)
low.defvjp(low_keep, low_pass)
low_back.defvjp(back_keep, back_low)
norm_eps = 1e-06
highest = lax.Precision.HIGHEST

def normed(source, gain_row, shift_row):
    average = lax.optimization_barrier(jnp.mean(source, axis=-1, keepdims=True))
    centered = source - average
    spread = lax.optimization_barrier(jnp.mean(centered * centered, axis=-1, keepdims=True))
    return centered * lax.rsqrt(spread + norm_eps) * gain_row + shift_row

def position_lookup_matrix(query_block, random_rows, block_count):
    fixed_slots = jnp.stack([query_block - 1, query_block, query_block + 1, jnp.zeros_like(query_block), jnp.zeros_like(query_block) + (block_count - 1)], axis=1)
    slot_live = jnp.stack([query_block >= 1, query_block >= 0, query_block <= block_count - 2, query_block >= 2, query_block <= block_count - 3], axis=1)
    fixed_slots = jnp.clip(fixed_slots, 0, block_count - 1).astype(jnp.int32)
    out_shape = random_rows.shape[:-1] + (5,)
    slot_index = jnp.concatenate([jnp.broadcast_to(fixed_slots, out_shape), random_rows.astype(jnp.int32)], axis=-1)
    random_live = jnp.ones((slot_live.shape[0], random_rows.shape[-1]), dtype=jnp.bool_)
    return (slot_index, jnp.concatenate([slot_live, random_live], axis=1))

def attend(query_rows, key_rows, value_rows, segment, slot_index, slot_live):
    heads_all, block_count, block_len, head_dim = query_rows.shape
    flat_index = slot_index.reshape(heads_all, -1).astype(jnp.int32)
    global_index = (flat_index + (jnp.arange(heads_all, dtype=jnp.int32) * block_count)[:, None]).reshape(-1)
    picked_keys = jnp.take(key_rows.reshape(heads_all * block_count, block_len, head_dim), global_index, axis=0).reshape(heads_all, block_count, -1, head_dim)
    picked_values = jnp.take(value_rows.reshape(heads_all * block_count, block_len, head_dim), global_index, axis=0).reshape(heads_all, block_count, -1, head_dim)
    seg_blocks = segment.reshape(block_count, block_len)
    key_segments = jnp.take(seg_blocks, flat_index, axis=0).reshape(heads_all, block_count, -1)
    live_cols = jnp.repeat(slot_live, block_len, axis=1)
    allowed = live_cols[None, :, None, :] & (seg_blocks[None, :, :, None] == key_segments[:, :, None, :])
    scores = low_back(jnp.einsum('hnad,hnkd->hnak', query_rows, picked_keys, precision=highest) * head_dim ** (-0.5))
    masked = jnp.where(allowed, scores, -1e+30)
    peak = lax.optimization_barrier(jnp.max(masked, axis=-1, keepdims=True))
    expo = jnp.where(allowed, jnp.exp(masked - peak), 0.0)
    attn_probs = expo / lax.optimization_barrier(jnp.sum(expo, axis=-1, keepdims=True))
    return jnp.einsum('hnak,hnkd->hnad', low(attn_probs), picked_values, precision=highest)

def by_head(source):
    return source.reshape(LENGTH // BLK, BLK, HEADS, HD).transpose(2, 0, 1, 3)

def layer(current, params, segment, slot_index, slot_live):
    query_key_value_weight, mixer_exit_projection_matrix, ffn_input_weight, perceptron_exit_matrix, qv_bias, mid_bias, shifts, gains = params
    width_local = D // N_TENSOR
    hidden_local = FF // N_TENSOR
    reduced_hidden_input = low(current)
    qkv_parts = []
    for group in range(N_TENSOR):
        own_copy = low_back(reduced_hidden_input)
        qkv_parts.append(jnp.einsum('ld,dcw->lcw', own_copy, query_key_value_weight[:, :, group * width_local:(group + 1) * width_local], precision=highest))
    query_key_value_full = jnp.concatenate(qkv_parts, axis=2)
    bias_rows = qv_bias.reshape(2, D)
    query_rows = low_back(low(query_key_value_full[:, 0] + bias_rows[0]))
    key_rows = low_back(low(query_key_value_full[:, 1]))
    value_rows = low_back(low(query_key_value_full[:, 2] + bias_rows[1]))
    attention_result = jax.checkpoint(attend)(by_head(query_rows), by_head(key_rows), by_head(value_rows), segment, slot_index, slot_live)
    attention_result = low_back(low(attention_result.transpose(1, 2, 0, 3).reshape(LENGTH, D)))
    attended = jnp.zeros_like(current)
    for group in range(N_TENSOR):
        lower = group * width_local
        upper = lower + width_local
        attended = attended + low_back(low(jnp.dot(attention_result[:, lower:upper], mixer_exit_projection_matrix[lower:upper], precision=highest)))
    first = normed(current + attended + shifts[0], gains[0], shifts[1])
    reduced_leading = low(first)
    hidden_bias = mid_bias.reshape(FF)
    branch = jnp.zeros_like(current)
    for group in range(N_TENSOR):
        lower = group * hidden_local
        upper = lower + hidden_local
        own_copy = low_back(reduced_leading)
        pre_act = low_back(jnp.dot(own_copy, ffn_input_weight[:, lower:upper], precision=highest) + hidden_bias[lower:upper])
        gelu_hidden = low(jax.nn.gelu(pre_act, approximate=True))
        branch = branch + low_back(low(jnp.dot(gelu_hidden, perceptron_exit_matrix[lower:upper], precision=highest)))
    return normed(first + branch + shifts[2], gains[1], shifts[3])

def reference(x_in, cotangent, segment_ids, random_blocks, query_key_value_weight, mixer_exit_projection_matrix, ffn_input_weight, perceptron_exit_matrix, qv_bias, mid_bias, shifts, gains):
    masters = (query_key_value_weight, mixer_exit_projection_matrix, ffn_input_weight, perceptron_exit_matrix, qv_bias, mid_bias, shifts, gains)
    block_count = LENGTH // BLK
    query_block = jnp.arange(block_count, dtype=jnp.int32)

    def forward(params, source_rows, segment, random_rows):
        slot_index, slot_live = position_lookup_matrix(query_block, random_rows, block_count)
        rounded = jax.tree.map(low, params)
        current = source_rows
        for layer_no in range(LAYERS):
            current = layer(current, tuple((stacked[layer_no] for stacked in rounded)), segment, slot_index, slot_live)
        return current

    def per_sequence(totals, inputs):
        source_rows, seq_cot, segment, random_rows = inputs

        def wrapped(params, begin_rows):
            return forward(params, begin_rows, segment, random_rows)
        result, backward_fn = jax.vjp(wrapped, masters, source_rows)
        parameter_derivatives, begin_grad = backward_fn(seq_cot)
        return (jax.tree.map(jnp.add, totals, parameter_derivatives), (result.astype(jnp.bfloat16), begin_grad))
    zero_grads = jax.tree.map(jnp.zeros_like, masters)
    totals, outputs = lax.scan(per_sequence, zero_grads, (x_in.astype(jnp.float32), cotangent.astype(jnp.float32), segment_ids, random_blocks))
    return (outputs[0], outputs[1], totals[0], totals[1], totals[2], totals[3], totals[4], totals[5], totals[6], totals[7])
```

```python
import functools

import jax
import jax.numpy as jnp
from jax import lax
from jax.experimental import pallas as pl
from jax.experimental.pallas import tpu as pltpu
from jax.sharding import PartitionSpec as P

BLK = 64
LAYERS = 2
EPS = 1e-06
NEG = -1e30
BF = jnp.bfloat16
F32 = jnp.float32
MESH = pl.DeviceIdType.MESH


def nn(a, b):
    return lax.dot_general(a, b, (((1,), (0,)), ((), ())), preferred_element_type=F32)


def nt(a, b):
    return lax.dot_general(a, b, (((1,), (1,)), ((), ())), preferred_element_type=F32)


def tn(a, b):
    return lax.dot_general(a, b, (((0,), (0,)), ((), ())), preferred_element_type=F32)


def normalise(z):
    mu = jnp.mean(z, axis=-1, keepdims=True)
    c = z - mu
    rs = lax.rsqrt(jnp.mean(c * c, axis=-1, keepdims=True) + EPS)
    return c * rs, rs


def norm_back(dn, n, rs):
    return (dn - jnp.mean(dn, axis=-1, keepdims=True) - n * jnp.mean(dn * n, axis=-1, keepdims=True)) * rs


def low_lanes(shape):
    return lax.broadcasted_iota(jnp.int32, shape, len(shape) - 1) % 128 < 64


def body(
    direct, nz, rw,
    wl, sm, xin, cot, segk, segqm,
    act, dxo, gout, gsm,
    W, SG, SV, XA, KV, QP, OO, LSE, H1, DG, G, N1, N2, RS1, RS2, XR, DZ, EB,
    PB, rsib, ry, DXP, xsib, xy, xz, ACC, MX, LS, DKV, DU, DQ, DO, DEL, XRV, ZRV, SL, St1, St2, Sz, Sx,
    wg_s, wg_r, ax_s, ax_r, a4_s, a4_r, r4_s, r4_r, r16_s, r16_r, g_s, g_r, s_s, s_r,
):
    d, z, t = lax.axis_index("dp"), lax.axis_index("seq"), lax.axis_index("tensor")
    c = t % 2
    y = t // 2
    sib, yp = 2 * y + (1 - c), 2 * (1 - y) + c
    DM = XA.shape[2]
    TL = xin.shape[0]
    QT = TL // 4
    HALF = TL // 2
    dsib, dyp = (d, z, sib), (d, z, yp)
    zk = [lax.rem(z + k, nz) for k in range(nz)]
    zm = [lax.rem(z - k + nz, nz) for k in range(nz)]
    pending = []

    bar = pltpu.get_barrier_semaphore()
    peers = [dsib, dyp] + [(d, zk[k], t) for k in range(1, nz)]
    if direct:
        dx_dev = (1 - d, z, t)
        peers.append(dx_dev)
    for p in peers:
        pl.semaphore_signal(bar, inc=1, device_id=p, device_id_type=MESH)
    pl.semaphore_wait(bar, len(peers))

    def send(src, dst, ss, rs, dev):
        cp = pltpu.make_async_remote_copy(src_ref=src, dst_ref=dst, send_sem=ss, recv_sem=rs, device_id=dev, device_id_type=MESH)
        cp.start()
        return cp

    def rows(start, n):
        return pl.ds(pl.multiple_of(start, n if n % 16 == 0 else 16), n)

    own = rows(t * QT, QT)

    wz = {}
    wx = {}
    if direct:
        slot = d * nz + z

        def w_z(p):
            if p == 6:
                SG[slot] = sm[...]
                src = sm
                dst = SG.at[slot]
            else:
                W[p, rows(slot * rw, rw), :] = wl[p]
                src = wl.at[p]
                dst = W.at[p, rows(slot * rw, rw), :]
            wz[p] = [send(src, dst, wg_s.at[p, k], wg_r.at[p, k], (d, zk[k], t)) for k in range(1, nz)]

        def w_x(p):
            for cp in wz[p]:
                cp.wait_recv()
            if p == 6:
                ref = SG.at[pl.ds(d * nz, nz)]
            else:
                ref = W.at[p, rows(d * (nz * rw), nz * rw), :]
            wx[p] = send(ref, ref, wg_s.at[p, 0], wg_r.at[p, 0], dx_dev)

        def w_fin(p):
            wx[p].wait_recv()

        def w_sent(p):
            for cp in wz[p]:
                cp.wait_send()
            wx[p].wait_send()
    else:

        def w_z(p):
            if p == 6:
                SV[...] = sm[...]
            else:
                W[p] = wl[p]

        def w_x(p):
            pass

        w_fin = w_sent = w_x

    def ag4(i, ref):
        own_rows = ref.at[own, :]
        cps = [
            send(own_rows, own_rows, a4_s.at[i, 0], a4_r.at[i, 0], dsib),
            send(own_rows, own_rows, a4_s.at[i, 1], a4_r.at[i, 1], dyp),
        ]

        def fin():
            cps[1].wait_recv()
            r = ref.at[rows(yp * QT, QT), :]
            cps.append(send(r, r, a4_s.at[i, 2], a4_r.at[i, 2], dsib))
            cps[0].wait_recv()
            cps[2].wait_recv()

        def sent():
            for cp in cps:
                cp.wait_send()

        return fin, sent

    def rs4(i, part, filler=None):
        r0 = [(1 - y) * HALF, y * HALF]
        cps = []
        for k in range(2):
            PB[rows(r0[k], HALF), :] = part(rows(r0[k], HALF)).astype(BF)
            cps.append(send(PB.at[rows(r0[k] + (1 - c) * QT, QT), :], rsib.at[k], r4_s.at[i, k], r4_r.at[i, k], dsib))
            if k == 0:
                cps[0].wait_recv()
                mine = rows(r0[0] + c * QT, QT)
                PB[mine, :] = (PB[mine, :].astype(F32) + rsib[0].astype(F32)).astype(BF)
                ycp = send(PB.at[mine, :], ry, r4_s.at[i, 2], r4_r.at[i, 2], dyp)
        if filler is not None:
            filler()
        cps[1].wait_recv()
        ycp.wait_recv()
        total = PB[own, :].astype(F32) + rsib[1].astype(F32) + ry[...].astype(F32)
        cps[0].wait_send()
        cps[1].wait_send()
        ycp.wait_send()
        return total

    def xgather(l):
        st = {}

        def src_rows(j, q):
            return XA.at[l, rows(zm[j] * TL + q * QT, QT), :]

        def start():
            r = src_rows(0, t)
            if l > 0:
                st["c", 0] = send(r, r, ax_s.at[l, nz], ax_r.at[l, nz], dsib)
                st["y", 0] = send(r, r, ax_s.at[l, 2 * nz], ax_r.at[l, 2 * nz], dyp)
            for k in range(1, nz):
                st["z", k] = send(r, r, ax_s.at[l, k], ax_r.at[l, k], (d, zk[k], t))

        def mid(j):
            st["z", j].wait_recv()
            r = src_rows(j, t)
            st["y", j] = send(r, r, ax_s.at[l, 2 * nz + j], ax_r.at[l, 2 * nz + j], dyp)
            st["c", j] = send(r, r, ax_s.at[l, nz + j], ax_r.at[l, nz + j], dsib)

        def fwd(j):
            st["y", j].wait_recv()
            r = src_rows(j, yp)
            st["c2", j] = send(r, r, ax_s.at[l, 3 * nz + j], ax_r.at[l, 3 * nz + j], dsib)

        def fin(j):
            st["c", j].wait_recv()
            st["c2", j].wait_recv()

        def sent():
            for cp in st.values():
                cp.wait_send()

        return start, mid, fwd, fin, sent

    def small(l, r):
        return SV[l, r : r + 1, :]

    def kv_proj(l, j):
        r = rows(zm[j] * TL, TL)
        bias = SV[l, 8:9, 0:384]
        KV[l, r, :] = (nn(XA[l, r, :], W[3 * l, :, 0:384]) + bias).astype(BF)

    def q_proj(l):
        bias = SV[l, 7:8, 0:256]
        q = (nn(XA[l, rows(z * TL, TL), :], W[3 * l, :, 384:640]) + bias).astype(BF).astype(F32) * 0.125
        a, b = q[:, 0:128], q[:, 128:256]
        lo = low_lanes(a.shape)
        QP[l, :, 0:128] = jnp.where(lo, a, 0.0).astype(BF)
        QP[l, :, 128:256] = jnp.where(lo, 0.0, a).astype(BF)
        QP[l, :, 256:384] = jnp.where(lo, b, 0.0).astype(BF)

    nb = TL // BLK

    def masked_scores(l, h, hl, r, j):
        kv = KV[l, r, pl.ds(hl, 128)]
        s = nt(kv, QP[l, :, pl.ds(hl, 128)])
        sq = segqm[h, pl.ds(pl.multiple_of(zm[j] * nb, nb), nb), :]
        sk = segk[r, :]
        parts = []
        for b in range(nb):
            skb = jnp.concatenate([sk[b * BLK : (b + 1) * BLK]] * (TL // 128), axis=1)
            parts.append(jnp.where(skb == sq[b : b + 1], s[b * BLK : (b + 1) * BLK], NEG))
        return kv, jnp.concatenate(parts, axis=0)

    def attend(l, j):
        r = rows(zm[j] * TL, TL)

        def head(h, carry):
            hl = pl.multiple_of(h * 128, 128)
            kv, s = masked_scores(l, h, hl, r, j)
            top = jnp.max(s, axis=0, keepdims=True)
            if j > 0:
                before = MX[h]
                top = jnp.maximum(before, top)
            e = jnp.exp(s - top)
            total = jnp.sum(e, axis=0, keepdims=True)
            o = tn(kv, e.astype(BF))
            if j > 0:
                a = jnp.exp(before - top)
                total = total + LS[h] * a
                o = o + ACC[h] * a
            MX[h] = top
            LS[h] = total
            ACC[h] = o
            return carry

        lax.fori_loop(0, 3, head, 0)

    def attend_end(l):
        o = []
        for h in range(3):
            LSE[3 * l + h] = MX[h] + jnp.log(LS[h])
            o.append((ACC[h] / LS[h]).T)
        lo = low_lanes(o[0].shape)
        OO[l, :, 0:128] = jnp.where(lo, 0.0, o[2]).astype(BF)
        OO[l, :, 128:256] = jnp.where(lo, o[1], o[0]).astype(BF)

    def gelu_parts(u):
        k = 0.7978845608028654
        th = jnp.tanh(k * (u + 0.044715 * u * u * u))
        g = 0.5 * u * (1.0 + th)
        dg = 0.5 * (1.0 + th) + 0.5 * u * (1.0 - th * th) * (k * (1.0 + 3 * 0.044715 * u * u))
        return g, dg

    def forward(l, bg):
        start, mid, fwd, fin, sent = xg[l]
        if l > 0:
            start()
            mid(1)
            fwd(0)
            fin(0)
        q_proj(l)
        kv_proj(l, 0)
        if l > 0:
            mid(2)
        attend(l, 0)
        bg[0]()
        if l > 0:
            mid(3)
            fwd(1)
        for j in range(1, nz):
            fin(j)
            kv_proj(l, j)
            if j + 1 < nz:
                if l > 0:
                    fwd(j + 1)
            attend(l, j)
            if j == nz - 2:
                bg[1]()
        attend_end(l)
        sent()
        wo = W[3 * l, :, 512:768]
        r = rs4(3 * l, lambda rr: nt(OO[l, rr, :], wo))
        z1 = XR[...] + r + small(l, 0)
        n1, rs1 = normalise(z1)
        N1[l] = n1
        RS1[l] = rs1
        h1 = n1 * small(l, 4) + small(l, 1)
        H1[l, own, :] = h1.astype(BF)
        XR[...] = h1
        done, gone = ag4(4 * l, H1.at[l])
        bg[2]()
        done()
        w_fin(3 * l + 1)
        w_fin(3 * l + 2)

        def ffn(rr):
            u = nn(H1[l, rr, :], W[3 * l + 1]) + small(l, 6)
            g, dg = gelu_parts(u)
            DG[l, rr, :] = dg.astype(BF)
            gb = g.astype(BF)
            G[l, rr, :] = gb
            return nt(gb, W[3 * l + 2])

        r = rs4(3 * l + 1, ffn, gone)
        bg[3]()
        z2 = XR[...] + r + small(l, 2)
        n2, rs2 = normalise(z2)
        N2[l] = n2
        RS2[l] = rs2
        out = n2 * small(l, 5) + small(l, 3)
        XR[...] = out
        return out.astype(BF)

    gx = {}
    gz = {}

    if direct:

        def g_start(p):
            ref = W.at[p, rows((1 - d) * (nz * rw), nz * rw), :]
            gx[p] = send(ref, XRV.at[p], g_s.at[p, 0], g_r.at[p, 0], dx_dev)

        def g_mid(p):
            gx[p].wait_recv()
            r = rows(d * (nz * rw), nz * rw)
            W[p, r, :] = (W[p, r, :].astype(F32) + XRV[p].astype(F32)).astype(BF)
            gz[p] = [
                send(W.at[p, rows((d * nz + zk[k]) * rw, rw), :], ZRV.at[p, k - 1], g_s.at[p, k], g_r.at[p, k], (d, zk[k], t))
                for k in range(1, nz)
            ]

        def g_fin(p):
            for cp in gz[p]:
                cp.wait_recv()
            tot = W[p, rows((d * nz + z) * rw, rw), :].astype(F32)
            for k in range(nz - 1):
                tot = tot + ZRV[p, k].astype(F32)
            gout[p] = tot
            pending.append(gx[p])
            pending.extend(gz[p])
    else:

        def g_start(p):
            gout[p] = W[p]

        def g_mid(p):
            pass

        g_fin = g_mid

    def backward(l, bg):
        dy = DZ[...]
        n2 = N2[l]
        SL[l, 3:4, :] = jnp.sum(dy, axis=0, keepdims=True)
        SL[l, 5:6, :] = jnp.sum(dy * n2, axis=0, keepdims=True)
        dz2 = norm_back(dy * small(l, 5), n2, RS2[l])
        SL[l, 2:3, :] = jnp.sum(dz2, axis=0, keepdims=True)
        DZ[...] = dz2
        EB[2 * l + 1, own, :] = dz2.astype(BF)
        done, gone = ag4(4 * l + 2, EB.at[2 * l + 1])
        bg[0]()
        done()

        def ffn_back(rr):
            dgm = nn(EB[2 * l + 1, rr, :], W[3 * l + 2])
            du = (dgm * DG[l, rr, :].astype(F32)).astype(BF)
            DU[rr, :] = du
            return nt(du, W[3 * l + 1])

        def fill():
            gone()
            w_sent(3 * l + 2)
            w_sent(3 * l + 1)
            W[3 * l + 2] = tn(EB[2 * l + 1], G[l]).astype(BF)
            g_start(3 * l + 2)
            W[3 * l + 1] = tn(H1[l], DU[...]).astype(BF)
            g_start(3 * l + 1)
            SL[l, 6:7, :] = jnp.sum(DU[...].astype(F32), axis=0, keepdims=True)

        r = rs4(3 * l + 2, ffn_back, fill)
        dh1 = DZ[...] + r
        n1 = N1[l]
        SL[l, 1:2, :] = jnp.sum(dh1, axis=0, keepdims=True)
        SL[l, 4:5, :] = jnp.sum(dh1 * n1, axis=0, keepdims=True)
        dz1 = norm_back(dh1 * small(l, 4), n1, RS1[l])
        SL[l, 0:1, :] = jnp.sum(dz1, axis=0, keepdims=True)
        DZ[...] = dz1
        EB[2 * l, own, :] = dz1.astype(BF)
        done, gone1 = ag4(4 * l + 3, EB.at[2 * l])
        bg[1]()
        done()
        doo = nn(EB[2 * l], W[3 * l, :, 512:768]).astype(BF).astype(F32)
        lo = low_lanes((TL, 128))
        da, db = doo[:, 0:128], doo[:, 128:256]
        DO[:, 0:128] = jnp.where(lo, 0.0, db).astype(BF)
        DO[:, 128:256] = jnp.where(lo, db, 0.0).astype(BF)
        DO[:, 256:384] = jnp.where(lo, 0.0, da).astype(BF)
        prod = (doo * OO[l].astype(F32)).T
        DEL[0] = jnp.sum(prod[192:256], axis=0, keepdims=True)
        DEL[1] = jnp.sum(prod[128:192], axis=0, keepdims=True)
        DEL[2] = jnp.sum(prod[64:128], axis=0, keepdims=True)

        xs = {}
        order = list(range(1, nz)) + [0]

        def attend_back(j, first):
            r = rows(zm[j] * TL, TL)

            def head(h, carry):
                hl = pl.multiple_of(h * 128, 128)
                kv, s = masked_scores(l, h, hl, r, j)
                q = QP[l, :, pl.ds(hl, 128)]
                do = DO[:, pl.ds(hl, 128)]
                p = jnp.exp(s - LSE[3 * l + h])
                dp = nt(kv, do)
                ds = (p * (dp - DEL[h])).astype(BF)
                DKV[r, pl.ds(hl, 128)] = (nn(ds, q) + nn(p.astype(BF), do)).astype(BF)
                dq = tn(kv, ds)
                if first:
                    ACC[h] = dq
                else:
                    ACC[h] = ACC[h] + dq
                return carry

            lax.fori_loop(0, 3, head, 0)

        def dx_parts(j):
            for k in range(2):
                r0 = [(1 - y) * HALF, y * HALF][k]
                v = nt(DKV[rows(zm[j] * TL + r0, HALF), :], W[3 * l, :, 0:384])
                if j == 0:
                    v = v + nt(DQ[rows(r0, HALF), :], W[3 * l, :, 384:640])
                DXP[j, rows(r0, HALF), :] = v.astype(BF)
                xs["c", j, k] = send(DXP.at[j, rows(r0 + (1 - c) * QT, QT), :], xsib.at[j, k], r16_s.at[l, 3 * j + k], r16_r.at[l, 3 * j + k], dsib)

        def dx_y(j):
            xs["c", j, 0].wait_recv()
            mine = rows(yp * QT, QT)
            DXP[j, mine, :] = (DXP[j, mine, :].astype(F32) + xsib[j, 0].astype(F32)).astype(BF)
            xs["y", j] = send(DXP.at[j, mine, :], xy.at[j], r16_s.at[l, 3 * j + 2], r16_r.at[l, 3 * j + 2], dyp)

        def dx_z(j):
            xs["c", j, 1].wait_recv()
            xs["y", j].wait_recv()
            tot = DXP[j, own, :].astype(F32) + xsib[j, 1].astype(F32) + xy[j].astype(F32)
            if j == 0:
                return tot
            DXP[j, own, :] = tot.astype(BF)
            xs["z", j] = send(DXP.at[j, own, :], xz.at[l, j - 1], r16_s.at[l, 3 * nz + j - 1], r16_r.at[l, 3 * nz + j - 1], (d, zm[j], t))

        for i, j in enumerate(order):
            attend_back(j, i == 0)
            if i >= 2:
                dx_z(order[i - 2])
            if i == 1:
                bg[2]()
            if j == 0:
                a01 = ACC[0]
                hi = lax.broadcasted_iota(jnp.int32, a01.shape, 0) < 64
                DQ[:, 0:128] = (jnp.where(hi, a01, ACC[1]).T * 0.125).astype(BF)
                DQ[:, 128:256] = (jnp.where(hi, ACC[2], 0.0).T * 0.125).astype(BF)
            dx_parts(j)
            dx_y(j)
        dx_z(order[nz - 2])
        gone1()
        w_sent(3 * l)
        xown = XA[l, rows(z * TL, TL), :]
        gq = tn(xown, DQ[...])
        go = tn(EB[2 * l], OO[l])
        gkv = tn(XA[l], DKV[...])
        mine_total = dx_z(0)
        W[3 * l, :, 0:384] = gkv.astype(BF)
        W[3 * l, :, 384:512] = gq[:, 0:128].astype(BF)
        W[3 * l, :, 512:640] = (gq[:, 128:256] + go[:, 0:128]).astype(BF)
        W[3 * l, :, 640:768] = go[:, 128:256].astype(BF)
        g_start(3 * l)
        SL[l, 7:8, 0:384] = jnp.sum(DKV[...].astype(F32), axis=0, keepdims=True)
        SL[l, 7:8, 384:640] = jnp.sum(DQ[...].astype(F32), axis=0, keepdims=True)
        SL[l, 7:8, 640:768] = jnp.zeros((1, 128), F32)
        tot = DZ[...] + mine_total
        for j in range(1, nz):
            xs["z", j].wait_recv()
            tot = tot + xz[l, j - 1].astype(F32)
        DZ[...] = tot
        for cp in xs.values():
            cp.wait_send()
        return tot

    xg = [xgather(0), xgather(1)]
    XA[0, rows(z * TL, TL), :] = xin[...]
    XR[...] = xin[own, :].astype(F32)
    w_z(6)
    xg[0][0]()
    w_z(0)
    for j in range(1, nz):
        xg[0][1](j)
    w_x(6)
    w_x(0)
    w_z(1)
    for j in range(1, nz):
        xg[0][2](j)
    w_fin(6)
    if direct:
        wide = DM - 128
        nslot = SG.shape[0]
        for l in range(LAYERS):
            acc = jnp.zeros((16, DM), F32)
            cmp_ = jnp.zeros((8, DM), F32)
            for s_ in range(nslot):
                piece = jnp.concatenate([SG[s_, l], jnp.zeros((16, wide), F32)], axis=1)
                acc = acc + (pltpu.roll(piece, s_ * rw, 1) if s_ else piece)
                cmp_ = cmp_ + (pltpu.roll(piece[8:16], s_ * (rw // 4), 1) if s_ else piece[8:16])
            bq, bv = cmp_[0:1], cmp_[1:2]
            lane = lax.broadcasted_iota(jnp.int32, (1, DM), 1)
            kvb = jnp.where((lane >= 64) & (lane < 192), pltpu.roll(bv, 64, 1), 0.0) + jnp.where(
                (lane >= 320) & (lane < 384), pltpu.roll(bv, 192, 1), 0.0
            )
            SV[l, 0:8, :] = acc[0:8]
            SV[l, 7:8, :] = bq
            SV[l, 8:9, :] = kvb
    w_fin(0)

    def after_first():
        w_x(1)
        w_z(2)

    def b2():
        w_x(2)
        w_z(3)

    def b3():
        pass

    def b4():
        w_x(3)
        w_z(4)

    x1 = forward(0, [after_first, b2, b3, b4])
    XA[1, rows(z * TL + t * QT, QT), :] = x1
    w_fin(3)

    def c1():
        w_x(4)
        w_z(5)

    def c2():
        w_x(5)

    nop = lambda: None
    x2 = forward(1, [c1, c2, nop, nop])
    EB[0, own, :] = x2
    act_done, act_sent = ag4(1, EB.at[0])
    DZ[...] = cot[own, :].astype(F32)

    def act_end():
        act_done()
        act[...] = EB[0]
        act_sent()

    def m5():
        g_mid(5)

    def m4():
        g_mid(4)

    backward(1, [act_end, m5, m4])

    def m3():
        g_mid(3)
        g_fin(5)

    def m2():
        g_mid(2)
        g_fin(4)

    def m1():
        g_mid(1)
        g_fin(3)

    dx = backward(0, [m3, m2, m1])
    EB[3, own, :] = dx.astype(BF)
    dx_done, dx_sent = ag4(5, EB.at[3])

    cps = [send(SL, St1, s_s.at[0], s_r.at[0], dsib)]
    cps[0].wait_recv()
    cps[0].wait_send()
    keep = lax.broadcasted_iota(jnp.int32, SL.shape, 1) < 6
    SL[...] = SL[...] + jnp.where(keep, St1[...], 0.0)
    cps.append(send(SL, St2, s_s.at[1], s_r.at[1], dyp))
    cps[1].wait_recv()
    cps[1].wait_send()
    SL[...] = SL[...] + jnp.where(keep, St2[...], 0.0)
    zc = [send(SL, Sz.at[k - 1], s_s.at[1 + k], s_r.at[1 + k], (d, zk[k], t)) for k in range(1, nz)]
    for cp in zc:
        cp.wait_recv()
    for cp in zc:
        cp.wait_send()
    tot = SL[...]
    for k in range(nz - 1):
        tot = tot + Sz[k]
    g_mid(0)
    if direct:
        SL[...] = tot
        xc = send(SL, Sx, s_s.at[1 + nz], s_r.at[1 + nz], dx_dev)
        xc.wait_recv()
        xc.wait_send()
        tot = tot + Sx[...]
    gsm[...] = tot
    g_fin(2)
    g_fin(1)
    dx_done()
    dxo[...] = EB[3]
    dx_sent()
    g_fin(0)
    w_sent(6)
    for cp in pending:
        cp.wait_send()


def shards(dp, nz, nt_, x_in, cotangent, segment_ids, random_blocks, wqkv, wo, w1, w2, qv_bias, mid_bias, shifts, gains):
    rw = wqkv.shape[1]
    direct = dp == 2 and rw % 16 == 0
    TL, DM = x_in.shape[1], x_in.shape[2]
    length = segment_ids.shape[1]
    z = lax.axis_index("seq")
    slot = lax.axis_index("dp") * nz + z
    axes = ("dp", "seq")

    qw, kw, vw = [wqkv[:, :, i, :].reshape(LAYERS, rw, 3, 64) for i in range(3)]
    ot = wo.transpose(0, 2, 1).reshape(LAYERS, rw, 3, 64)
    attn = jnp.concatenate(
        [kw[:, :, 0], vw[:, :, 0], vw[:, :, 1], kw[:, :, 1], kw[:, :, 2], vw[:, :, 2],
         qw[:, :, 0], qw[:, :, 1], qw[:, :, 2], ot[:, :, 2], ot[:, :, 1], ot[:, :, 0]], axis=2)
    wl = jnp.stack([attn, w1, w2.transpose(0, 2, 1)], axis=1).astype(BF).reshape(3 * LAYERS, rw, DM)

    def low(v):
        return v.astype(BF).astype(F32)

    if direct:
        def lanes(v):
            return jnp.pad(low(v), ((0, 0), (0, 0), (0, 128 - v.shape[2])))
        sm = jnp.concatenate(
            [lanes(shifts), lanes(gains), lanes(mid_bias), jnp.zeros((LAYERS, 1, 128), F32), lanes(qv_bias[:, :, 0]),
             jnp.zeros((LAYERS, 6, 128), F32)], axis=1)
    else:
        wl = lax.all_gather(wl, axes, axis=1, tiled=True)
        sh = lax.all_gather(shifts.astype(BF), axes, axis=2, tiled=True).astype(F32)
        ga = lax.all_gather(gains.astype(BF), axes, axis=2, tiled=True).astype(F32)
        mb = lax.all_gather(mid_bias.astype(BF), axes, axis=2, tiled=True).astype(F32)
        qv = lax.all_gather(qv_bias[:, :, 0].astype(BF), axes, axis=2, tiled=True).astype(F32)
        bq, bv = qv[:, 0:1], qv[:, 1:2]
        gap = jnp.zeros((LAYERS, 1, 64), F32)
        kvb = jnp.concatenate([gap, bv[..., 0:128], gap, gap, bv[..., 128:192]], axis=2)
        fit = lambda v: jnp.pad(v, ((0, 0), (0, 0), (0, DM - v.shape[2])))
        sm = jnp.concatenate([sh, ga, mb, fit(bq), fit(kvb), jnp.zeros((LAYERS, 7, DM), F32)], axis=1)

    nblk = length // BLK
    nb = TL // BLK
    seg = segment_ids[0]
    segk = jnp.broadcast_to(seg[:, None], (length, 128))
    rnd = lax.dynamic_slice_in_dim(random_blocks[0], z * nb, nb, axis=1)
    qi = (z * nb + jnp.arange(nb, dtype=jnp.int32))[None, :, None]
    kj = jnp.arange(nblk, dtype=jnp.int32)[None, None, :]
    ok = (jnp.abs(qi - kj) <= 1) | (kj == 0) | (kj == nblk - 1)
    ok = ok | jnp.any(rnd[:, :, :, None] == kj[:, :, None, :], axis=2)
    segq = lax.dynamic_slice_in_dim(seg, z * TL, TL)
    heads = rnd.shape[0]
    segqm = jnp.where(ok.transpose(0, 2, 1)[:, :, :, None], segq.reshape(1, 1, nb, BLK), -1).reshape(heads, nblk, TL)

    QT = TL // 4
    L = LAYERS
    nslot = dp * nz if direct else 1
    grw = rw if direct else DM
    vm = pl.BlockSpec(memory_space=pltpu.VMEM)
    dma = pltpu.SemaphoreType.DMA
    xr = nz * rw if direct else 16
    scratch = [
        pltpu.VMEM((3 * L, DM, DM), BF),
        pltpu.VMEM((nslot, L, 16, 128), F32),
        pltpu.VMEM((L, 16, DM), F32),
        pltpu.VMEM((L, length, DM), BF),
        pltpu.VMEM((L, length, 384), BF),
        pltpu.VMEM((L, TL, 384), BF),
        pltpu.VMEM((L, TL, 256), BF),
        pltpu.VMEM((3 * L, 1, TL), F32),
        pltpu.VMEM((L, TL, DM), BF),
        pltpu.VMEM((L, TL, DM), BF),
        pltpu.VMEM((L, TL, DM), BF),
        pltpu.VMEM((L, QT, DM), F32),
        pltpu.VMEM((L, QT, DM), F32),
        pltpu.VMEM((L, QT, 1), F32),
        pltpu.VMEM((L, QT, 1), F32),
        pltpu.VMEM((QT, DM), F32),
        pltpu.VMEM((QT, DM), F32),
        pltpu.VMEM((2 * L, TL, DM), BF),
        pltpu.VMEM((TL, DM), BF),
        pltpu.VMEM((2, QT, DM), BF),
        pltpu.VMEM((QT, DM), BF),
        pltpu.VMEM((nz, TL, DM), BF),
        pltpu.VMEM((nz, 2, QT, DM), BF),
        pltpu.VMEM((nz, QT, DM), BF),
        pltpu.VMEM((L, nz - 1, QT, DM), BF),
        pltpu.VMEM((3, 128, TL), F32),
        pltpu.VMEM((3, 1, TL), F32),
        pltpu.VMEM((3, 1, TL), F32),
        pltpu.VMEM((length, 384), BF),
        pltpu.VMEM((TL, DM), BF),
        pltpu.VMEM((TL, 256), BF),
        pltpu.VMEM((TL, 384), BF),
        pltpu.VMEM((3, 1, TL), F32),
        pltpu.VMEM((3 * L, xr, DM) if direct else (1, 16, 128), BF),
        pltpu.VMEM((3 * L, nz - 1, rw, DM) if direct else (1, 1, 16, 128), BF),
        pltpu.VMEM((L, 8, DM), F32),
        pltpu.VMEM((L, 8, DM), F32),
        pltpu.VMEM((L, 8, DM), F32),
        pltpu.VMEM((nz - 1, L, 8, DM), F32),
        pltpu.VMEM((L, 8, DM), F32),
        dma((7, nz)), dma((7, nz)),
        dma((L, 4 * nz)), dma((L, 4 * nz)),
        dma((8, 3)), dma((8, 3)),
        dma((6, 3)), dma((6, 3)),
        dma((L, 4 * nz)), dma((L, 4 * nz)),
        dma((6, nz)), dma((6, nz)),
        dma((2 + nz,)), dma((2 + nz,)),
    ]
    act, dx, gout, gsm = pl.pallas_call(
        functools.partial(body, direct, nz, rw),
        out_shape=(
            jax.ShapeDtypeStruct((TL, DM), BF),
            jax.ShapeDtypeStruct((TL, DM), BF),
            jax.ShapeDtypeStruct((3 * L, grw, DM), F32 if direct else BF),
            jax.ShapeDtypeStruct((L, 8, DM), F32),
        ),
        in_specs=[vm] * 6,
        out_specs=(vm,) * 4,
        scratch_shapes=scratch,
        compiler_params=pltpu.CompilerParams(collective_id=0, has_side_effects=True, vmem_limit_bytes=60 * 2**20),
        name="encoder",
    )(wl, sm, x_in[0], cotangent[0], segk, segqm)

    if not direct:
        gout = lax.psum_scatter(gout.astype(F32), axes, scatter_dimension=1, tiled=True)
        gsm = lax.psum(gsm, "dp")
    gout = gout.reshape(L, 3, rw, DM)
    ga, g1, g2 = gout[:, 0], gout[:, 1], gout[:, 2]
    pc = [ga[:, :, i * 64 : (i + 1) * 64] for i in range(12)]
    gq = jnp.concatenate([pc[6], pc[7], pc[8]], axis=2)
    gk = jnp.concatenate([pc[0], pc[3], pc[4]], axis=2)
    gv = jnp.concatenate([pc[1], pc[2], pc[5]], axis=2)
    go = jnp.concatenate([pc[11], pc[10], pc[9]], axis=2).transpose(0, 2, 1)
    sl = lax.dynamic_slice_in_dim(gsm[:, 0:7], slot * rw, rw, axis=2)
    dbq = gsm[:, 7, 384:576]
    dbv = jnp.concatenate([gsm[:, 7, 64:192], gsm[:, 7, 320:384]], axis=1)
    qv = lax.dynamic_slice_in_dim(jnp.stack([dbq, dbv], axis=1), slot * (rw // 4), rw // 4, axis=2)
    return (
        act[None],
        dx[None].astype(F32),
        jnp.stack([gq, gk, gv], axis=2),
        go,
        g1,
        g2.transpose(0, 2, 1),
        qv[:, :, None, :],
        sl[:, 6:7],
        sl[:, 0:4],
        sl[:, 4:6],
    )


def solution(mesh):
    both = ("dp", "seq")
    weights = (
        P(None, both, None, "tensor"),
        P(None, "tensor", both),
        P(None, both, "tensor"),
        P(None, "tensor", both),
        P(None, None, "tensor", both),
        P(None, "tensor", both),
        P(None, None, both),
        P(None, None, both),
    )
    tokens = P("dp", "seq", None)
    in_specs = (tokens, tokens, P("dp", None), P("dp", "tensor", None, None)) + weights
    out_specs = (tokens, tokens) + weights
    fn = functools.partial(shards, mesh.shape["dp"], mesh.shape["seq"], mesh.shape["tensor"])
    return jax.shard_map(fn, mesh=mesh, in_specs=in_specs, out_specs=out_specs, check_vma=False)
```

```python
import functools

import jax
import jax.numpy as jnp
from jax import lax
from jax.experimental import pallas as pl
from jax.experimental.pallas import tpu as pltpu
from jax.sharding import PartitionSpec as P

BLK = 64
LAYERS = 2
EPS = 1e-06
NEG = -1e30
BF = jnp.bfloat16
F32 = jnp.float32
MESH = pl.DeviceIdType.MESH


def nn(a, b):
    return lax.dot_general(a, b, (((1,), (0,)), ((), ())), preferred_element_type=F32)


def nt(a, b):
    return lax.dot_general(a, b, (((1,), (1,)), ((), ())), preferred_element_type=F32)


def tn(a, b):
    return lax.dot_general(a, b, (((0,), (0,)), ((), ())), preferred_element_type=F32)


def normalise(z):
    mu = jnp.mean(z, axis=-1, keepdims=True)
    c = z - mu
    rs = lax.rsqrt(jnp.mean(c * c, axis=-1, keepdims=True) + EPS)
    return c * rs, rs


def norm_back(dn, n, rs):
    return (dn - jnp.mean(dn, axis=-1, keepdims=True) - n * jnp.mean(dn * n, axis=-1, keepdims=True)) * rs


def low_lanes(shape):
    return lax.broadcasted_iota(jnp.int32, shape, len(shape) - 1) % 128 < 64


def body(
    direct, nz, rw,
    wl, sm, xin, cot, segk, segqm,
    act, dxo, gout, gsm,
    W, SG, SV, XA, KV, QP, OO, LSE, H1, DG, G, N1, N2, RS1, RS2, XR, DZ, EB,
    PB, rsib, ry, DXP, xsib, xy, xz, ACC, MX, LS, DKV, DU, DQ, DO, DEL, XRV, ZRV, SL, St1, St2, Sz, Sx,
    wg_s, wg_r, ax_s, ax_r, a4_s, a4_r, r4_s, r4_r, r16_s, r16_r, g_s, g_r, s_s, s_r,
):
    d, z, t = lax.axis_index("dp"), lax.axis_index("seq"), lax.axis_index("tensor")
    c = t % 2
    y = t // 2
    sib, yp = 2 * y + (1 - c), 2 * (1 - y) + c
    DM = XA.shape[2]
    TL = xin.shape[0]
    QT = TL // 4
    HALF = TL // 2
    dsib, dyp = (d, z, sib), (d, z, yp)
    zk = [lax.rem(z + k, nz) for k in range(nz)]
    upper = z // 2
    edge = (1 - z) * (1 - upper) + (z - 2) * upper
    inner = 1 - edge
    ck = [z] + [o + upper * (nz - 1 - 2 * o) for o in (edge, 2, 3)]
    pending = []

    bar = pltpu.get_barrier_semaphore()
    peers = [dsib, dyp] + [(d, zk[k], t) for k in range(1, nz)]
    if direct:
        dx_dev = (1 - d, z, t)
        peers.append(dx_dev)
    for p in peers:
        pl.semaphore_signal(bar, inc=1, device_id=p, device_id_type=MESH)
    pl.semaphore_wait(bar, len(peers))

    def send(src, dst, ss, rs, dev):
        cp = pltpu.make_async_remote_copy(src_ref=src, dst_ref=dst, send_sem=ss, recv_sem=rs, device_id=dev, device_id_type=MESH)
        cp.start()
        return cp

    def rows(start, n):
        return pl.ds(pl.multiple_of(start, n if n % 16 == 0 else 16), n)

    own = rows(t * QT, QT)

    def copy_to(src, dst, ss, rs, dev):
        return pltpu.make_async_remote_copy(src_ref=src, dst_ref=dst, send_sem=ss, recv_sem=rs, device_id=dev, device_id_type=MESH)

    if direct:
        slot = d * nz + z

        def w_ref(p, k):
            if p == 6:
                return SG.at[d * nz + k]
            return W.at[p, rows((d * nz + k) * rw, rw), :]

        def w_own(p):
            src = sm if p == 6 else wl.at[p]
            dst = w_ref(p, z)
            out = []
            for i, step in enumerate((1, 2, -1, -2)):
                ok = z + step < nz if step > 0 else z + step >= 0
                out.append((ok, copy_to(src, dst, wg_s.at[p, i], wg_r.at[p, z], (d, z + step, t))))
            return out

        def w_over(p, k):
            return copy_to(w_ref(p, k), w_ref(p, k), wg_s.at[p, 5 + k], wg_r.at[p, nz + k], dx_dev)

        def w_hop(p):
            return copy_to(w_ref(p, ck[3]), w_ref(p, ck[3]), wg_s.at[p, 4], wg_r.at[p, ck[3]], (d, nz - 1 - ck[3], t))

        def w_wait(p, k):
            copy_to(w_ref(p, k), w_ref(p, k), wg_s.at[p, 4], wg_r.at[p, k], dx_dev).wait_recv()

        def w_a(p):
            if p == 6:
                SG[slot] = sm[...]
            else:
                W[p, rows(slot * rw, rw), :] = wl[p]
            for ok, cp in w_own(p):
                pl.when(ok)(cp.start)

        def w_o(p):
            src = sm if p == 6 else wl.at[p]
            copy_to(src, w_ref(p, z), wg_s.at[p, 5 + z], wg_r.at[p, nz + z], dx_dev).start()

        def w_b(p):
            @pl.when(inner == 1)
            def _():
                w_wait(p, ck[3])
                w_hop(p).start()

        def w_c(p):
            for k in ck[1:3]:
                w_wait(p, k)
                w_over(p, k).start()

        def w_d(p):
            @pl.when(edge == 1)
            def _():
                w_wait(p, ck[3])

            w_over(p, ck[3]).start()

        def w_fin(p):
            for k in range(nz):
                w_over(p, k).wait_recv()

        def w_sent(p):
            for ok, cp in w_own(p):
                pl.when(ok)(cp.wait_send)

            @pl.when(inner == 1)
            def _():
                w_hop(p).wait_send()

            for k in ck:
                w_over(p, k).wait_send()
    else:

        def w_a(p):
            if p == 6:
                SV[...] = sm[...]
            else:
                W[p] = wl[p]

        def w_b(p):
            pass

        w_o = w_c = w_d = w_fin = w_sent = w_b

    ST = QT // 2

    def own_part(b):
        return rows(t * QT + b * ST, ST)

    def ag4(i, ref):
        st = {}

        def put(b):
            r = ref.at[own_part(b), :]
            st["c", b] = send(r, r, a4_s.at[i, b], a4_r.at[i, b], dsib)
            st["y", b] = send(r, r, a4_s.at[i, 2 + b], a4_r.at[i, 2 + b], dyp)

        def fin():
            for b in range(2):
                st["y", b].wait_recv()
                r = ref.at[rows(yp * QT + b * ST, ST), :]
                st["o", b] = send(r, r, a4_s.at[i, 4 + b], a4_r.at[i, 4 + b], dsib)
            for b in range(2):
                st["c", b].wait_recv()
                st["o", b].wait_recv()

        def sent():
            for cp in st.values():
                cp.wait_send()

        return put, fin, sent

    def rs4(i, part, consume, filler=None):
        r0 = [(1 - y) * HALF, y * HALF]
        st = {}
        for k in range(2):
            PB[rows(r0[k], HALF), :] = part(rows(r0[k], HALF)).astype(BF)
            for b in range(2):
                st["c", k, b] = send(
                    PB.at[rows(r0[k] + (1 - c) * QT + b * ST, ST), :], rsib.at[k, b], r4_s.at[i, 2 * k + b], r4_r.at[i, 2 * k + b], dsib
                )
            if k == 0:
                for b in range(2):
                    st["c", 0, b].wait_recv()
                    mine = rows(r0[0] + c * QT + b * ST, ST)
                    PB[mine, :] = (PB[mine, :].astype(F32) + rsib[0, b].astype(F32)).astype(BF)
                    st["y", b] = send(PB.at[mine, :], ry.at[b], r4_s.at[i, 4 + b], r4_r.at[i, 4 + b], dyp)
        if filler is not None:
            filler()
        for b in range(2):
            st["c", 1, b].wait_recv()
            st["y", b].wait_recv()
            consume(b, PB[own_part(b), :].astype(F32) + rsib[1, b].astype(F32) + ry[b].astype(F32))
        for cp in st.values():
            cp.wait_send()

    def xgather(l):
        st = {}

        def src_rows(k, q):
            return XA.at[l, rows(k * TL + q * QT, QT), :]

        def along(k, to, kind):
            r = src_rows(k, t)
            return copy_to(r, r, ax_s.at[l, kind * nz + k], ax_r.at[l, k], (d, to, t))

        def hop(j):
            right = (z - ck[j] + nz) // nz
            to = z - 1 + 2 * right
            return (to >= 0) & (to < nz), along(ck[j], to, 0)

        ends = [(z < nz - 1, along(z, z + 1, 0)), (z > 0, along(z, z - 1, 1))]

        def local(j):
            r = src_rows(ck[j], t)
            st["y", j] = send(r, r, ax_s.at[l, 2 * nz + ck[j]], ax_r.at[l, nz + ck[j]], dyp)
            st["c", j] = send(r, r, ax_s.at[l, 3 * nz + ck[j]], ax_r.at[l, 2 * nz + ck[j]], dsib)

        def start():
            for ok, cp in ends:
                pl.when(ok)(cp.start)
            if l > 0:
                local(0)

        def arrive(j):
            along(ck[j], z, 0).wait_recv()
            ok, cp = hop(j)
            pl.when(ok)(cp.start)
            local(j)

        def fwd(j):
            st["y", j].wait_recv()
            r = src_rows(ck[j], yp)
            st["c2", j] = send(r, r, ax_s.at[l, 4 * nz + ck[j]], ax_r.at[l, 3 * nz + ck[j]], dsib)

        def fin(j):
            st["c", j].wait_recv()
            st["c2", j].wait_recv()

        def sent():
            for ok, cp in ends + [hop(j) for j in range(1, nz)]:
                pl.when(ok)(cp.wait_send)
            for cp in st.values():
                cp.wait_send()

        return start, arrive, fwd, fin, sent

    def small(l, r):
        return SV[l, r : r + 1, :]

    def kv_proj(l, j):
        r = rows(ck[j] * TL, TL)
        bias = SV[l, 8:9, 0:384]
        KV[l, r, :] = (nn(XA[l, r, :], W[3 * l, :, 0:384]) + bias).astype(BF)

    def q_proj(l):
        bias = SV[l, 7:8, 0:256]
        q = (nn(XA[l, rows(z * TL, TL), :], W[3 * l, :, 384:640]) + bias).astype(BF).astype(F32) * 0.125
        a, b = q[:, 0:128], q[:, 128:256]
        lo = low_lanes(a.shape)
        QP[l, :, 0:128] = jnp.where(lo, a, 0.0).astype(BF)
        QP[l, :, 128:256] = jnp.where(lo, 0.0, a).astype(BF)
        QP[l, :, 256:384] = jnp.where(lo, b, 0.0).astype(BF)

    nb = TL // BLK

    def masked_scores(l, h, hl, r, j):
        kv = KV[l, r, pl.ds(hl, 128)]
        s = nt(kv, QP[l, :, pl.ds(hl, 128)])
        sq = segqm[h, pl.ds(pl.multiple_of(ck[j] * nb, nb), nb), :]
        sk = segk[r, :]
        parts = []
        for b in range(nb):
            skb = jnp.concatenate([sk[b * BLK : (b + 1) * BLK]] * (TL // 128), axis=1)
            parts.append(jnp.where(skb == sq[b : b + 1], s[b * BLK : (b + 1) * BLK], NEG))
        return kv, jnp.concatenate(parts, axis=0)

    def attend(l, j):
        r = rows(ck[j] * TL, TL)

        def head(h, carry):
            hl = pl.multiple_of(h * 128, 128)
            kv, s = masked_scores(l, h, hl, r, j)
            top = jnp.max(s, axis=0, keepdims=True)
            if j > 0:
                before = MX[h]
                top = jnp.maximum(before, top)
            e = jnp.exp(s - top)
            total = jnp.sum(e, axis=0, keepdims=True)
            o = tn(kv, e.astype(BF))
            if j > 0:
                a = jnp.exp(before - top)
                total = total + LS[h] * a
                o = o + ACC[h] * a
            MX[h] = top
            LS[h] = total
            ACC[h] = o
            return carry

        lax.fori_loop(0, 3, head, 0)

    def attend_end(l):
        o = []
        for h in range(3):
            LSE[3 * l + h] = MX[h] + jnp.log(LS[h])
            o.append((ACC[h] / LS[h]).T)
        lo = low_lanes(o[0].shape)
        OO[l, :, 0:128] = jnp.where(lo, 0.0, o[2]).astype(BF)
        OO[l, :, 128:256] = jnp.where(lo, o[1], o[0]).astype(BF)

    def gelu_parts(u):
        k = 0.7978845608028654
        th = jnp.tanh(k * (u + 0.044715 * u * u * u))
        g = 0.5 * u * (1.0 + th)
        dg = 0.5 * (1.0 + th) + 0.5 * u * (1.0 - th * th) * (k * (1.0 + 3 * 0.044715 * u * u))
        return g, dg

    seen = []

    def forward(l, bg, then):
        start, arrive, fwd, fin, sent = xg[l]
        if l > 0:
            start()
            arrive(1)
            fwd(0)
            fin(0)
            w_fin(3)
        q_proj(l)
        kv_proj(l, 0)
        arrive(2)
        fwd(1)
        attend(l, 0)
        arrive(3)
        fwd(2)
        bg[0]()
        for j in range(1, nz):
            fin(j)
            kv_proj(l, j)
            attend(l, j)
            if j == 1:
                fwd(3)
            bg[j]()
        attend_end(l)
        sent()
        wo = W[3 * l, :, 512:768]
        put, done, gone = ag4(4 * l, H1.at[l])

        def first(b, r):
            part = pl.ds(b * ST, ST)
            z1 = XR[part, :] + r + small(l, 0)
            n1, rs1 = normalise(z1)
            N1[l, part, :] = n1
            RS1[l, part, :] = rs1
            h1 = n1 * small(l, 4) + small(l, 1)
            H1[l, own_part(b), :] = h1.astype(BF)
            XR[part, :] = h1
            put(b)

        rs4(3 * l, lambda rr: nt(OO[l, rr, :], wo), first, bg[4])
        bg[5]()
        done()
        w_fin(3 * l + 1)

        def ffn(rr):
            u = nn(H1[l, rr, :], W[3 * l + 1]) + small(l, 6)
            g, dg = gelu_parts(u)
            DG[l, rr, :] = dg.astype(BF)
            gb = g.astype(BF)
            G[l, rr, :] = gb
            if l not in seen:
                seen.append(l)
                w_fin(3 * l + 2)
            return nt(gb, W[3 * l + 2])

        def fill():
            gone()
            bg[6]()

        def second(b, r):
            part = pl.ds(b * ST, ST)
            z2 = XR[part, :] + r + small(l, 2)
            n2, rs2 = normalise(z2)
            N2[l, part, :] = n2
            RS2[l, part, :] = rs2
            out = n2 * small(l, 5) + small(l, 3)
            XR[part, :] = out
            then(b, out)

        rs4(3 * l + 1, ffn, second, fill)
        bg[7]()

    gx = {}
    gz = {}

    if direct:

        def g_start(p):
            for k in ck[::-1]:
                gx[p, len(gx)] = send(
                    W.at[p, rows(((1 - d) * nz + k) * rw, rw), :], XRV.at[p, rows(k * rw, rw), :], g_s.at[p, k], g_r.at[p, k], dx_dev
                )

        def g_mid(p):
            gz[p] = []
            for k in ck[::-1]:
                r = rows((d * nz + k) * rw, rw)
                x = XRV.at[p, rows(k * rw, rw), :]
                copy_to(x, x, g_s.at[p, k], g_r.at[p, k], dx_dev).wait_recv()
                W[p, r, :] = (W[p, r, :].astype(F32) + x[...].astype(F32)).astype(BF)
                if k is not z:
                    gz[p].append(send(W.at[p, r, :], ZRV.at[p, z], g_s.at[p, nz + k], g_r.at[p, nz + z], (d, k, t)))

        def g_fin(p):
            tot = W[p, rows((d * nz + z) * rw, rw), :].astype(F32)
            for k in ck[1:]:
                x = ZRV.at[p, k]
                copy_to(x, x, g_s.at[p, nz + k], g_r.at[p, nz + k], dx_dev).wait_recv()
                tot = tot + x[...].astype(F32)
            gout[p] = tot
            pending.extend(gz[p])
    else:

        def g_start(p):
            gout[p] = W[p]

        def g_mid(p):
            pass

        g_fin = g_mid

    def accumulate(l, row, b, v):
        v = jnp.sum(v, axis=0, keepdims=True)
        SL[l, row : row + 1, :] = v if b == 0 else SL[l, row : row + 1, :] + v

    def second_back(l):
        put, done, gone = ag4(4 * l + 2, EB.at[2 * l + 1])

        def one(b, dy):
            part = pl.ds(b * ST, ST)
            n2 = N2[l, part, :]
            accumulate(l, 3, b, dy)
            accumulate(l, 5, b, dy * n2)
            dz2 = norm_back(dy * small(l, 5), n2, RS2[l, part, :])
            accumulate(l, 2, b, dz2)
            DZ[part, :] = dz2
            EB[2 * l + 1, own_part(b), :] = dz2.astype(BF)
            put(b)

        return one, done, gone

    def backward(l, bg, done, gone, then):
        bg.get(0, nop)()
        done()

        def ffn_back(rr):
            dgm = nn(EB[2 * l + 1, rr, :], W[3 * l + 2])
            du = (dgm * DG[l, rr, :].astype(F32)).astype(BF)
            DU[rr, :] = du
            return nt(du, W[3 * l + 1])

        def fill():
            gone()
            w_sent(3 * l + 2)
            w_sent(3 * l + 1)
            W[3 * l + 2] = tn(EB[2 * l + 1], G[l]).astype(BF)
            g_start(3 * l + 2)
            W[3 * l + 1] = tn(H1[l], DU[...]).astype(BF)
            g_start(3 * l + 1)
            SL[l, 6:7, :] = jnp.sum(DU[...].astype(F32), axis=0, keepdims=True)
            bg.get(1, nop)()

        put, done1, gone1 = ag4(4 * l + 3, EB.at[2 * l])

        def first_back(b, r):
            part = pl.ds(b * ST, ST)
            dh1 = DZ[part, :] + r
            n1 = N1[l, part, :]
            dz1 = norm_back(dh1 * small(l, 4), n1, RS1[l, part, :])
            DZ[part, :] = dz1
            EB[2 * l, own_part(b), :] = dz1.astype(BF)
            put(b)
            accumulate(l, 1, b, dh1)
            accumulate(l, 4, b, dh1 * n1)
            accumulate(l, 0, b, dz1)

        rs4(3 * l + 2, ffn_back, first_back, fill)
        bg.get(2, nop)()
        done1()
        doo = nn(EB[2 * l], W[3 * l, :, 512:768]).astype(BF).astype(F32)
        lo = low_lanes((TL, 128))
        da, db = doo[:, 0:128], doo[:, 128:256]
        DO[:, 0:128] = jnp.where(lo, 0.0, db).astype(BF)
        DO[:, 128:256] = jnp.where(lo, db, 0.0).astype(BF)
        DO[:, 256:384] = jnp.where(lo, 0.0, da).astype(BF)
        prod = (doo * OO[l].astype(F32)).T
        DEL[0] = jnp.sum(prod[192:256], axis=0, keepdims=True)
        DEL[1] = jnp.sum(prod[128:192], axis=0, keepdims=True)
        DEL[2] = jnp.sum(prod[64:128], axis=0, keepdims=True)

        xs = {}
        order = list(range(nz - 1, 0, -1)) + [0]

        def attend_back(j, first):
            r = rows(ck[j] * TL, TL)

            def head(h, carry):
                hl = pl.multiple_of(h * 128, 128)
                kv, s = masked_scores(l, h, hl, r, j)
                q = QP[l, :, pl.ds(hl, 128)]
                do = DO[:, pl.ds(hl, 128)]
                p = jnp.exp(s - LSE[3 * l + h])
                dp = nt(kv, do)
                ds = (p * (dp - DEL[h])).astype(BF)
                DKV[r, pl.ds(hl, 128)] = (nn(ds, q) + nn(p.astype(BF), do)).astype(BF)
                dq = tn(kv, ds)
                if first:
                    ACC[h] = dq
                else:
                    ACC[h] = ACC[h] + dq
                return carry

            lax.fori_loop(0, 3, head, 0)

        def dx_parts(j):
            for k in range(2):
                r0 = [(1 - y) * HALF, y * HALF][k]
                v = nt(DKV[rows(ck[j] * TL + r0, HALF), :], W[3 * l, :, 0:384])
                if j == 0:
                    v = v + nt(DQ[rows(r0, HALF), :], W[3 * l, :, 384:640])
                DXP[j, rows(r0, HALF), :] = v.astype(BF)
                xs["c", j, k] = send(DXP.at[j, rows(r0 + (1 - c) * QT, QT), :], xsib.at[j, k], r16_s.at[l, 3 * j + k], r16_r.at[l, 3 * j + k], dsib)

        def dx_y(j):
            xs["c", j, 0].wait_recv()
            mine = rows(yp * QT, QT)
            DXP[j, mine, :] = (DXP[j, mine, :].astype(F32) + xsib[j, 0].astype(F32)).astype(BF)
            xs["y", j] = send(DXP.at[j, mine, :], xy.at[j], r16_s.at[l, 3 * j + 2], r16_r.at[l, 3 * j + 2], dyp)

        def dx_z(j):
            xs["c", j, 1].wait_recv()
            xs["y", j].wait_recv()
            tot = DXP[j, own, :].astype(F32) + xsib[j, 1].astype(F32) + xy[j].astype(F32)
            if j == 0:
                return tot
            DXP[j, own, :] = tot.astype(BF)
            xs["z", j] = send(DXP.at[j, own, :], xz.at[l, z], r16_s.at[l, 3 * nz + ck[j]], r16_r.at[l, 3 * nz + z], (d, ck[j], t))

        for i, j in enumerate(order):
            attend_back(j, i == 0)
            if i >= 2:
                dx_z(order[i - 2])
            if i < 2:
                bg.get(3 + i, nop)()
            if j == 0:
                a01 = ACC[0]
                hi = lax.broadcasted_iota(jnp.int32, a01.shape, 0) < 64
                DQ[:, 0:128] = (jnp.where(hi, a01, ACC[1]).T * 0.125).astype(BF)
                DQ[:, 128:256] = (jnp.where(hi, ACC[2], 0.0).T * 0.125).astype(BF)
            dx_parts(j)
            dx_y(j)
        gone1()
        w_sent(3 * l)
        xown = XA[l, rows(z * TL, TL), :]
        gq = tn(xown, DQ[...])
        go = tn(EB[2 * l], OO[l])
        gkv = tn(XA[l], DKV[...])
        SL[l, 7:8, 0:384] = jnp.sum(DKV[...].astype(F32), axis=0, keepdims=True)
        SL[l, 7:8, 384:640] = jnp.sum(DQ[...].astype(F32), axis=0, keepdims=True)
        SL[l, 7:8, 640:768] = jnp.zeros((1, 128), F32)
        W[3 * l, :, 0:384] = gkv.astype(BF)
        W[3 * l, :, 384:512] = gq[:, 0:128].astype(BF)
        W[3 * l, :, 512:640] = (gq[:, 128:256] + go[:, 0:128]).astype(BF)
        W[3 * l, :, 640:768] = go[:, 128:256].astype(BF)
        g_start(3 * l)
        dx_z(order[nz - 2])
        bg.get(5, nop)()
        tot = DZ[...] + dx_z(0)
        for k in ck[1:]:
            x = xz.at[l, k]
            copy_to(x, x, r16_s.at[l, 3 * nz + k], r16_r.at[l, 3 * nz + k], dsib).wait_recv()
            tot = tot + x[...].astype(F32)
        then(tot)
        for cp in xs.values():
            cp.wait_send()

    xg = [xgather(0), xgather(1)]

    def run(*steps):
        def go():
            for fn, *a in steps:
                fn(*a)

        return go

    nop = run()
    for p in (6, 0, 1, 2):
        w_o(p)
    w_a(6)
    w_a(0)
    XA[0, rows(z * TL, TL), :] = xin[...]
    XR[...] = xin[own, :].astype(F32)
    w_b(6)
    w_b(0)
    w_c(6)
    w_c(0)
    xg[0][0]()
    w_d(6)
    w_d(0)
    for p in (3, 4, 5):
        w_o(p)
    w_fin(6)
    if direct:
        wide = DM - 128
        nslot = SG.shape[0]
        for l in range(LAYERS):
            acc = jnp.zeros((16, DM), F32)
            cmp_ = jnp.zeros((8, DM), F32)
            for s_ in range(nslot):
                piece = jnp.concatenate([SG[s_, l], jnp.zeros((16, wide), F32)], axis=1)
                acc = acc + (pltpu.roll(piece, s_ * rw, 1) if s_ else piece)
                cmp_ = cmp_ + (pltpu.roll(piece[8:16], s_ * (rw // 4), 1) if s_ else piece[8:16])
            bq, bv = cmp_[0:1], cmp_[1:2]
            lane = lax.broadcasted_iota(jnp.int32, (1, DM), 1)
            kvb = jnp.where((lane >= 64) & (lane < 192), pltpu.roll(bv, 64, 1), 0.0) + jnp.where(
                (lane >= 320) & (lane < 384), pltpu.roll(bv, 192, 1), 0.0
            )
            SV[l, 0:8, :] = acc[0:8]
            SV[l, 7:8, :] = bq
            SV[l, 8:9, :] = kvb
    xg[0][1](1)
    w_fin(0)
    def next_input(b, v):
        XA[1, rows(z * TL + t * QT + b * ST, ST), :] = v.astype(BF)

    forward(0, [
        run((w_a, 1)),
        nop,
        run((w_b, 1)),
        run((w_a, 2), (w_c, 1)),
        run((w_d, 1), (w_b, 2)),
        run((w_c, 2), (w_d, 2), (w_a, 3)),
        run((w_b, 3), (w_c, 3)),
        run((w_d, 3), (w_a, 4)),
    ], next_input)
    start_back, done, gone = second_back(1)

    def last_output(b, v):
        start_back(b, cot[own_part(b), :].astype(F32))
        EB[0, own_part(b), :] = v.astype(BF)

    forward(1, [
        run((w_b, 4)),
        run((w_c, 4)),
        run((w_d, 4)),
        run((w_a, 5)),
        run((w_b, 5)),
        run((w_c, 5), (w_d, 5)),
        nop,
        nop,
    ], last_output)
    act_put, act_done, act_sent = ag4(1, EB.at[0])

    def act_start():
        act_put(0)
        act_put(1)

    def act_end():
        act_done()
        act[...] = EB[0]
        act_sent()

    lower = second_back(0)

    def to_lower(dy):
        for b in range(2):
            lower[0](b, dy[b * ST : (b + 1) * ST])

    backward(1, {0: run((act_start,)), 1: run((act_end,)), 3: run((g_mid, 5)), 5: run((g_mid, 4))}, done, gone, to_lower)

    keep = lax.broadcasted_iota(jnp.int32, SL.shape, 1) < 6

    def s1():
        cp = send(SL, St1, s_s.at[0], s_r.at[0], dsib)
        cp.wait_recv()
        cp.wait_send()
        SL[...] = SL[...] + jnp.where(keep, St1[...], 0.0)
        sc.append(send(SL, St2, s_s.at[1], s_r.at[1], dyp))

    sc = []
    dx_put, dx_done, dx_sent = ag4(5, EB.at[3])

    def to_output(dx):
        EB[3, own, :] = dx.astype(BF)
        dx_put(0)
        dx_put(1)

    backward(
        0, {1: run((g_mid, 3), (g_fin, 5)), 3: run((g_mid, 2), (g_fin, 4)), 5: run((s1,), (g_mid, 1), (g_fin, 3))}, lower[1], lower[2], to_output
    )

    sc[0].wait_recv()
    sc[0].wait_send()
    SL[...] = SL[...] + jnp.where(keep, St2[...], 0.0)
    zc = [send(SL, Sz.at[k - 1], s_s.at[1 + k], s_r.at[1 + k], (d, zk[k], t)) for k in range(1, nz)]
    g_mid(0)
    for cp in zc:
        cp.wait_recv()
    for cp in zc:
        cp.wait_send()
    tot = SL[...]
    for k in range(nz - 1):
        tot = tot + Sz[k]
    if direct:
        SL[...] = tot
        xc = send(SL, Sx, s_s.at[1 + nz], s_r.at[1 + nz], dx_dev)
    dx_done()
    dxo[...] = EB[3]
    dx_sent()
    g_fin(2)
    g_fin(1)
    if direct:
        xc.wait_recv()
        xc.wait_send()
        tot = tot + Sx[...]
    gsm[...] = tot
    g_fin(0)
    w_sent(6)
    for cp in pending + list(gx.values()):
        cp.wait_send()


def shards(dp, nz, nt_, x_in, cotangent, segment_ids, random_blocks, wqkv, wo, w1, w2, qv_bias, mid_bias, shifts, gains):
    rw = wqkv.shape[1]
    direct = dp == 2 and rw % 16 == 0
    TL, DM = x_in.shape[1], x_in.shape[2]
    length = segment_ids.shape[1]
    z = lax.axis_index("seq")
    slot = lax.axis_index("dp") * nz + z
    axes = ("dp", "seq")

    qw, kw, vw = [wqkv[:, :, i, :].reshape(LAYERS, rw, 3, 64) for i in range(3)]
    ot = wo.transpose(0, 2, 1).reshape(LAYERS, rw, 3, 64)
    attn = jnp.concatenate(
        [kw[:, :, 0], vw[:, :, 0], vw[:, :, 1], kw[:, :, 1], kw[:, :, 2], vw[:, :, 2],
         qw[:, :, 0], qw[:, :, 1], qw[:, :, 2], ot[:, :, 2], ot[:, :, 1], ot[:, :, 0]], axis=2)
    wl = jnp.stack([attn, w1, w2.transpose(0, 2, 1)], axis=1).astype(BF).reshape(3 * LAYERS, rw, DM)

    def low(v):
        return v.astype(BF).astype(F32)

    if direct:
        def lanes(v):
            return jnp.pad(low(v), ((0, 0), (0, 0), (0, 128 - v.shape[2])))
        sm = jnp.concatenate(
            [lanes(shifts), lanes(gains), lanes(mid_bias), jnp.zeros((LAYERS, 1, 128), F32), lanes(qv_bias[:, :, 0]),
             jnp.zeros((LAYERS, 6, 128), F32)], axis=1)
    else:
        wl = lax.all_gather(wl, axes, axis=1, tiled=True)
        sh = lax.all_gather(shifts.astype(BF), axes, axis=2, tiled=True).astype(F32)
        ga = lax.all_gather(gains.astype(BF), axes, axis=2, tiled=True).astype(F32)
        mb = lax.all_gather(mid_bias.astype(BF), axes, axis=2, tiled=True).astype(F32)
        qv = lax.all_gather(qv_bias[:, :, 0].astype(BF), axes, axis=2, tiled=True).astype(F32)
        bq, bv = qv[:, 0:1], qv[:, 1:2]
        gap = jnp.zeros((LAYERS, 1, 64), F32)
        kvb = jnp.concatenate([gap, bv[..., 0:128], gap, gap, bv[..., 128:192]], axis=2)
        fit = lambda v: jnp.pad(v, ((0, 0), (0, 0), (0, DM - v.shape[2])))
        sm = jnp.concatenate([sh, ga, mb, fit(bq), fit(kvb), jnp.zeros((LAYERS, 7, DM), F32)], axis=1)

    nblk = length // BLK
    nb = TL // BLK
    seg = segment_ids[0]
    segk = jnp.broadcast_to(seg[:, None], (length, 128))
    rnd = lax.dynamic_slice_in_dim(random_blocks[0], z * nb, nb, axis=1)
    qi = (z * nb + jnp.arange(nb, dtype=jnp.int32))[None, :, None]
    kj = jnp.arange(nblk, dtype=jnp.int32)[None, None, :]
    ok = (jnp.abs(qi - kj) <= 1) | (kj == 0) | (kj == nblk - 1)
    ok = ok | jnp.any(rnd[:, :, :, None] == kj[:, :, None, :], axis=2)
    segq = lax.dynamic_slice_in_dim(seg, z * TL, TL)
    heads = rnd.shape[0]
    segqm = jnp.where(ok.transpose(0, 2, 1)[:, :, :, None], segq.reshape(1, 1, nb, BLK), -1).reshape(heads, nblk, TL)

    QT = TL // 4
    L = LAYERS
    nslot = dp * nz if direct else 1
    grw = rw if direct else DM
    vm = pl.BlockSpec(memory_space=pltpu.VMEM)
    dma = pltpu.SemaphoreType.DMA
    xr = nz * rw if direct else 16
    scratch = [
        pltpu.VMEM((3 * L, DM, DM), BF),
        pltpu.VMEM((nslot, L, 16, 128), F32),
        pltpu.VMEM((L, 16, DM), F32),
        pltpu.VMEM((L, length, DM), BF),
        pltpu.VMEM((L, length, 384), BF),
        pltpu.VMEM((L, TL, 384), BF),
        pltpu.VMEM((L, TL, 256), BF),
        pltpu.VMEM((3 * L, 1, TL), F32),
        pltpu.VMEM((L, TL, DM), BF),
        pltpu.VMEM((L, TL, DM), BF),
        pltpu.VMEM((L, TL, DM), BF),
        pltpu.VMEM((L, QT, DM), F32),
        pltpu.VMEM((L, QT, DM), F32),
        pltpu.VMEM((L, QT, 1), F32),
        pltpu.VMEM((L, QT, 1), F32),
        pltpu.VMEM((QT, DM), F32),
        pltpu.VMEM((QT, DM), F32),
        pltpu.VMEM((2 * L, TL, DM), BF),
        pltpu.VMEM((TL, DM), BF),
        pltpu.VMEM((2, 2, QT // 2, DM), BF),
        pltpu.VMEM((2, QT // 2, DM), BF),
        pltpu.VMEM((nz, TL, DM), BF),
        pltpu.VMEM((nz, 2, QT, DM), BF),
        pltpu.VMEM((nz, QT, DM), BF),
        pltpu.VMEM((L, nz, QT, DM), BF),
        pltpu.VMEM((3, 128, TL), F32),
        pltpu.VMEM((3, 1, TL), F32),
        pltpu.VMEM((3, 1, TL), F32),
        pltpu.VMEM((length, 384), BF),
        pltpu.VMEM((TL, DM), BF),
        pltpu.VMEM((TL, 256), BF),
        pltpu.VMEM((TL, 384), BF),
        pltpu.VMEM((3, 1, TL), F32),
        pltpu.VMEM((3 * L, xr, DM) if direct else (1, 16, 128), BF),
        pltpu.VMEM((3 * L, nz, rw, DM) if direct else (1, 1, 16, 128), BF),
        pltpu.VMEM((L, 8, DM), F32),
        pltpu.VMEM((L, 8, DM), F32),
        pltpu.VMEM((L, 8, DM), F32),
        pltpu.VMEM((nz - 1, L, 8, DM), F32),
        pltpu.VMEM((L, 8, DM), F32),
        dma((7, 5 + nz)), dma((7, 2 * nz)),
        dma((L, 5 * nz)), dma((L, 4 * nz)),
        dma((8, 6)), dma((8, 6)),
        dma((6, 6)), dma((6, 6)),
        dma((L, 4 * nz)), dma((L, 4 * nz)),
        dma((6, 2 * nz)), dma((6, 2 * nz)),
        dma((2 + nz,)), dma((2 + nz,)),
    ]
    act, dx, gout, gsm = pl.pallas_call(
        functools.partial(body, direct, nz, rw),
        out_shape=(
            jax.ShapeDtypeStruct((TL, DM), BF),
            jax.ShapeDtypeStruct((TL, DM), BF),
            jax.ShapeDtypeStruct((3 * L, grw, DM), F32 if direct else BF),
            jax.ShapeDtypeStruct((L, 8, DM), F32),
        ),
        in_specs=[vm] * 6,
        out_specs=(vm,) * 4,
        scratch_shapes=scratch,
        compiler_params=pltpu.CompilerParams(collective_id=0, has_side_effects=True, vmem_limit_bytes=60 * 2**20),
        name="encoder",
    )(wl, sm, x_in[0], cotangent[0], segk, segqm)

    if not direct:
        gout = lax.psum_scatter(gout.astype(F32), axes, scatter_dimension=1, tiled=True)
        gsm = lax.psum(gsm, "dp")
    gout = gout.reshape(L, 3, rw, DM)
    ga, g1, g2 = gout[:, 0], gout[:, 1], gout[:, 2]
    pc = [ga[:, :, i * 64 : (i + 1) * 64] for i in range(12)]
    gq = jnp.concatenate([pc[6], pc[7], pc[8]], axis=2)
    gk = jnp.concatenate([pc[0], pc[3], pc[4]], axis=2)
    gv = jnp.concatenate([pc[1], pc[2], pc[5]], axis=2)
    go = jnp.concatenate([pc[11], pc[10], pc[9]], axis=2).transpose(0, 2, 1)
    sl = lax.dynamic_slice_in_dim(gsm[:, 0:7], slot * rw, rw, axis=2)
    dbq = gsm[:, 7, 384:576]
    dbv = jnp.concatenate([gsm[:, 7, 64:192], gsm[:, 7, 320:384]], axis=1)
    qv = lax.dynamic_slice_in_dim(jnp.stack([dbq, dbv], axis=1), slot * (rw // 4), rw // 4, axis=2)
    return (
        act[None],
        dx[None].astype(F32),
        jnp.stack([gq, gk, gv], axis=2),
        go,
        g1,
        g2.transpose(0, 2, 1),
        qv[:, :, None, :],
        sl[:, 6:7],
        sl[:, 0:4],
        sl[:, 4:6],
    )


def solution(mesh):
    both = ("dp", "seq")
    weights = (
        P(None, both, None, "tensor"),
        P(None, "tensor", both),
        P(None, both, "tensor"),
        P(None, "tensor", both),
        P(None, None, "tensor", both),
        P(None, "tensor", both),
        P(None, None, both),
        P(None, None, both),
    )
    tokens = P("dp", "seq", None)
    in_specs = (tokens, tokens, P("dp", None), P("dp", "tensor", None, None)) + weights
    out_specs = (tokens, tokens) + weights
    fn = functools.partial(shards, mesh.shape["dp"], mesh.shape["seq"], mesh.shape["tensor"])
    return jax.shard_map(fn, mesh=mesh, in_specs=in_specs, out_specs=out_specs, check_vma=False)
```

```python
import functools

import jax
import jax.numpy as jnp
from jax import lax
from jax.experimental import pallas as pl
from jax.experimental.pallas import tpu as pltpu
from jax.sharding import PartitionSpec as P

BLK = 64
LAYERS = 2
EPS = 1e-06
NEG = -1e30
BF = jnp.bfloat16
F32 = jnp.float32
MESH = pl.DeviceIdType.MESH


def nn(a, b):
    return lax.dot_general(a, b, (((1,), (0,)), ((), ())), preferred_element_type=F32)


def nt(a, b):
    return lax.dot_general(a, b, (((1,), (1,)), ((), ())), preferred_element_type=F32)


def tn(a, b):
    return lax.dot_general(a, b, (((0,), (0,)), ((), ())), preferred_element_type=F32)


def normalise(z):
    mu = jnp.mean(z, axis=-1, keepdims=True)
    c = z - mu
    rs = lax.rsqrt(jnp.mean(c * c, axis=-1, keepdims=True) + EPS)
    return c * rs, rs


def norm_back(dn, n, rs):
    return (dn - jnp.mean(dn, axis=-1, keepdims=True) - n * jnp.mean(dn * n, axis=-1, keepdims=True)) * rs


def low_lanes(shape):
    return lax.broadcasted_iota(jnp.int32, shape, len(shape) - 1) % 128 < 64


def body(
    direct, nz, rw, n_in, *refs
):
    ins, refs = refs[:n_in], refs[n_in:]
    if direct:
        wl, xin, cot, seg, rnd, sh_in, ga_in, mb_in, qv_in = ins
        act, dxo, gq_out, go_out, g1_out, g2_out, gsm = refs[:7]
        refs = refs[7:]
    else:
        wl, xin, cot, seg, rnd, sm = ins
        act, dxo, gout, gsm = refs[:4]
        refs = refs[4:]
    (
    W, SG, SV, XA, KV, QP, OO, LSE, H1, DG, G, N1, N2, RS1, RS2, XR, DZ, EB,
    PB, rsib, ry, DXP, xsib, xy, xz, ACC, MX, LS, DKV, DU, DQ, DO, DEL, XRV, ZRV, SL, St1, St2, Sz, Sx,
        SMS, segk, segqm, SA,
        wg_s, wg_r, ax_s, ax_r, a4_s, a4_r, r4_s, r4_r, r16_s, r16_r, g_s, g_r, s_s, s_r,
    ) = refs
    if direct:
        sm = SMS
    d, z, t = lax.axis_index("dp"), lax.axis_index("seq"), lax.axis_index("tensor")
    c = t % 2
    y = t // 2
    sib, yp = 2 * y + (1 - c), 2 * (1 - y) + c
    DM = XA.shape[2]
    TL = xin.shape[0]
    QT = TL // 4
    HALF = TL // 2
    dsib, dyp = (d, z, sib), (d, z, yp)
    zk = [lax.rem(z + k, nz) for k in range(nz)]
    upper = z // 2
    edge = (1 - z) * (1 - upper) + (z - 2) * upper
    inner = 1 - edge
    ck = [z] + [o + upper * (nz - 1 - 2 * o) for o in (edge, 2, 3)]

    bar = pltpu.get_barrier_semaphore()
    peers = [dsib, dyp] + [(d, zk[k], t) for k in range(1, nz)]
    if direct:
        dx_dev = (1 - d, z, t)
        peers.append(dx_dev)
    for p in peers:
        pl.semaphore_signal(bar, inc=1, device_id=p, device_id_type=MESH)
    pl.semaphore_wait(bar, len(peers))

    def send(src, dst, ss, rs, dev):
        cp = pltpu.make_async_remote_copy(src_ref=src, dst_ref=dst, send_sem=ss, recv_sem=rs, device_id=dev, device_id_type=MESH)
        cp.start()
        return cp

    def rows(start, n):
        return pl.ds(pl.multiple_of(start, n if n % 16 == 0 else 16), n)

    own = rows(t * QT, QT)

    def copy_to(src, dst, ss, rs, dev):
        return pltpu.make_async_remote_copy(src_ref=src, dst_ref=dst, send_sem=ss, recv_sem=rs, device_id=dev, device_id_type=MESH)

    if direct:
        slot = d * nz + z

        def w_ref(p, k):
            if p == 6:
                return SG.at[d * nz + k]
            return W.at[p, rows((d * nz + k) * rw, rw), :]

        def w_own(p):
            src = sm if p == 6 else wl.at[p]
            dst = w_ref(p, z)
            out = []
            for i, step in enumerate((1, 2, -1, -2)):
                ok = z + step < nz if step > 0 else z + step >= 0
                out.append((ok, copy_to(src, dst, wg_s.at[p, i], wg_r.at[p, z], (d, z + step, t))))
            return out

        def w_over(p, k):
            return copy_to(w_ref(p, k), w_ref(p, k), wg_s.at[p, 5 + k], wg_r.at[p, nz + k], dx_dev)

        def w_hop(p):
            return copy_to(w_ref(p, ck[3]), w_ref(p, ck[3]), wg_s.at[p, 4], wg_r.at[p, ck[3]], (d, nz - 1 - ck[3], t))

        def w_wait(p, k):
            copy_to(w_ref(p, k), w_ref(p, k), wg_s.at[p, 4], wg_r.at[p, k], dx_dev).wait_recv()

        def w_a(p):
            if p == 6:
                SG[slot] = sm[...]
            else:
                W[p, rows(slot * rw, rw), :] = wl[p]
            for ok, cp in w_own(p):
                pl.when(ok)(cp.start)

        def w_o(p):
            src = sm if p == 6 else wl.at[p]
            copy_to(src, w_ref(p, z), wg_s.at[p, 5 + z], wg_r.at[p, nz + z], dx_dev).start()

        def w_b(p):
            @pl.when(inner == 1)
            def _():
                w_wait(p, ck[3])
                w_hop(p).start()

        def w_c(p):
            for k in ck[1:3]:
                w_wait(p, k)
                w_over(p, k).start()

        def w_d(p):
            @pl.when(edge == 1)
            def _():
                w_wait(p, ck[3])

            w_over(p, ck[3]).start()

        def w_fin(p):
            for k in range(nz):
                w_over(p, k).wait_recv()

        def w_sent(p):
            for ok, cp in w_own(p):
                pl.when(ok)(cp.wait_send)

            @pl.when(inner == 1)
            def _():
                w_hop(p).wait_send()

            for k in ck:
                w_over(p, k).wait_send()
    else:

        def w_a(p):
            if p == 6:
                SV[...] = sm[...]
            else:
                W[p] = wl[p]

        def w_b(p):
            pass

        w_o = w_c = w_d = w_fin = w_sent = w_b

    ST = QT // 2

    def own_part(b):
        return rows(t * QT + b * ST, ST)

    def ag4(i, ref):
        st = {}

        def put(b):
            r = ref.at[own_part(b), :]
            st["c", b] = send(r, r, a4_s.at[i, b], a4_r.at[i, b], dsib)
            st["y", b] = send(r, r, a4_s.at[i, 2 + b], a4_r.at[i, 2 + b], dyp)

        def fin():
            for b in range(2):
                st["y", b].wait_recv()
                r = ref.at[rows(yp * QT + b * ST, ST), :]
                st["o", b] = send(r, r, a4_s.at[i, 4 + b], a4_r.at[i, 4 + b], dsib)
            for b in range(2):
                st["c", b].wait_recv()
                st["o", b].wait_recv()

        def sent():
            for cp in st.values():
                cp.wait_send()

        return put, fin, sent

    def rs4(i, part, consume, filler=None):
        r0 = [(1 - y) * HALF, y * HALF]
        st = {}
        for k in range(2):
            PB[rows(r0[k], HALF), :] = part(rows(r0[k], HALF)).astype(BF)
            for b in range(2):
                st["c", k, b] = send(
                    PB.at[rows(r0[k] + (1 - c) * QT + b * ST, ST), :], rsib.at[k, b], r4_s.at[i, 2 * k + b], r4_r.at[i, 2 * k + b], dsib
                )
            if k == 0:
                for b in range(2):
                    st["c", 0, b].wait_recv()
                    mine = rows(r0[0] + c * QT + b * ST, ST)
                    PB[mine, :] = (PB[mine, :].astype(F32) + rsib[0, b].astype(F32)).astype(BF)
                    st["y", b] = send(PB.at[mine, :], ry.at[b], r4_s.at[i, 4 + b], r4_r.at[i, 4 + b], dyp)
        if filler is not None:
            filler()
        for b in range(2):
            st["c", 1, b].wait_recv()
            st["y", b].wait_recv()
            consume(b, PB[own_part(b), :].astype(F32) + rsib[1, b].astype(F32) + ry[b].astype(F32))
        for cp in st.values():
            cp.wait_send()

    def xgather(l):
        st = {}

        def src_rows(k, q):
            return XA.at[l, rows(k * TL + q * QT, QT), :]

        def along(k, to, kind):
            r = src_rows(k, t)
            return copy_to(r, r, ax_s.at[l, kind * nz + k], ax_r.at[l, k], (d, to, t))

        def hop(j):
            right = (z - ck[j] + nz) // nz
            to = z - 1 + 2 * right
            return (to >= 0) & (to < nz), along(ck[j], to, 0)

        ends = [(z < nz - 1, along(z, z + 1, 0)), (z > 0, along(z, z - 1, 1))]

        def local(j):
            r = src_rows(ck[j], t)
            st["y", j] = send(r, r, ax_s.at[l, 2 * nz + ck[j]], ax_r.at[l, nz + ck[j]], dyp)
            st["c", j] = send(r, r, ax_s.at[l, 3 * nz + ck[j]], ax_r.at[l, 2 * nz + ck[j]], dsib)

        def start():
            for ok, cp in ends:
                pl.when(ok)(cp.start)
            if l > 0:
                local(0)

        def arrive(j):
            along(ck[j], z, 0).wait_recv()
            ok, cp = hop(j)
            pl.when(ok)(cp.start)
            local(j)

        def fwd(j):
            st["y", j].wait_recv()
            r = src_rows(ck[j], yp)
            st["c2", j] = send(r, r, ax_s.at[l, 4 * nz + ck[j]], ax_r.at[l, 3 * nz + ck[j]], dsib)

        def fin(j):
            st["c", j].wait_recv()
            st["c2", j].wait_recv()

        def sent():
            for ok, cp in ends + [hop(j) for j in range(1, nz)]:
                pl.when(ok)(cp.wait_send)
            for cp in st.values():
                cp.wait_send()

        return start, arrive, fwd, fin, sent

    def small(l, r):
        return SV[l, r : r + 1, :]

    def kv_proj(l, j):
        r = rows(ck[j] * TL, TL)
        bias = SV[l, 8:9, 0:384]
        KV[l, r, :] = (nn(XA[l, r, :], W[3 * l, :, 0:384]) + bias).astype(BF)

    def q_proj(l):
        bias = SV[l, 7:8, 0:256]
        q = (nn(XA[l, rows(z * TL, TL), :], W[3 * l, :, 384:640]) + bias).astype(BF).astype(F32) * 0.125
        a, b = q[:, 0:128], q[:, 128:256]
        lo = low_lanes(a.shape)
        QP[l, :, 0:128] = jnp.where(lo, a, 0.0).astype(BF)
        QP[l, :, 128:256] = jnp.where(lo, 0.0, a).astype(BF)
        QP[l, :, 256:384] = jnp.where(lo, b, 0.0).astype(BF)

    nb = TL // BLK

    def masked_scores(l, h, hl, r, j):
        kv = KV[l, r, pl.ds(hl, 128)]
        s = nt(kv, QP[l, :, pl.ds(hl, 128)])
        sq = segqm[h, pl.ds(pl.multiple_of(ck[j] * nb, nb), nb), :]
        sk = segk[r, :]
        parts = []
        for b in range(nb):
            skb = jnp.concatenate([sk[b * BLK : (b + 1) * BLK]] * (TL // 128), axis=1)
            parts.append(jnp.where(skb == sq[b : b + 1], s[b * BLK : (b + 1) * BLK], NEG))
        return kv, jnp.concatenate(parts, axis=0)

    def attend(l, j):
        r = rows(ck[j] * TL, TL)

        def head(h, carry):
            hl = pl.multiple_of(h * 128, 128)
            kv, s = masked_scores(l, h, hl, r, j)
            top = jnp.max(s, axis=0, keepdims=True)
            if j > 0:
                before = MX[h]
                top = jnp.maximum(before, top)
            e = jnp.exp(s - top)
            total = jnp.sum(e, axis=0, keepdims=True)
            o = tn(kv, e.astype(BF))
            if j > 0:
                a = jnp.exp(before - top)
                total = total + LS[h] * a
                o = o + ACC[h] * a
            MX[h] = top
            LS[h] = total
            ACC[h] = o
            return carry

        lax.fori_loop(0, 3, head, 0)

    def attend_end(l):
        o = []
        for h in range(3):
            LSE[3 * l + h] = MX[h] + jnp.log(LS[h])
            o.append((ACC[h] / LS[h]).T)
        lo = low_lanes(o[0].shape)
        OO[l, :, 0:128] = jnp.where(lo, 0.0, o[2]).astype(BF)
        OO[l, :, 128:256] = jnp.where(lo, o[1], o[0]).astype(BF)

    def gelu_parts(u):
        k = 0.7978845608028654
        th = jnp.tanh(k * (u + 0.044715 * u * u * u))
        g = 0.5 * u * (1.0 + th)
        dg = 0.5 * (1.0 + th) + 0.5 * u * (1.0 - th * th) * (k * (1.0 + 3 * 0.044715 * u * u))
        return g, dg

    seen = []

    def forward(l, bg, then):
        start, arrive, fwd, fin, sent = xg[l]
        if l > 0:
            start()
            arrive(1)
            fwd(0)
            fin(0)
            w_fin(3)
        q_proj(l)
        kv_proj(l, 0)
        arrive(2)
        fwd(1)
        attend(l, 0)
        arrive(3)
        fwd(2)
        bg[0]()
        for j in range(1, nz):
            fin(j)
            kv_proj(l, j)
            attend(l, j)
            if j == 1:
                fwd(3)
            bg[j]()
        attend_end(l)
        sent()
        wo = W[3 * l, :, 512:768]
        put, done, gone = ag4(4 * l, H1.at[l])

        def first(b, r):
            part = pl.ds(b * ST, ST)
            z1 = XR[part, :] + r + small(l, 0)
            n1, rs1 = normalise(z1)
            N1[l, part, :] = n1
            RS1[l, part, :] = rs1
            h1 = n1 * small(l, 4) + small(l, 1)
            H1[l, own_part(b), :] = h1.astype(BF)
            XR[part, :] = h1
            put(b)

        rs4(3 * l, lambda rr: nt(OO[l, rr, :], wo), first, bg[4])
        bg[5]()
        done()
        w_fin(3 * l + 1)

        def ffn(rr):
            u = nn(H1[l, rr, :], W[3 * l + 1]) + small(l, 6)
            g, dg = gelu_parts(u)
            DG[l, rr, :] = dg.astype(BF)
            gb = g.astype(BF)
            G[l, rr, :] = gb
            if l not in seen:
                seen.append(l)
                w_fin(3 * l + 2)
            return nt(gb, W[3 * l + 2])

        def fill():
            gone()
            bg[6]()

        def second(b, r):
            part = pl.ds(b * ST, ST)
            z2 = XR[part, :] + r + small(l, 2)
            n2, rs2 = normalise(z2)
            N2[l, part, :] = n2
            RS2[l, part, :] = rs2
            out = n2 * small(l, 5) + small(l, 3)
            XR[part, :] = out
            then(b, out)

        rs4(3 * l + 1, ffn, second, fill)
        bg[7]()

    gx = {}

    if direct:

        def g_start(p):
            for k in ck[::-1]:
                gx[p, len(gx)] = send(
                    W.at[p, rows(((1 - d) * nz + k) * rw, rw), :], XRV.at[p, rows(k * rw, rw), :], g_s.at[p, k], g_r.at[p, k], dx_dev
                )

        def g_slot(p, k):
            return W.at[p, rows((d * nz + k) * rw, rw), :]

        def g_to(p, part, to, slot_there):
            return copy_to(g_slot(p, part), ZRV.at[p, slot_there], g_s.at[p, nz + part], g_r.at[p, nz + slot_there], (d, to, t))

        def g_landed(p, k):
            x = ZRV.at[p, k]
            copy_to(x, x, g_s.at[p, nz + k], g_r.at[p, nz + k], dx_dev).wait_recv()

        def g_far(p):
            return lambda: g_to(p, ck[3], ck[1], ck[1]), lambda: g_to(p, ck[3], ck[3], z)

        def g_mid(p):
            for k in ck[::-1]:
                r = g_slot(p, k)
                x = XRV.at[p, rows(k * rw, rw), :]
                copy_to(x, x, g_s.at[p, k], g_r.at[p, k], dx_dev).wait_recv()
                r[...] = (r[...].astype(F32) + x[...].astype(F32)).astype(BF)
                if k is ck[3]:
                    pl.when(edge == 1)(g_far(p)[0]().start)
                elif k is not z:
                    g_to(p, k, k, z).start()

        def g_add(p):
            @pl.when(inner == 1)
            def _():
                g_landed(p, z)
                r = g_slot(p, ck[3])
                r[...] = (r[...].astype(F32) + ZRV[p, z].astype(F32)).astype(BF)
                g_far(p)[1]().start()

        def g_fin(p):
            l = p // 3
            goal = (SA, g1_out.at[l], g2_out.at[l])[p % 3]
            tot = g_slot(p, z)[...].astype(F32)
            for k in ck[1:3]:
                g_landed(p, k)
                tot = tot + ZRV[p, k].astype(F32)
            goal[...] = tot

            @pl.when(inner == 1)
            def _():
                g_landed(p, ck[3])
                goal[...] = goal[...] + ZRV[p, ck[3]].astype(F32)
                g_far(p)[1]().wait_send()

            pl.when(edge == 1)(g_far(p)[0]().wait_send)
            for k in ck[1:3]:
                g_to(p, k, k, z).wait_send()
            if p % 3 == 0:
                tile = [SA[:, 128 * i : 128 * (i + 1)] for i in range(6)]
                lo = low_lanes(tile[0].shape)
                gq_out[l, 0, :, 0:128] = tile[3]
                gq_out[l, 0, :, 128:192] = tile[4][:, 0:64]
                gq_out[l, 1, :, 0:128] = jnp.where(lo, tile[0], tile[1])
                gq_out[l, 1, :, 128:192] = tile[2][:, 0:64]
                gq_out[l, 2, :, 0:128] = pltpu.roll(jnp.where(lo, tile[1], tile[0]), 64, 1)
                gq_out[l, 2, :, 128:192] = pltpu.roll(tile[2], 64, 1)[:, 0:64]
                go_out[l, :, 0:128] = pltpu.roll(tile[5], 64, 1)
                go_out[l, :, 128:192] = pltpu.roll(tile[4], 64, 1)[:, 0:64]
    else:

        def g_start(p):
            gout[p] = W[p]

        def g_mid(p):
            pass

        g_add = g_fin = g_mid

    def accumulate(l, row, b, v):
        v = jnp.sum(v, axis=0, keepdims=True)
        SL[l, row : row + 1, :] = v if b == 0 else SL[l, row : row + 1, :] + v

    def second_back(l):
        put, done, gone = ag4(4 * l + 2, EB.at[2 * l + 1])

        def one(b, dy):
            part = pl.ds(b * ST, ST)
            n2 = N2[l, part, :]
            accumulate(l, 3, b, dy)
            accumulate(l, 5, b, dy * n2)
            dz2 = norm_back(dy * small(l, 5), n2, RS2[l, part, :])
            accumulate(l, 2, b, dz2)
            DZ[part, :] = dz2
            EB[2 * l + 1, own_part(b), :] = dz2.astype(BF)
            put(b)

        return one, done, gone

    def backward(l, bg, done, gone, then):
        bg.get(0, nop)()
        done()

        def ffn_back(rr):
            dgm = nn(EB[2 * l + 1, rr, :], W[3 * l + 2])
            du = (dgm * DG[l, rr, :].astype(F32)).astype(BF)
            DU[rr, :] = du
            return nt(du, W[3 * l + 1])

        def fill():
            gone()
            w_sent(3 * l + 2)
            w_sent(3 * l + 1)
            W[3 * l + 2] = tn(EB[2 * l + 1], G[l]).astype(BF)
            g_start(3 * l + 2)
            W[3 * l + 1] = tn(H1[l], DU[...]).astype(BF)
            g_start(3 * l + 1)
            SL[l, 6:7, :] = jnp.sum(DU[...].astype(F32), axis=0, keepdims=True)
            bg.get(1, nop)()

        put, done1, gone1 = ag4(4 * l + 3, EB.at[2 * l])

        def first_back(b, r):
            part = pl.ds(b * ST, ST)
            dh1 = DZ[part, :] + r
            n1 = N1[l, part, :]
            dz1 = norm_back(dh1 * small(l, 4), n1, RS1[l, part, :])
            DZ[part, :] = dz1
            EB[2 * l, own_part(b), :] = dz1.astype(BF)
            put(b)
            accumulate(l, 1, b, dh1)
            accumulate(l, 4, b, dh1 * n1)
            accumulate(l, 0, b, dz1)

        rs4(3 * l + 2, ffn_back, first_back, fill)
        bg.get(2, nop)()
        done1()
        doo = nn(EB[2 * l], W[3 * l, :, 512:768]).astype(BF).astype(F32)
        lo = low_lanes((TL, 128))
        da, db = doo[:, 0:128], doo[:, 128:256]
        DO[:, 0:128] = jnp.where(lo, 0.0, db).astype(BF)
        DO[:, 128:256] = jnp.where(lo, db, 0.0).astype(BF)
        DO[:, 256:384] = jnp.where(lo, 0.0, da).astype(BF)
        prod = (doo * OO[l].astype(F32)).T
        DEL[0] = jnp.sum(prod[192:256], axis=0, keepdims=True)
        DEL[1] = jnp.sum(prod[128:192], axis=0, keepdims=True)
        DEL[2] = jnp.sum(prod[64:128], axis=0, keepdims=True)

        xs = {}
        order = list(range(nz - 1, 0, -1)) + [0]

        def attend_back(j, first):
            r = rows(ck[j] * TL, TL)

            def head(h, carry):
                hl = pl.multiple_of(h * 128, 128)
                kv, s = masked_scores(l, h, hl, r, j)
                q = QP[l, :, pl.ds(hl, 128)]
                do = DO[:, pl.ds(hl, 128)]
                p = jnp.exp(s - LSE[3 * l + h])
                dp = nt(kv, do)
                ds = (p * (dp - DEL[h])).astype(BF)
                DKV[r, pl.ds(hl, 128)] = (nn(ds, q) + nn(p.astype(BF), do)).astype(BF)
                dq = tn(kv, ds)
                if first:
                    ACC[h] = dq
                else:
                    ACC[h] = ACC[h] + dq
                return carry

            lax.fori_loop(0, 3, head, 0)

        def dx_parts(j):
            for k in range(2):
                r0 = [(1 - y) * HALF, y * HALF][k]
                v = nt(DKV[rows(ck[j] * TL + r0, HALF), :], W[3 * l, :, 0:384])
                if j == 0:
                    v = v + nt(DQ[rows(r0, HALF), :], W[3 * l, :, 384:640])
                DXP[j, rows(r0, HALF), :] = v.astype(BF)
                xs["c", j, k] = send(DXP.at[j, rows(r0 + (1 - c) * QT, QT), :], xsib.at[j, k], r16_s.at[l, 3 * j + k], r16_r.at[l, 3 * j + k], dsib)

        def dx_y(j):
            xs["c", j, 0].wait_recv()
            mine = rows(yp * QT, QT)
            DXP[j, mine, :] = (DXP[j, mine, :].astype(F32) + xsib[j, 0].astype(F32)).astype(BF)
            xs["y", j] = send(DXP.at[j, mine, :], xy.at[j], r16_s.at[l, 3 * j + 2], r16_r.at[l, 3 * j + 2], dyp)

        def dx_z(j):
            xs["c", j, 1].wait_recv()
            xs["y", j].wait_recv()
            tot = DXP[j, own, :].astype(F32) + xsib[j, 1].astype(F32) + xy[j].astype(F32)
            if j == 0:
                return tot
            DXP[j, own, :] = tot.astype(BF)
            if j == nz - 1:
                pl.when(edge == 1)(dx_far()[0]().start)
            else:
                dx_to(j, ck[j], z).start()

        def dx_to(j, to, there):
            return copy_to(DXP.at[j, own, :], xz.at[l, there], r16_s.at[l, 3 * nz + ck[j]], r16_r.at[l, 3 * nz + there], (d, to, t))

        def dx_far():
            return lambda: dx_to(nz - 1, ck[1], ck[1]), lambda: dx_to(nz - 1, ck[nz - 1], z)

        def dx_landed(k):
            x = xz.at[l, k]
            copy_to(x, x, r16_s.at[l, 3 * nz + k], r16_r.at[l, 3 * nz + k], dsib).wait_recv()

        def dx_add():
            @pl.when(inner == 1)
            def _():
                dx_landed(z)
                j = nz - 1
                DXP[j, own, :] = (DXP[j, own, :].astype(F32) + xz[l, z].astype(F32)).astype(BF)
                dx_far()[1]().start()

        for i, j in enumerate(order):
            attend_back(j, i == 0)
            if i >= 2:
                dx_z(order[i - 2])
            if i < 2:
                bg.get(3 + i, nop)()
            if j == 0:
                a01 = ACC[0]
                hi = lax.broadcasted_iota(jnp.int32, a01.shape, 0) < 64
                DQ[:, 0:128] = (jnp.where(hi, a01, ACC[1]).T * 0.125).astype(BF)
                DQ[:, 128:256] = (jnp.where(hi, ACC[2], 0.0).T * 0.125).astype(BF)
            dx_parts(j)
            dx_y(j)
        gone1()
        w_sent(3 * l)
        xown = XA[l, rows(z * TL, TL), :]
        gq = tn(xown, DQ[...])
        go = tn(EB[2 * l], OO[l])
        gkv = tn(XA[l], DKV[...])
        SL[l, 7:8, 0:384] = jnp.sum(DKV[...].astype(F32), axis=0, keepdims=True)
        SL[l, 7:8, 384:640] = jnp.sum(DQ[...].astype(F32), axis=0, keepdims=True)
        SL[l, 7:8, 640:768] = jnp.zeros((1, 128), F32)
        W[3 * l, :, 0:384] = gkv.astype(BF)
        W[3 * l, :, 384:512] = gq[:, 0:128].astype(BF)
        W[3 * l, :, 512:640] = (gq[:, 128:256] + go[:, 0:128]).astype(BF)
        W[3 * l, :, 640:768] = go[:, 128:256].astype(BF)
        g_start(3 * l)
        dx_z(order[nz - 2])
        dx_add()
        bg.get(5, nop)()
        DZ[...] = DZ[...] + dx_z(0)
        for k in ck[1:3]:
            dx_landed(k)
            DZ[...] = DZ[...] + xz[l, k].astype(F32)

        @pl.when(inner == 1)
        def _():
            dx_landed(ck[3])
            DZ[...] = DZ[...] + xz[l, ck[3]].astype(F32)
            dx_far()[1]().wait_send()

        then(DZ[...])
        pl.when(edge == 1)(dx_far()[0]().wait_send)
        for j in (1, 2):
            dx_to(j, ck[j], z).wait_send()
        for cp in xs.values():
            cp.wait_send()

    xg = [xgather(0), xgather(1)]

    def masks():
        length = seg.shape[1]
        nblk = length // BLK
        for i in range(length // 128):
            row = seg[:, 128 * i : 128 * (i + 1)].astype(F32)
            segk[128 * i : 128 * (i + 1), :] = jnp.broadcast_to(row, (128, 128)).T
        segq = seg[:, pl.ds(pl.multiple_of(z * TL, TL), TL)].astype(F32)
        block = lax.broadcasted_iota(jnp.int32, (1, TL), 1) // BLK
        key = lax.broadcasted_iota(jnp.int32, (nblk, TL), 0)
        away = key - (z * nb + lax.broadcasted_iota(jnp.int32, (nblk, TL), 1) // BLK)
        near = (away >= -1) & (away <= 1) | (key == 0) | (key == nblk - 1)
        for h in range(3):
            ok = near
            for r in range(rnd.shape[2]):
                pick = jnp.zeros((1, TL), jnp.int32)
                for b in range(nb):
                    pick = jnp.where(block == b, rnd[h, z * nb + b, r], pick)
                ok = ok | (key == pick)
            segqm[h] = jnp.where(ok, segq, -1.0)

    def run(*steps):
        def go():
            for fn, *a in steps:
                fn(*a)

        return go

    nop = run()
    if direct:
        SMS[...] = jnp.zeros_like(SMS)
        for l in range(LAYERS):
            SMS[l, 0:4, 0:rw] = sh_in[l].astype(BF).astype(F32)
            SMS[l, 4:6, 0:rw] = ga_in[l].astype(BF).astype(F32)
            SMS[l, 6:7, 0:rw] = mb_in[l].astype(BF).astype(F32)
            SMS[l, 8:10, 0 : rw // 4] = qv_in[l].astype(BF).astype(F32)
    for p in (6, 0, 1, 2):
        w_o(p)
    w_a(6)
    w_a(0)
    XA[0, rows(z * TL, TL), :] = xin[...]
    XR[...] = xin[own, :].astype(F32)
    w_b(6)
    w_b(0)
    w_c(6)
    w_c(0)
    xg[0][0]()
    masks()
    w_d(6)
    w_d(0)
    for p in (3, 4, 5):
        w_o(p)
    w_fin(6)
    if direct:
        wide = DM - 128
        nslot = SG.shape[0]
        for l in range(LAYERS):
            acc = jnp.zeros((16, DM), F32)
            cmp_ = jnp.zeros((8, DM), F32)
            for s_ in range(nslot):
                piece = jnp.concatenate([SG[s_, l], jnp.zeros((16, wide), F32)], axis=1)
                acc = acc + (pltpu.roll(piece, s_ * rw, 1) if s_ else piece)
                cmp_ = cmp_ + (pltpu.roll(piece[8:16], s_ * (rw // 4), 1) if s_ else piece[8:16])
            bq, bv = cmp_[0:1], cmp_[1:2]
            lane = lax.broadcasted_iota(jnp.int32, (1, DM), 1)
            kvb = jnp.where((lane >= 64) & (lane < 192), pltpu.roll(bv, 64, 1), 0.0) + jnp.where(
                (lane >= 320) & (lane < 384), pltpu.roll(bv, 192, 1), 0.0
            )
            SV[l, 0:8, :] = acc[0:8]
            SV[l, 7:8, :] = bq
            SV[l, 8:9, :] = kvb
    xg[0][1](1)
    w_fin(0)
    def next_input(b, v):
        XA[1, rows(z * TL + t * QT + b * ST, ST), :] = v.astype(BF)

    forward(0, [
        run((w_a, 1)),
        run(),
        run((w_b, 1)),
        run((w_a, 2), (w_c, 1)),
        run((w_d, 1), (w_b, 2), (w_a, 3)),
        run((w_c, 2), (w_d, 2)),
        run((w_b, 3), (w_a, 4), (w_c, 3)),
        run((w_d, 3)),
    ], next_input)
    start_back, done, gone = second_back(1)

    def last_output(b, v):
        start_back(b, cot[own_part(b), :].astype(F32))
        EB[0, own_part(b), :] = v.astype(BF)

    forward(1, [
        run((w_b, 4), (w_a, 5)),
        run((w_c, 4)),
        run((w_d, 4)),
        run(),
        run((w_b, 5)),
        run((w_c, 5), (w_d, 5)),
        run(),
        run(),
    ], last_output)
    act_put, act_done, act_sent = ag4(1, EB.at[0])

    def act_start():
        act_put(0)
        act_put(1)

    def act_end():
        act_done()
        act[...] = EB[0]
        act_sent()

    lower = second_back(0)

    def to_lower(dy):
        for b in range(2):
            lower[0](b, dy[b * ST : (b + 1) * ST])

    backward(1, {0: run((act_start,)), 1: run((act_end,)), 3: run((g_mid, 5)), 4: run((g_add, 5)), 5: run((g_mid, 4))}, done, gone, to_lower)

    keep = lax.broadcasted_iota(jnp.int32, SL.shape, 1) < 6

    def s1():
        cp = send(SL, St1, s_s.at[0], s_r.at[0], dsib)
        cp.wait_recv()
        cp.wait_send()
        SL[...] = SL[...] + jnp.where(keep, St1[...], 0.0)
        sc.append(send(SL, St2, s_s.at[1], s_r.at[1], dyp))

    sc = []
    dx_put, dx_done, dx_sent = ag4(5, EB.at[3])

    def to_output(dx):
        EB[3, own, :] = dx.astype(BF)
        dx_put(0)
        dx_put(1)

    backward(
        0, {1: run((g_add, 4), (g_mid, 3), (g_fin, 5)), 3: run((g_add, 3), (g_mid, 2), (g_fin, 4)), 4: run((g_add, 2)), 5: run((s1,), (g_mid, 1), (g_fin, 3))}, lower[1], lower[2], to_output
    )

    sc[0].wait_recv()
    sc[0].wait_send()
    SL[...] = SL[...] + jnp.where(keep, St2[...], 0.0)
    zc = [send(SL, Sz.at[k - 1], s_s.at[1 + k], s_r.at[1 + k], (d, zk[k], t)) for k in range(1, nz)]
    g_add(1)
    g_mid(0)
    for cp in zc:
        cp.wait_recv()
    for cp in zc:
        cp.wait_send()
    tot = SL[...]
    for k in range(nz - 1):
        tot = tot + Sz[k]
    if direct:
        SL[...] = tot
        xc = send(SL, Sx, s_s.at[1 + nz], s_r.at[1 + nz], dx_dev)
    g_add(0)
    dx_done()
    dxo[...] = EB[3].astype(F32)
    dx_sent()
    g_fin(2)
    g_fin(1)
    if direct:
        xc.wait_recv()
        xc.wait_send()
        tot = tot + Sx[...]
    if direct:
        lane = lax.broadcasted_iota(jnp.int32, (8, DM), 1)
        for l in range(LAYERS):
            x = tot[l]
            gsm[l, 0:8, :] = pltpu.roll(x, lax.rem(DM - slot * rw, DM), 1)[:, 0:128]
            gq = pltpu.roll(x, DM - 384, 1)
            gv = jnp.where(lane < 128, pltpu.roll(x, DM - 64, 1), pltpu.roll(x, DM - 192, 1))
            back = lax.rem(DM - slot * (rw // 4), DM)
            gsm[l, 8:16, :] = pltpu.roll(gq, back, 1)[:, 0:128]
            gsm[l, 16:24, :] = pltpu.roll(gv, back, 1)[:, 0:128]
    else:
        gsm[...] = tot
    g_fin(0)
    w_sent(6)
    for cp in list(gx.values()):
        cp.wait_send()


def shards(dp, nz, nt_, x_in, cotangent, segment_ids, random_blocks, wqkv, wo, w1, w2, qv_bias, mid_bias, shifts, gains):
    rw = wqkv.shape[1]
    direct = dp == 2 and rw % 16 == 0
    TL, DM = x_in.shape[1], x_in.shape[2]
    length = segment_ids.shape[1]
    z = lax.axis_index("seq")
    slot = lax.axis_index("dp") * nz + z
    axes = ("dp", "seq")

    qw, kw, vw = [wqkv[:, :, i, :].reshape(LAYERS, rw, 3, 64) for i in range(3)]
    ot = wo.transpose(0, 2, 1).reshape(LAYERS, rw, 3, 64)
    attn = jnp.concatenate(
        [kw[:, :, 0], vw[:, :, 0], vw[:, :, 1], kw[:, :, 1], kw[:, :, 2], vw[:, :, 2],
         qw[:, :, 0], qw[:, :, 1], qw[:, :, 2], ot[:, :, 2], ot[:, :, 1], ot[:, :, 0]], axis=2)
    wl = jnp.stack([attn, w1, w2.transpose(0, 2, 1)], axis=1).astype(BF).reshape(3 * LAYERS, rw, DM)

    def low(v):
        return v.astype(BF).astype(F32)

    if direct:
        small_in = (shifts, gains, mid_bias, qv_bias[:, :, 0])
    else:
        wl = lax.all_gather(wl, axes, axis=1, tiled=True)
        sh = lax.all_gather(shifts.astype(BF), axes, axis=2, tiled=True).astype(F32)
        ga = lax.all_gather(gains.astype(BF), axes, axis=2, tiled=True).astype(F32)
        mb = lax.all_gather(mid_bias.astype(BF), axes, axis=2, tiled=True).astype(F32)
        qv = lax.all_gather(qv_bias[:, :, 0].astype(BF), axes, axis=2, tiled=True).astype(F32)
        bq, bv = qv[:, 0:1], qv[:, 1:2]
        gap = jnp.zeros((LAYERS, 1, 64), F32)
        kvb = jnp.concatenate([gap, bv[..., 0:128], gap, gap, bv[..., 128:192]], axis=2)
        fit = lambda v: jnp.pad(v, ((0, 0), (0, 0), (0, DM - v.shape[2])))
        sm = jnp.concatenate([sh, ga, mb, fit(bq), fit(kvb), jnp.zeros((LAYERS, 7, DM), F32)], axis=1)
        small_in = (sm,)

    QT = TL // 4
    L = LAYERS
    nslot = dp * nz if direct else 1
    vm = pl.BlockSpec(memory_space=pltpu.VMEM)
    dma = pltpu.SemaphoreType.DMA
    xr = nz * rw if direct else 16
    scratch = [
        pltpu.VMEM((3 * L, DM, DM), BF),
        pltpu.VMEM((nslot, L, 16, 128), F32),
        pltpu.VMEM((L, 16, DM), F32),
        pltpu.VMEM((L, length, DM), BF),
        pltpu.VMEM((L, length, 384), BF),
        pltpu.VMEM((L, TL, 384), BF),
        pltpu.VMEM((L, TL, 256), BF),
        pltpu.VMEM((3 * L, 1, TL), F32),
        pltpu.VMEM((L, TL, DM), BF),
        pltpu.VMEM((L, TL, DM), BF),
        pltpu.VMEM((L, TL, DM), BF),
        pltpu.VMEM((L, QT, DM), F32),
        pltpu.VMEM((L, QT, DM), F32),
        pltpu.VMEM((L, QT, 1), F32),
        pltpu.VMEM((L, QT, 1), F32),
        pltpu.VMEM((QT, DM), F32),
        pltpu.VMEM((QT, DM), F32),
        pltpu.VMEM((2 * L, TL, DM), BF),
        pltpu.VMEM((TL, DM), BF),
        pltpu.VMEM((2, 2, QT // 2, DM), BF),
        pltpu.VMEM((2, QT // 2, DM), BF),
        pltpu.VMEM((nz, TL, DM), BF),
        pltpu.VMEM((nz, 2, QT, DM), BF),
        pltpu.VMEM((nz, QT, DM), BF),
        pltpu.VMEM((L, nz, QT, DM), BF),
        pltpu.VMEM((3, 128, TL), F32),
        pltpu.VMEM((3, 1, TL), F32),
        pltpu.VMEM((3, 1, TL), F32),
        pltpu.VMEM((length, 384), BF),
        pltpu.VMEM((TL, DM), BF),
        pltpu.VMEM((TL, 256), BF),
        pltpu.VMEM((TL, 384), BF),
        pltpu.VMEM((3, 1, TL), F32),
        pltpu.VMEM((3 * L, xr, DM) if direct else (1, 16, 128), BF),
        pltpu.VMEM((3 * L, nz, rw, DM) if direct else (1, 1, 16, 128), BF),
        pltpu.VMEM((L, 8, DM), F32),
        pltpu.VMEM((L, 8, DM), F32),
        pltpu.VMEM((L, 8, DM), F32),
        pltpu.VMEM((nz - 1, L, 8, DM), F32),
        pltpu.VMEM((L, 8, DM), F32),
        pltpu.VMEM((L, 16, 128), F32),
        pltpu.VMEM((length, 128), F32),
        pltpu.VMEM((3, length // BLK, TL), F32),
        pltpu.VMEM((rw, DM) if direct else (8, 128), F32),
        dma((7, 5 + nz)), dma((7, 2 * nz)),
        dma((L, 5 * nz)), dma((L, 4 * nz)),
        dma((8, 6)), dma((8, 6)),
        dma((6, 6)), dma((6, 6)),
        dma((L, 4 * nz)), dma((L, 4 * nz)),
        dma((6, 2 * nz)), dma((6, 2 * nz)),
        dma((2 + nz,)), dma((2 + nz,)),
    ]
    tokens = (jax.ShapeDtypeStruct((TL, DM), BF), jax.ShapeDtypeStruct((TL, DM), F32))
    if direct:
        grads = [(L, 3, rw, 192), (L, rw, 192), (L, rw, DM), (L, rw, DM), (L, 24, 128)]
        out_shape = tokens + tuple(jax.ShapeDtypeStruct(g, F32) for g in grads)
    else:
        out_shape = tokens + (jax.ShapeDtypeStruct((3 * L, DM, DM), BF), jax.ShapeDtypeStruct((L, 8, DM), F32))
    args = (wl, x_in[0], cotangent[0], segment_ids, random_blocks[0]) + small_in
    results = pl.pallas_call(
        functools.partial(body, direct, nz, rw, len(args)),
        out_shape=out_shape,
        in_specs=[vm] * 4 + [pl.BlockSpec(memory_space=pltpu.SMEM)] + [vm] * len(small_in),
        out_specs=(vm,) * len(out_shape),
        scratch_shapes=scratch,
        compiler_params=pltpu.CompilerParams(collective_id=0, has_side_effects=True, vmem_limit_bytes=60 * 2**20),
        name="encoder",
    )(*args)
    act, dx = results[:2]
    if direct:
        gq, go, g1, g2, gsm = results[2:]
        return (
            act[None],
            dx[None],
            gq.transpose(0, 2, 1, 3),
            go.transpose(0, 2, 1),
            g1,
            g2.transpose(0, 2, 1),
            gsm[:, 15:24:8, None, : rw // 4],
            gsm[:, 6:7, :rw],
            gsm[:, 0:4, :rw],
            gsm[:, 4:6, :rw],
        )
    gout, gsm = results[2:]
    gout = lax.psum_scatter(gout.astype(F32), axes, scatter_dimension=1, tiled=True).reshape(L, 3, rw, DM)
    gsm = lax.psum(gsm, "dp")
    ga, g1, g2 = gout[:, 0], gout[:, 1], gout[:, 2]
    pc = [ga[:, :, i * 64 : (i + 1) * 64] for i in range(12)]
    gq = jnp.concatenate([pc[6], pc[7], pc[8]], axis=2)
    gk = jnp.concatenate([pc[0], pc[3], pc[4]], axis=2)
    gv = jnp.concatenate([pc[1], pc[2], pc[5]], axis=2)
    go = jnp.concatenate([pc[11], pc[10], pc[9]], axis=2).transpose(0, 2, 1)
    sl = lax.dynamic_slice_in_dim(gsm[:, 0:7], slot * rw, rw, axis=2)
    dbq = gsm[:, 7, 384:576]
    dbv = jnp.concatenate([gsm[:, 7, 64:192], gsm[:, 7, 320:384]], axis=1)
    qv = lax.dynamic_slice_in_dim(jnp.stack([dbq, dbv], axis=1), slot * (rw // 4), rw // 4, axis=2)
    return (
        act[None],
        dx[None],
        jnp.stack([gq, gk, gv], axis=2),
        go,
        g1,
        g2.transpose(0, 2, 1),
        qv[:, :, None, :],
        sl[:, 6:7],
        sl[:, 0:4],
        sl[:, 4:6],
    )


def solution(mesh):
    both = ("dp", "seq")
    weights = (
        P(None, both, None, "tensor"),
        P(None, "tensor", both),
        P(None, both, "tensor"),
        P(None, "tensor", both),
        P(None, None, "tensor", both),
        P(None, "tensor", both),
        P(None, None, both),
        P(None, None, both),
    )
    tokens = P("dp", "seq", None)
    in_specs = (tokens, tokens, P("dp", None), P("dp", "tensor", None, None)) + weights
    out_specs = (tokens, tokens) + weights
    fn = functools.partial(shards, mesh.shape["dp"], mesh.shape["seq"], mesh.shape["tensor"])
    return jax.shard_map(fn, mesh=mesh, in_specs=in_specs, out_specs=out_specs, check_vma=False)
```

```python
import functools

import jax
import jax.numpy as jnp
from jax import lax
from jax.experimental import pallas as pl
from jax.experimental.pallas import tpu as pltpu
from jax.sharding import PartitionSpec as P

BLK = 64
LAYERS = 2
EPS = 1e-06
NEG = -1e30
BF = jnp.bfloat16
F32 = jnp.float32
MESH = pl.DeviceIdType.MESH


def nn(a, b):
    return lax.dot_general(a, b, (((1,), (0,)), ((), ())), preferred_element_type=F32)


def nt(a, b):
    return lax.dot_general(a, b, (((1,), (1,)), ((), ())), preferred_element_type=F32)


def tn(a, b):
    return lax.dot_general(a, b, (((0,), (0,)), ((), ())), preferred_element_type=F32)


def normalise(z):
    mu = jnp.mean(z, axis=-1, keepdims=True)
    c = z - mu
    rs = lax.rsqrt(jnp.mean(c * c, axis=-1, keepdims=True) + EPS)
    return c * rs, rs


def norm_back(dn, n, rs):
    return (dn - jnp.mean(dn, axis=-1, keepdims=True) - n * jnp.mean(dn * n, axis=-1, keepdims=True)) * rs


def low_lanes(shape):
    return lax.broadcasted_iota(jnp.int32, shape, len(shape) - 1) % 128 < 64


def body(
    direct, nz, rw, n_in, *refs
):
    ins, refs = refs[:n_in], refs[n_in:]
    if direct:
        q_in, xin, cot, seg, rnd, o_in, w1_in, w2_in, sh_in, ga_in, mb_in, qv_in = ins
        act, dxo, gq_out, go_out, g1_out, g2_out, qv_out, mb_out, sh_out, ga_out = refs[:10]
        refs = refs[10:]
    else:
        wl, xin, cot, seg, rnd, sm = ins
        act, dxo, gout, gsm = refs[:4]
        refs = refs[4:]
    (
    W, SG, SV, XA, KV, QP, OO, LSE, H1, DG, G, N1, N2, RS1, RS2, XR, DZ, EB,
    PB, rsib, ry, DXP, xsib, xy, xz, ACC, MX, LS, DKV, DU, DQ, DO, DEL, XRV, ZRV, SL, St1, St2, Sz, Sx,
        SMS, segk, segqm, SA, WL,
        wg_s, wg_r, ax_s, ax_r, a4_s, a4_r, r4_s, r4_r, r16_s, r16_r, g_s, g_r, s_s, s_r,
    ) = refs
    if direct:
        sm, wl = SMS, WL
    d, z, t = lax.axis_index("dp"), lax.axis_index("seq"), lax.axis_index("tensor")
    c = t % 2
    y = t // 2
    sib, yp = 2 * y + (1 - c), 2 * (1 - y) + c
    DM = XA.shape[2]
    TL = xin.shape[0]
    QT = TL // 4
    HALF = TL // 2
    dsib, dyp = (d, z, sib), (d, z, yp)
    zk = [lax.rem(z + k, nz) for k in range(nz)]
    upper = z // 2
    edge = (1 - z) * (1 - upper) + (z - 2) * upper
    inner = 1 - edge
    ck = [z] + [o + upper * (nz - 1 - 2 * o) for o in (edge, 2, 3)]

    bar = pltpu.get_barrier_semaphore()
    peers = [dsib, dyp] + [(d, zk[k], t) for k in range(1, nz)]
    if direct:
        dx_dev = (1 - d, z, t)
        peers.append(dx_dev)
    for p in peers:
        pl.semaphore_signal(bar, inc=1, device_id=p, device_id_type=MESH)
    pl.semaphore_wait(bar, len(peers))

    def send(src, dst, ss, rs, dev):
        cp = pltpu.make_async_remote_copy(src_ref=src, dst_ref=dst, send_sem=ss, recv_sem=rs, device_id=dev, device_id_type=MESH)
        cp.start()
        return cp

    def rows(start, n):
        return pl.ds(pl.multiple_of(start, n if n % 16 == 0 else 16), n)

    own = rows(t * QT, QT)

    def copy_to(src, dst, ss, rs, dev):
        return pltpu.make_async_remote_copy(src_ref=src, dst_ref=dst, send_sem=ss, recv_sem=rs, device_id=dev, device_id_type=MESH)

    if direct:
        slot = d * nz + z

        def w_ref(p, k):
            if p == 6:
                return SG.at[d * nz + k]
            return W.at[p, rows((d * nz + k) * rw, rw), :]

        def w_own(p):
            src = sm if p == 6 else wl.at[p]
            dst = w_ref(p, z)
            out = []
            for i, step in enumerate((1, 2, -1, -2)):
                ok = z + step < nz if step > 0 else z + step >= 0
                out.append((ok, copy_to(src, dst, wg_s.at[p, i], wg_r.at[p, z], (d, z + step, t))))
            return out

        def w_over(p, k):
            return copy_to(w_ref(p, k), w_ref(p, k), wg_s.at[p, 5 + k], wg_r.at[p, nz + k], dx_dev)

        def w_hop(p):
            return copy_to(w_ref(p, ck[3]), w_ref(p, ck[3]), wg_s.at[p, 4], wg_r.at[p, ck[3]], (d, nz - 1 - ck[3], t))

        def w_wait(p, k):
            copy_to(w_ref(p, k), w_ref(p, k), wg_s.at[p, 4], wg_r.at[p, k], dx_dev).wait_recv()

        def w_a(p):
            if p == 6:
                SG[slot] = sm[...]
            else:
                W[p, rows(slot * rw, rw), :] = wl[p]
            for ok, cp in w_own(p):
                pl.when(ok)(cp.start)

        def w_o(p):
            src = sm if p == 6 else wl.at[p]
            copy_to(src, w_ref(p, z), wg_s.at[p, 5 + z], wg_r.at[p, nz + z], dx_dev).start()

        def w_b(p):
            @pl.when(inner == 1)
            def _():
                w_wait(p, ck[3])
                w_hop(p).start()

        def w_c(p):
            for k in ck[1:3]:
                w_wait(p, k)
                w_over(p, k).start()

        def w_d(p):
            @pl.when(edge == 1)
            def _():
                w_wait(p, ck[3])

            w_over(p, ck[3]).start()

        def w_fin(p):
            for k in range(nz):
                w_over(p, k).wait_recv()

        def w_sent(p):
            for ok, cp in w_own(p):
                pl.when(ok)(cp.wait_send)

            @pl.when(inner == 1)
            def _():
                w_hop(p).wait_send()

            for k in ck:
                w_over(p, k).wait_send()
    else:

        def w_a(p):
            if p == 6:
                SV[...] = sm[...]
            else:
                W[p] = wl[p]

        def w_b(p):
            pass

        w_o = w_c = w_d = w_fin = w_sent = w_b

    ST = QT // 2

    def own_part(b):
        return rows(t * QT + b * ST, ST)

    def ag4(i, ref):
        st = {}

        def put(b):
            r = ref.at[own_part(b), :]
            st["c", b] = send(r, r, a4_s.at[i, b], a4_r.at[i, b], dsib)
            st["y", b] = send(r, r, a4_s.at[i, 2 + b], a4_r.at[i, 2 + b], dyp)

        def fin():
            for b in range(2):
                st["y", b].wait_recv()
                r = ref.at[rows(yp * QT + b * ST, ST), :]
                st["o", b] = send(r, r, a4_s.at[i, 4 + b], a4_r.at[i, 4 + b], dsib)
            for b in range(2):
                st["c", b].wait_recv()
                st["o", b].wait_recv()

        def sent():
            for cp in st.values():
                cp.wait_send()

        return put, fin, sent

    def rs4(i, part, consume, filler=None):
        r0 = [(1 - y) * HALF, y * HALF]
        st = {}
        for k in range(2):
            PB[rows(r0[k], HALF), :] = part(rows(r0[k], HALF)).astype(BF)
            for b in range(2):
                st["c", k, b] = send(
                    PB.at[rows(r0[k] + (1 - c) * QT + b * ST, ST), :], rsib.at[k, b], r4_s.at[i, 2 * k + b], r4_r.at[i, 2 * k + b], dsib
                )
            if k == 0:
                for b in range(2):
                    st["c", 0, b].wait_recv()
                    mine = rows(r0[0] + c * QT + b * ST, ST)
                    PB[mine, :] = (PB[mine, :].astype(F32) + rsib[0, b].astype(F32)).astype(BF)
                    st["y", b] = send(PB.at[mine, :], ry.at[b], r4_s.at[i, 4 + b], r4_r.at[i, 4 + b], dyp)
        if filler is not None:
            filler()
        for b in range(2):
            st["c", 1, b].wait_recv()
            st["y", b].wait_recv()
            consume(b, PB[own_part(b), :].astype(F32) + rsib[1, b].astype(F32) + ry[b].astype(F32))
        for cp in st.values():
            cp.wait_send()

    def xgather(l):
        st = {}

        def src_rows(k, q):
            return XA.at[l, rows(k * TL + q * QT, QT), :]

        def along(k, to, kind):
            r = src_rows(k, t)
            return copy_to(r, r, ax_s.at[l, kind * nz + k], ax_r.at[l, k], (d, to, t))

        def hop(j):
            right = (z - ck[j] + nz) // nz
            to = z - 1 + 2 * right
            return (to >= 0) & (to < nz), along(ck[j], to, 0)

        ends = [(z < nz - 1, along(z, z + 1, 0)), (z > 0, along(z, z - 1, 1))]

        def local(j):
            r = src_rows(ck[j], t)
            st["y", j] = send(r, r, ax_s.at[l, 2 * nz + ck[j]], ax_r.at[l, nz + ck[j]], dyp)
            st["c", j] = send(r, r, ax_s.at[l, 3 * nz + ck[j]], ax_r.at[l, 2 * nz + ck[j]], dsib)

        def start():
            for ok, cp in ends:
                pl.when(ok)(cp.start)
            if l > 0:
                local(0)

        def arrive(j):
            along(ck[j], z, 0).wait_recv()
            ok, cp = hop(j)
            pl.when(ok)(cp.start)
            local(j)

        def fwd(j):
            st["y", j].wait_recv()
            r = src_rows(ck[j], yp)
            st["c2", j] = send(r, r, ax_s.at[l, 4 * nz + ck[j]], ax_r.at[l, 3 * nz + ck[j]], dsib)

        def fin(j):
            st["c", j].wait_recv()
            st["c2", j].wait_recv()

        def sent():
            for ok, cp in ends + [hop(j) for j in range(1, nz)]:
                pl.when(ok)(cp.wait_send)
            for cp in st.values():
                cp.wait_send()

        return start, arrive, fwd, fin, sent

    def small(l, r):
        return SV[l, r : r + 1, :]

    def kv_proj(l, j):
        r = rows(ck[j] * TL, TL)
        bias = SV[l, 8:9, 0:384]
        KV[l, r, :] = (nn(XA[l, r, :], W[3 * l, :, 0:384]) + bias).astype(BF)

    def q_proj(l):
        bias = SV[l, 7:8, 0:256]
        q = (nn(XA[l, rows(z * TL, TL), :], W[3 * l, :, 384:640]) + bias).astype(BF).astype(F32) * 0.125
        a, b = q[:, 0:128], q[:, 128:256]
        lo = low_lanes(a.shape)
        QP[l, :, 0:128] = jnp.where(lo, a, 0.0).astype(BF)
        QP[l, :, 128:256] = jnp.where(lo, 0.0, a).astype(BF)
        QP[l, :, 256:384] = jnp.where(lo, b, 0.0).astype(BF)

    nb = TL // BLK

    def masked_scores(l, h, hl, r, j):
        kv = KV[l, r, pl.ds(hl, 128)]
        s = nt(kv, QP[l, :, pl.ds(hl, 128)])
        sq = segqm[h, pl.ds(pl.multiple_of(ck[j] * nb, nb), nb), :]
        sk = segk[r, :]
        parts = []
        for b in range(nb):
            skb = jnp.concatenate([sk[b * BLK : (b + 1) * BLK]] * (TL // 128), axis=1)
            parts.append(jnp.where(skb == sq[b : b + 1], s[b * BLK : (b + 1) * BLK], NEG))
        return kv, jnp.concatenate(parts, axis=0)

    def attend(l, j):
        r = rows(ck[j] * TL, TL)

        def head(h, carry):
            hl = pl.multiple_of(h * 128, 128)
            kv, s = masked_scores(l, h, hl, r, j)
            top = jnp.max(s, axis=0, keepdims=True)
            if j > 0:
                before = MX[h]
                top = jnp.maximum(before, top)
            e = jnp.exp(s - top)
            total = jnp.sum(e, axis=0, keepdims=True)
            o = tn(kv, e.astype(BF))
            if j > 0:
                a = jnp.exp(before - top)
                total = total + LS[h] * a
                o = o + ACC[h] * a
            MX[h] = top
            LS[h] = total
            ACC[h] = o
            return carry

        lax.fori_loop(0, 3, head, 0)

    def attend_end(l):
        o = []
        for h in range(3):
            LSE[3 * l + h] = MX[h] + jnp.log(LS[h])
            o.append((ACC[h] / LS[h]).T)
        lo = low_lanes(o[0].shape)
        OO[l, :, 0:128] = jnp.where(lo, 0.0, o[2]).astype(BF)
        OO[l, :, 128:256] = jnp.where(lo, o[1], o[0]).astype(BF)

    def gelu_parts(u):
        k = 0.7978845608028654
        th = jnp.tanh(k * (u + 0.044715 * u * u * u))
        g = 0.5 * u * (1.0 + th)
        dg = 0.5 * (1.0 + th) + 0.5 * u * (1.0 - th * th) * (k * (1.0 + 3 * 0.044715 * u * u))
        return g, dg

    seen = []

    def forward(l, bg, then):
        start, arrive, fwd, fin, sent = xg[l]
        if l > 0:
            start()
            arrive(1)
            fwd(0)
            fin(0)
            w_fin(3)
        q_proj(l)
        kv_proj(l, 0)
        arrive(2)
        fwd(1)
        attend(l, 0)
        arrive(3)
        fwd(2)
        bg[0]()
        for j in range(1, nz):
            fin(j)
            kv_proj(l, j)
            attend(l, j)
            if j == 1:
                fwd(3)
            bg[j]()
        attend_end(l)
        sent()
        wo = W[3 * l, :, 512:768]
        put, done, gone = ag4(4 * l, H1.at[l])

        def first(b, r):
            part = pl.ds(b * ST, ST)
            z1 = XR[part, :] + r + small(l, 0)
            n1, rs1 = normalise(z1)
            N1[l, part, :] = n1
            RS1[l, part, :] = rs1
            h1 = n1 * small(l, 4) + small(l, 1)
            H1[l, own_part(b), :] = h1.astype(BF)
            XR[part, :] = h1
            put(b)

        rs4(3 * l, lambda rr: nt(OO[l, rr, :], wo), first, bg[4])
        bg[5]()
        done()
        w_fin(3 * l + 1)

        def ffn(rr):
            u = nn(H1[l, rr, :], W[3 * l + 1]) + small(l, 6)
            g, dg = gelu_parts(u)
            DG[l, rr, :] = dg.astype(BF)
            gb = g.astype(BF)
            G[l, rr, :] = gb
            if l not in seen:
                seen.append(l)
                w_fin(3 * l + 2)
            return nt(gb, W[3 * l + 2])

        def fill():
            gone()
            bg[6]()

        def second(b, r):
            part = pl.ds(b * ST, ST)
            z2 = XR[part, :] + r + small(l, 2)
            n2, rs2 = normalise(z2)
            N2[l, part, :] = n2
            RS2[l, part, :] = rs2
            out = n2 * small(l, 5) + small(l, 3)
            XR[part, :] = out
            then(b, out)

        rs4(3 * l + 1, ffn, second, fill)
        bg[7]()

    gx = {}

    if direct:

        def g_start(p):
            for k in ck[::-1]:
                gx[p, len(gx)] = send(
                    W.at[p, rows(((1 - d) * nz + k) * rw, rw), :], XRV.at[p, rows(k * rw, rw), :], g_s.at[p, k], g_r.at[p, k], dx_dev
                )

        def g_slot(p, k):
            return W.at[p, rows((d * nz + k) * rw, rw), :]

        def g_to(p, part, to, slot_there):
            return copy_to(g_slot(p, part), ZRV.at[p, slot_there], g_s.at[p, nz + part], g_r.at[p, nz + slot_there], (d, to, t))

        def g_landed(p, k):
            x = ZRV.at[p, k]
            copy_to(x, x, g_s.at[p, nz + k], g_r.at[p, nz + k], dx_dev).wait_recv()

        def g_far(p):
            return lambda: g_to(p, ck[3], ck[1], ck[1]), lambda: g_to(p, ck[3], ck[3], z)

        def g_mid(p):
            for k in ck[::-1]:
                r = g_slot(p, k)
                x = XRV.at[p, rows(k * rw, rw), :]
                copy_to(x, x, g_s.at[p, k], g_r.at[p, k], dx_dev).wait_recv()
                r[...] = (r[...].astype(F32) + x[...].astype(F32)).astype(BF)
                if k is ck[3]:
                    pl.when(edge == 1)(g_far(p)[0]().start)
                elif k is not z:
                    g_to(p, k, k, z).start()

        def g_add(p):
            @pl.when(inner == 1)
            def _():
                g_landed(p, z)
                r = g_slot(p, ck[3])
                r[...] = (r[...].astype(F32) + ZRV[p, z].astype(F32)).astype(BF)
                g_far(p)[1]().start()

        def g_fin(p):
            l = p // 3
            goal = (SA, g1_out.at[l], g2_out.at[l])[p % 3]
            tot = g_slot(p, z)[...].astype(F32)
            for k in ck[1:3]:
                g_landed(p, k)
                tot = tot + ZRV[p, k].astype(F32)
            goal[...] = tot

            @pl.when(inner == 1)
            def _():
                g_landed(p, ck[3])
                goal[...] = goal[...] + ZRV[p, ck[3]].astype(F32)
                g_far(p)[1]().wait_send()

            pl.when(edge == 1)(g_far(p)[0]().wait_send)
            for k in ck[1:3]:
                g_to(p, k, k, z).wait_send()
            if p % 3 == 0:
                tile = [SA[:, 128 * i : 128 * (i + 1)] for i in range(6)]
                lo = low_lanes(tile[0].shape)
                gq_out[l, 0, :, 0:128] = tile[3]
                gq_out[l, 0, :, 128:192] = tile[4][:, 0:64]
                gq_out[l, 1, :, 0:128] = jnp.where(lo, tile[0], tile[1])
                gq_out[l, 1, :, 128:192] = tile[2][:, 0:64]
                gq_out[l, 2, :, 0:128] = pltpu.roll(jnp.where(lo, tile[1], tile[0]), 64, 1)
                gq_out[l, 2, :, 128:192] = pltpu.roll(tile[2], 64, 1)[:, 0:64]
                go_out[l, :, 0:128] = pltpu.roll(tile[5], 64, 1)
                go_out[l, :, 128:192] = pltpu.roll(tile[4], 64, 1)[:, 0:64]
    else:

        def g_start(p):
            gout[p] = W[p]

        def g_mid(p):
            pass

        g_add = g_fin = g_mid

    def accumulate(l, row, b, v):
        v = jnp.sum(v, axis=0, keepdims=True)
        SL[l, row : row + 1, :] = v if b == 0 else SL[l, row : row + 1, :] + v

    def second_back(l):
        put, done, gone = ag4(4 * l + 2, EB.at[2 * l + 1])

        def one(b, dy):
            part = pl.ds(b * ST, ST)
            n2 = N2[l, part, :]
            accumulate(l, 3, b, dy)
            accumulate(l, 5, b, dy * n2)
            dz2 = norm_back(dy * small(l, 5), n2, RS2[l, part, :])
            accumulate(l, 2, b, dz2)
            DZ[part, :] = dz2
            EB[2 * l + 1, own_part(b), :] = dz2.astype(BF)
            put(b)

        return one, done, gone

    def backward(l, bg, done, gone, then):
        bg.get(0, nop)()
        done()

        def ffn_back(rr):
            dgm = nn(EB[2 * l + 1, rr, :], W[3 * l + 2])
            du = (dgm * DG[l, rr, :].astype(F32)).astype(BF)
            DU[rr, :] = du
            return nt(du, W[3 * l + 1])

        def fill():
            gone()
            w_sent(3 * l + 2)
            w_sent(3 * l + 1)
            W[3 * l + 2] = tn(EB[2 * l + 1], G[l]).astype(BF)
            g_start(3 * l + 2)
            W[3 * l + 1] = tn(H1[l], DU[...]).astype(BF)
            g_start(3 * l + 1)
            SL[l, 6:7, :] = jnp.sum(DU[...].astype(F32), axis=0, keepdims=True)
            bg.get(1, nop)()

        put, done1, gone1 = ag4(4 * l + 3, EB.at[2 * l])

        def first_back(b, r):
            part = pl.ds(b * ST, ST)
            dh1 = DZ[part, :] + r
            n1 = N1[l, part, :]
            dz1 = norm_back(dh1 * small(l, 4), n1, RS1[l, part, :])
            DZ[part, :] = dz1
            EB[2 * l, own_part(b), :] = dz1.astype(BF)
            put(b)
            accumulate(l, 1, b, dh1)
            accumulate(l, 4, b, dh1 * n1)
            accumulate(l, 0, b, dz1)

        rs4(3 * l + 2, ffn_back, first_back, fill)
        bg.get(2, nop)()
        done1()
        doo = nn(EB[2 * l], W[3 * l, :, 512:768]).astype(BF).astype(F32)
        lo = low_lanes((TL, 128))
        da, db = doo[:, 0:128], doo[:, 128:256]
        DO[:, 0:128] = jnp.where(lo, 0.0, db).astype(BF)
        DO[:, 128:256] = jnp.where(lo, db, 0.0).astype(BF)
        DO[:, 256:384] = jnp.where(lo, 0.0, da).astype(BF)
        prod = (doo * OO[l].astype(F32)).T
        DEL[0] = jnp.sum(prod[192:256], axis=0, keepdims=True)
        DEL[1] = jnp.sum(prod[128:192], axis=0, keepdims=True)
        DEL[2] = jnp.sum(prod[64:128], axis=0, keepdims=True)

        xs = {}
        order = list(range(nz - 1, 0, -1)) + [0]

        def attend_back(j, first):
            r = rows(ck[j] * TL, TL)

            def head(h, carry):
                hl = pl.multiple_of(h * 128, 128)
                kv, s = masked_scores(l, h, hl, r, j)
                q = QP[l, :, pl.ds(hl, 128)]
                do = DO[:, pl.ds(hl, 128)]
                p = jnp.exp(s - LSE[3 * l + h])
                dp = nt(kv, do)
                ds = (p * (dp - DEL[h])).astype(BF)
                DKV[r, pl.ds(hl, 128)] = (nn(ds, q) + nn(p.astype(BF), do)).astype(BF)
                dq = tn(kv, ds)
                if first:
                    ACC[h] = dq
                else:
                    ACC[h] = ACC[h] + dq
                return carry

            lax.fori_loop(0, 3, head, 0)

        def dx_parts(j):
            for k in range(2):
                r0 = [(1 - y) * HALF, y * HALF][k]
                v = nt(DKV[rows(ck[j] * TL + r0, HALF), :], W[3 * l, :, 0:384])
                if j == 0:
                    v = v + nt(DQ[rows(r0, HALF), :], W[3 * l, :, 384:640])
                DXP[j, rows(r0, HALF), :] = v.astype(BF)
                xs["c", j, k] = send(DXP.at[j, rows(r0 + (1 - c) * QT, QT), :], xsib.at[j, k], r16_s.at[l, 3 * j + k], r16_r.at[l, 3 * j + k], dsib)

        def dx_y(j):
            xs["c", j, 0].wait_recv()
            mine = rows(yp * QT, QT)
            DXP[j, mine, :] = (DXP[j, mine, :].astype(F32) + xsib[j, 0].astype(F32)).astype(BF)
            xs["y", j] = send(DXP.at[j, mine, :], xy.at[j], r16_s.at[l, 3 * j + 2], r16_r.at[l, 3 * j + 2], dyp)

        def dx_z(j):
            xs["c", j, 1].wait_recv()
            xs["y", j].wait_recv()
            tot = DXP[j, own, :].astype(F32) + xsib[j, 1].astype(F32) + xy[j].astype(F32)
            if j == 0:
                return tot
            DXP[j, own, :] = tot.astype(BF)
            if j == nz - 1:
                pl.when(edge == 1)(dx_far()[0]().start)
            else:
                dx_to(j, ck[j], z).start()

        def dx_to(j, to, there):
            return copy_to(DXP.at[j, own, :], xz.at[l, there], r16_s.at[l, 3 * nz + ck[j]], r16_r.at[l, 3 * nz + there], (d, to, t))

        def dx_far():
            return lambda: dx_to(nz - 1, ck[1], ck[1]), lambda: dx_to(nz - 1, ck[nz - 1], z)

        def dx_landed(k):
            x = xz.at[l, k]
            copy_to(x, x, r16_s.at[l, 3 * nz + k], r16_r.at[l, 3 * nz + k], dsib).wait_recv()

        def dx_add():
            @pl.when(inner == 1)
            def _():
                dx_landed(z)
                j = nz - 1
                DXP[j, own, :] = (DXP[j, own, :].astype(F32) + xz[l, z].astype(F32)).astype(BF)
                dx_far()[1]().start()

        for i, j in enumerate(order):
            attend_back(j, i == 0)
            if i >= 2:
                dx_z(order[i - 2])
            if i < 2:
                bg.get(3 + i, nop)()
            if j == 0:
                a01 = ACC[0]
                hi = lax.broadcasted_iota(jnp.int32, a01.shape, 0) < 64
                DQ[:, 0:128] = (jnp.where(hi, a01, ACC[1]).T * 0.125).astype(BF)
                DQ[:, 128:256] = (jnp.where(hi, ACC[2], 0.0).T * 0.125).astype(BF)
            dx_parts(j)
            dx_y(j)
        gone1()
        w_sent(3 * l)
        xown = XA[l, rows(z * TL, TL), :]
        gq = tn(xown, DQ[...])
        go = tn(EB[2 * l], OO[l])
        gkv = tn(XA[l], DKV[...])
        SL[l, 7:8, 0:384] = jnp.sum(DKV[...].astype(F32), axis=0, keepdims=True)
        SL[l, 7:8, 384:640] = jnp.sum(DQ[...].astype(F32), axis=0, keepdims=True)
        SL[l, 7:8, 640:768] = jnp.zeros((1, 128), F32)
        W[3 * l, :, 0:384] = gkv.astype(BF)
        W[3 * l, :, 384:512] = gq[:, 0:128].astype(BF)
        W[3 * l, :, 512:640] = (gq[:, 128:256] + go[:, 0:128]).astype(BF)
        W[3 * l, :, 640:768] = go[:, 128:256].astype(BF)
        g_start(3 * l)
        dx_z(order[nz - 2])
        dx_add()
        bg.get(5, nop)()
        DZ[...] = DZ[...] + dx_z(0)
        for k in ck[1:3]:
            dx_landed(k)
            DZ[...] = DZ[...] + xz[l, k].astype(F32)

        @pl.when(inner == 1)
        def _():
            dx_landed(ck[3])
            DZ[...] = DZ[...] + xz[l, ck[3]].astype(F32)
            dx_far()[1]().wait_send()

        then(DZ[...])
        pl.when(edge == 1)(dx_far()[0]().wait_send)
        for j in (1, 2):
            dx_to(j, ck[j], z).wait_send()
        for cp in xs.values():
            cp.wait_send()

    xg = [xgather(0), xgather(1)]

    def pack(p):
        l = p // 3
        if p % 3:
            WL[p] = (w1_in, w2_in)[p % 3 - 1][l].astype(BF)
            return
        eye = lax.broadcasted_iota(jnp.int32, (rw, rw), 0) == lax.broadcasted_iota(jnp.int32, (rw, rw), 1)
        ot = nt(jnp.where(eye, 1.0, 0.0).astype(BF), o_in[l].astype(BF))

        def split(v):
            last = v[:, 128:192]
            return v[:, 0:128], jnp.concatenate([last, last], axis=1)

        (qa, qb), (ka, kb), (va, vb) = [split(q_in[l, i]) for i in range(3)]
        oa, ob = split(ot)
        lo = low_lanes(qa.shape)
        va = pltpu.roll(va, 64, 1)
        tiles = (
            jnp.where(lo, ka, va), jnp.where(lo, va, ka), jnp.where(lo, kb, vb), qa, jnp.where(lo, qb, ob), pltpu.roll(oa, 64, 1),
        )
        for i, v in enumerate(tiles):
            WL[p, :, 128 * i : 128 * (i + 1)] = v.astype(BF)

    def masks():
        length = seg.shape[1]
        nblk = length // BLK
        for i in range(length // 128):
            row = seg[:, 128 * i : 128 * (i + 1)].astype(F32)
            segk[128 * i : 128 * (i + 1), :] = jnp.broadcast_to(row, (128, 128)).T
        segq = seg[:, pl.ds(pl.multiple_of(z * TL, TL), TL)].astype(F32)
        block = lax.broadcasted_iota(jnp.int32, (1, TL), 1) // BLK
        key = lax.broadcasted_iota(jnp.int32, (nblk, TL), 0)
        away = key - (z * nb + lax.broadcasted_iota(jnp.int32, (nblk, TL), 1) // BLK)
        near = (away >= -1) & (away <= 1) | (key == 0) | (key == nblk - 1)
        for h in range(3):
            ok = near
            for r in range(rnd.shape[2]):
                pick = jnp.zeros((1, TL), jnp.int32)
                for b in range(nb):
                    pick = jnp.where(block == b, rnd[h, z * nb + b, r], pick)
                ok = ok | (key == pick)
            segqm[h] = jnp.where(ok, segq, -1.0)

    def run(*steps):
        def go():
            for fn, *a in steps:
                fn(*a)

        return go

    nop = run()
    if direct:
        SMS[...] = jnp.zeros_like(SMS)
        for l in range(LAYERS):
            SMS[l, 0:4, 0:rw] = sh_in[l].astype(BF).astype(F32)
            SMS[l, 4:6, 0:rw] = ga_in[l].astype(BF).astype(F32)
            SMS[l, 6:7, 0:rw] = mb_in[l].astype(BF).astype(F32)
            SMS[l, 8:10, 0 : rw // 4] = qv_in[l].astype(BF).astype(F32)
    if direct:
        pack(0)
    w_o(6)
    w_o(0)
    w_a(6)
    w_a(0)
    XA[0, rows(z * TL, TL), :] = xin[...]
    XR[...] = xin[own, :].astype(F32)
    if direct:
        for p in range(1, 3 * LAYERS):
            pack(p)
    w_o(1)
    w_o(2)
    w_b(6)
    w_b(0)
    w_c(6)
    w_c(0)
    xg[0][0]()
    masks()
    w_d(6)
    w_d(0)
    for p in (3, 4, 5):
        w_o(p)
    w_fin(6)
    if direct:
        wide = DM - 128
        nslot = SG.shape[0]
        for l in range(LAYERS):
            acc = jnp.zeros((16, DM), F32)
            cmp_ = jnp.zeros((8, DM), F32)
            for s_ in range(nslot):
                piece = jnp.concatenate([SG[s_, l], jnp.zeros((16, wide), F32)], axis=1)
                acc = acc + (pltpu.roll(piece, s_ * rw, 1) if s_ else piece)
                cmp_ = cmp_ + (pltpu.roll(piece[8:16], s_ * (rw // 4), 1) if s_ else piece[8:16])
            bq, bv = cmp_[0:1], cmp_[1:2]
            lane = lax.broadcasted_iota(jnp.int32, (1, DM), 1)
            kvb = jnp.where((lane >= 64) & (lane < 192), pltpu.roll(bv, 64, 1), 0.0) + jnp.where(
                (lane >= 320) & (lane < 384), pltpu.roll(bv, 192, 1), 0.0
            )
            SV[l, 0:8, :] = acc[0:8]
            SV[l, 7:8, :] = bq
            SV[l, 8:9, :] = kvb
    xg[0][1](1)
    w_fin(0)
    def next_input(b, v):
        XA[1, rows(z * TL + t * QT + b * ST, ST), :] = v.astype(BF)

    forward(0, [
        run((w_a, 1)),
        run(),
        run((w_b, 1)),
        run((w_a, 2), (w_c, 1)),
        run((w_d, 1), (w_b, 2), (w_a, 3)),
        run((w_c, 2), (w_d, 2)),
        run((w_b, 3), (w_a, 4), (w_c, 3)),
        run((w_d, 3)),
    ], next_input)
    start_back, done, gone = second_back(1)

    def last_output(b, v):
        start_back(b, cot[own_part(b), :].astype(F32))
        EB[0, own_part(b), :] = v.astype(BF)

    forward(1, [
        run((w_b, 4)),
        run((w_c, 4)),
        run((w_d, 4)),
        run((w_a, 5)),
        run((w_b, 5)),
        run((w_c, 5), (w_d, 5)),
        run(),
        run(),
    ], last_output)
    act_put, act_done, act_sent = ag4(1, EB.at[0])

    def act_start():
        act_put(0)
        act_put(1)

    def act_end():
        act_done()
        act[...] = EB[0]
        act_sent()

    lower = second_back(0)

    def to_lower(dy):
        for b in range(2):
            lower[0](b, dy[b * ST : (b + 1) * ST])

    backward(1, {0: run((act_start,)), 1: run((act_end,)), 3: run((g_mid, 5)), 4: run((g_add, 5)), 5: nop}, done, gone, to_lower)

    keep = lax.broadcasted_iota(jnp.int32, SL.shape, 1) < 6

    def s1():
        cp = send(SL, St1, s_s.at[0], s_r.at[0], dsib)
        cp.wait_recv()
        cp.wait_send()
        SL[...] = SL[...] + jnp.where(keep, St1[...], 0.0)
        sc.append(send(SL, St2, s_s.at[1], s_r.at[1], dyp))

    sc = []
    dx_put, dx_done, dx_sent = ag4(5, EB.at[3])

    def to_output(dx):
        EB[3, own, :] = dx.astype(BF)
        dx_put(0)
        dx_put(1)

    backward(
        0, {0: run((g_mid, 4)), 1: run((g_add, 4), (g_mid, 3), (g_fin, 5)), 3: run((g_add, 3), (g_mid, 2), (g_fin, 4)), 4: run((g_add, 2)), 5: run((s1,), (g_mid, 1), (g_fin, 3))}, lower[1], lower[2], to_output
    )

    sc[0].wait_recv()
    sc[0].wait_send()
    SL[...] = SL[...] + jnp.where(keep, St2[...], 0.0)
    zc = [send(SL, Sz.at[k - 1], s_s.at[1 + k], s_r.at[1 + k], (d, zk[k], t)) for k in range(1, nz)]
    g_add(1)
    g_mid(0)
    for cp in zc:
        cp.wait_recv()
    for cp in zc:
        cp.wait_send()
    tot = SL[...]
    for k in range(nz - 1):
        tot = tot + Sz[k]
    if direct:
        SL[...] = tot
        xc = send(SL, Sx, s_s.at[1 + nz], s_r.at[1 + nz], dx_dev)
    g_add(0)
    dx_done()
    dxo[...] = EB[3].astype(F32)
    dx_sent()
    g_fin(2)
    g_fin(1)
    if direct:
        xc.wait_recv()
        xc.wait_send()
        tot = tot + Sx[...]
    if direct:
        lane = lax.broadcasted_iota(jnp.int32, (8, DM), 1)
        for l in range(LAYERS):
            x = tot[l]
            own_cols = pltpu.roll(x, lax.rem(DM - slot * rw, DM), 1)
            sh_out[l] = own_cols[0:4, 0:rw]
            ga_out[l] = own_cols[4:6, 0:rw]
            mb_out[l] = own_cols[6:7, 0:rw]
            gq = pltpu.roll(x, DM - 384, 1)
            gv = jnp.where(lane < 128, pltpu.roll(x, DM - 64, 1), pltpu.roll(x, DM - 192, 1))
            back = lax.rem(DM - slot * (rw // 4), DM)
            qv_out[l, 0:1, :] = pltpu.roll(gq, back, 1)[7:8, 0 : rw // 4]
            qv_out[l, 1:2, :] = pltpu.roll(gv, back, 1)[7:8, 0 : rw // 4]
    else:
        gsm[...] = tot
    g_fin(0)
    w_sent(6)
    for cp in list(gx.values()):
        cp.wait_send()


def shards(dp, nz, nt_, x_in, cotangent, segment_ids, random_blocks, wqkv, wo, w1, w2, qv_bias, mid_bias, shifts, gains):
    rw = wqkv.shape[1]
    direct = dp == 2 and rw % 16 == 0
    TL, DM = x_in.shape[1], x_in.shape[2]
    length = segment_ids.shape[1]
    z = lax.axis_index("seq")
    slot = lax.axis_index("dp") * nz + z
    axes = ("dp", "seq")


    if direct:
        first_in = wqkv.transpose(0, 2, 1, 3)
        small_in = (wo, w1, w2.transpose(0, 2, 1), shifts, gains, mid_bias, qv_bias[:, :, 0])
    else:
        qw, kw, vw = [wqkv[:, :, i, :].reshape(LAYERS, rw, 3, 64) for i in range(3)]
        ot = wo.transpose(0, 2, 1).reshape(LAYERS, rw, 3, 64)
        attn = jnp.concatenate(
            [kw[:, :, 0], vw[:, :, 0], vw[:, :, 1], kw[:, :, 1], kw[:, :, 2], vw[:, :, 2],
             qw[:, :, 0], qw[:, :, 1], qw[:, :, 2], ot[:, :, 2], ot[:, :, 1], ot[:, :, 0]], axis=2)
        wl = jnp.stack([attn, w1, w2.transpose(0, 2, 1)], axis=1).astype(BF).reshape(3 * LAYERS, rw, DM)
        first_in = lax.all_gather(wl, axes, axis=1, tiled=True)
        sh = lax.all_gather(shifts.astype(BF), axes, axis=2, tiled=True).astype(F32)
        ga = lax.all_gather(gains.astype(BF), axes, axis=2, tiled=True).astype(F32)
        mb = lax.all_gather(mid_bias.astype(BF), axes, axis=2, tiled=True).astype(F32)
        qv = lax.all_gather(qv_bias[:, :, 0].astype(BF), axes, axis=2, tiled=True).astype(F32)
        bq, bv = qv[:, 0:1], qv[:, 1:2]
        gap = jnp.zeros((LAYERS, 1, 64), F32)
        kvb = jnp.concatenate([gap, bv[..., 0:128], gap, gap, bv[..., 128:192]], axis=2)
        fit = lambda v: jnp.pad(v, ((0, 0), (0, 0), (0, DM - v.shape[2])))
        sm = jnp.concatenate([sh, ga, mb, fit(bq), fit(kvb), jnp.zeros((LAYERS, 7, DM), F32)], axis=1)
        small_in = (sm,)

    QT = TL // 4
    L = LAYERS
    nslot = dp * nz if direct else 1
    vm = pl.BlockSpec(memory_space=pltpu.VMEM)
    dma = pltpu.SemaphoreType.DMA
    xr = nz * rw if direct else 16
    scratch = [
        pltpu.VMEM((3 * L, DM, DM), BF),
        pltpu.VMEM((nslot, L, 16, 128), F32),
        pltpu.VMEM((L, 16, DM), F32),
        pltpu.VMEM((L, length, DM), BF),
        pltpu.VMEM((L, length, 384), BF),
        pltpu.VMEM((L, TL, 384), BF),
        pltpu.VMEM((L, TL, 256), BF),
        pltpu.VMEM((3 * L, 1, TL), F32),
        pltpu.VMEM((L, TL, DM), BF),
        pltpu.VMEM((L, TL, DM), BF),
        pltpu.VMEM((L, TL, DM), BF),
        pltpu.VMEM((L, QT, DM), F32),
        pltpu.VMEM((L, QT, DM), F32),
        pltpu.VMEM((L, QT, 1), F32),
        pltpu.VMEM((L, QT, 1), F32),
        pltpu.VMEM((QT, DM), F32),
        pltpu.VMEM((QT, DM), F32),
        pltpu.VMEM((2 * L, TL, DM), BF),
        pltpu.VMEM((TL, DM), BF),
        pltpu.VMEM((2, 2, QT // 2, DM), BF),
        pltpu.VMEM((2, QT // 2, DM), BF),
        pltpu.VMEM((nz, TL, DM), BF),
        pltpu.VMEM((nz, 2, QT, DM), BF),
        pltpu.VMEM((nz, QT, DM), BF),
        pltpu.VMEM((L, nz, QT, DM), BF),
        pltpu.VMEM((3, 128, TL), F32),
        pltpu.VMEM((3, 1, TL), F32),
        pltpu.VMEM((3, 1, TL), F32),
        pltpu.VMEM((length, 384), BF),
        pltpu.VMEM((TL, DM), BF),
        pltpu.VMEM((TL, 256), BF),
        pltpu.VMEM((TL, 384), BF),
        pltpu.VMEM((3, 1, TL), F32),
        pltpu.VMEM((3 * L, xr, DM) if direct else (1, 16, 128), BF),
        pltpu.VMEM((3 * L, nz, rw, DM) if direct else (1, 1, 16, 128), BF),
        pltpu.VMEM((L, 8, DM), F32),
        pltpu.VMEM((L, 8, DM), F32),
        pltpu.VMEM((L, 8, DM), F32),
        pltpu.VMEM((nz - 1, L, 8, DM), F32),
        pltpu.VMEM((L, 8, DM), F32),
        pltpu.VMEM((L, 16, 128), F32),
        pltpu.VMEM((length, 128), F32),
        pltpu.VMEM((3, length // BLK, TL), F32),
        pltpu.VMEM((rw, DM) if direct else (8, 128), F32),
        pltpu.VMEM((3 * L, rw, DM) if direct else (1, 16, 128), BF),
        dma((7, 5 + nz)), dma((7, 2 * nz)),
        dma((L, 5 * nz)), dma((L, 4 * nz)),
        dma((8, 6)), dma((8, 6)),
        dma((6, 6)), dma((6, 6)),
        dma((L, 4 * nz)), dma((L, 4 * nz)),
        dma((6, 2 * nz)), dma((6, 2 * nz)),
        dma((2 + nz,)), dma((2 + nz,)),
    ]
    tokens = (jax.ShapeDtypeStruct((TL, DM), BF), jax.ShapeDtypeStruct((TL, DM), F32))
    if direct:
        grads = [(L, 3, rw, 192), (L, rw, 192), (L, rw, DM), (L, rw, DM), (L, 2, rw // 4), (L, 1, rw), (L, 4, rw), (L, 2, rw)]
        out_shape = tokens + tuple(jax.ShapeDtypeStruct(g, F32) for g in grads)
    else:
        out_shape = tokens + (jax.ShapeDtypeStruct((3 * L, DM, DM), BF), jax.ShapeDtypeStruct((L, 8, DM), F32))
    args = (first_in, x_in[0], cotangent[0], segment_ids, random_blocks[0]) + small_in
    results = pl.pallas_call(
        functools.partial(body, direct, nz, rw, len(args)),
        out_shape=out_shape,
        in_specs=[vm] * 4 + [pl.BlockSpec(memory_space=pltpu.SMEM)] + [vm] * len(small_in),
        out_specs=(vm,) * len(out_shape),
        scratch_shapes=scratch,
        compiler_params=pltpu.CompilerParams(collective_id=0, has_side_effects=True, vmem_limit_bytes=60 * 2**20),
        name="encoder",
    )(*args)
    act, dx = results[:2]
    if direct:
        gq, go, g1, g2, gqv, gmid, gsh, gga = results[2:]
        return (
            act[None],
            dx[None],
            gq.transpose(0, 2, 1, 3),
            go.transpose(0, 2, 1),
            g1,
            g2.transpose(0, 2, 1),
            gqv[:, :, None, :],
            gmid,
            gsh,
            gga,
        )
    gout, gsm = results[2:]
    gout = lax.psum_scatter(gout.astype(F32), axes, scatter_dimension=1, tiled=True).reshape(L, 3, rw, DM)
    gsm = lax.psum(gsm, "dp")
    ga, g1, g2 = gout[:, 0], gout[:, 1], gout[:, 2]
    pc = [ga[:, :, i * 64 : (i + 1) * 64] for i in range(12)]
    gq = jnp.concatenate([pc[6], pc[7], pc[8]], axis=2)
    gk = jnp.concatenate([pc[0], pc[3], pc[4]], axis=2)
    gv = jnp.concatenate([pc[1], pc[2], pc[5]], axis=2)
    go = jnp.concatenate([pc[11], pc[10], pc[9]], axis=2).transpose(0, 2, 1)
    sl = lax.dynamic_slice_in_dim(gsm[:, 0:7], slot * rw, rw, axis=2)
    dbq = gsm[:, 7, 384:576]
    dbv = jnp.concatenate([gsm[:, 7, 64:192], gsm[:, 7, 320:384]], axis=1)
    qv = lax.dynamic_slice_in_dim(jnp.stack([dbq, dbv], axis=1), slot * (rw // 4), rw // 4, axis=2)
    return (
        act[None],
        dx[None],
        jnp.stack([gq, gk, gv], axis=2),
        go,
        g1,
        g2.transpose(0, 2, 1),
        qv[:, :, None, :],
        sl[:, 6:7],
        sl[:, 0:4],
        sl[:, 4:6],
    )


def solution(mesh):
    both = ("dp", "seq")
    weights = (
        P(None, both, None, "tensor"),
        P(None, "tensor", both),
        P(None, both, "tensor"),
        P(None, "tensor", both),
        P(None, None, "tensor", both),
        P(None, "tensor", both),
        P(None, None, both),
        P(None, None, both),
    )
    tokens = P("dp", "seq", None)
    in_specs = (tokens, tokens, P("dp", None), P("dp", "tensor", None, None)) + weights
    out_specs = (tokens, tokens) + weights
    fn = functools.partial(shards, mesh.shape["dp"], mesh.shape["seq"], mesh.shape["tensor"])
    return jax.shard_map(fn, mesh=mesh, in_specs=in_specs, out_specs=out_specs, check_vma=False)
```

```python
import functools

import jax
import jax.numpy as jnp
from jax import lax
from jax.experimental import pallas as pl
from jax.experimental.pallas import tpu as pltpu
from jax.sharding import PartitionSpec as P

BLK = 64
LAYERS = 2
EPS = 1e-06
NEG = -1e30
BF = jnp.bfloat16
F32 = jnp.float32
MESH = pl.DeviceIdType.MESH


def nn(a, b):
    return lax.dot_general(a, b, (((1,), (0,)), ((), ())), preferred_element_type=F32)


def nt(a, b):
    return lax.dot_general(a, b, (((1,), (1,)), ((), ())), preferred_element_type=F32)


def tn(a, b):
    return lax.dot_general(a, b, (((0,), (0,)), ((), ())), preferred_element_type=F32)


def normalise(z):
    mu = jnp.mean(z, axis=-1, keepdims=True)
    c = z - mu
    rs = lax.rsqrt(jnp.mean(c * c, axis=-1, keepdims=True) + EPS)
    return c * rs, rs


def norm_back(dn, n, rs):
    return (dn - jnp.mean(dn, axis=-1, keepdims=True) - n * jnp.mean(dn * n, axis=-1, keepdims=True)) * rs


def low_lanes(shape):
    return lax.broadcasted_iota(jnp.int32, shape, len(shape) - 1) % 128 < 64


def body(
    direct, nz, rw, n_in, *refs
):
    ins, refs = refs[:n_in], refs[n_in:]
    if direct:
        q_in, xin, cot, seg, rnd, o_in, w1_in, w2_in, sh_in, ga_in, mb_in, qv_in = ins
        act, dxo, gq_out, go_out, g1_out, g2_out, gsm = refs[:7]
        refs = refs[7:]
    else:
        wl, xin, cot, seg, rnd, sm = ins
        act, dxo, gout, gsm = refs[:4]
        refs = refs[4:]
    (
    W, SG, SV, XA, KV, QP, OO, LSE, H1, DG, G, N1, N2, RS1, RS2, XR, DZ, EB,
    PB, rsib, ry, DXP, xsib, xy, xz, ACC, MX, LS, DKV, DU, DQ, DO, DEL, XRV, ZRV, SL, St1, St2, Sz, Sx,
        SMS, segk, segqm, SA, WL,
        wg_s, wg_r, ax_s, ax_r, a4_s, a4_r, r4_s, r4_r, r16_s, r16_r, g_s, g_r, s_s, s_r,
    ) = refs
    if direct:
        sm, wl = SMS, WL
    d, z, t = lax.axis_index("dp"), lax.axis_index("seq"), lax.axis_index("tensor")
    c = t % 2
    y = t // 2
    sib, yp = 2 * y + (1 - c), 2 * (1 - y) + c
    DM = XA.shape[2]
    TL = xin.shape[0]
    QT = TL // 4
    HALF = TL // 2
    dsib, dyp = (d, z, sib), (d, z, yp)
    zk = [lax.rem(z + k, nz) for k in range(nz)]
    upper = z // 2
    edge = (1 - z) * (1 - upper) + (z - 2) * upper
    inner = 1 - edge
    ck = [z] + [o + upper * (nz - 1 - 2 * o) for o in (edge, 2, 3)]

    bar = pltpu.get_barrier_semaphore()
    peers = [dsib, dyp] + [(d, zk[k], t) for k in range(1, nz)]
    if direct:
        dx_dev = (1 - d, z, t)
        peers.append(dx_dev)
    for p in peers:
        pl.semaphore_signal(bar, inc=1, device_id=p, device_id_type=MESH)
    pl.semaphore_wait(bar, len(peers))

    def send(src, dst, ss, rs, dev):
        cp = pltpu.make_async_remote_copy(src_ref=src, dst_ref=dst, send_sem=ss, recv_sem=rs, device_id=dev, device_id_type=MESH)
        cp.start()
        return cp

    def rows(start, n):
        return pl.ds(pl.multiple_of(start, n if n % 16 == 0 else 16), n)

    own = rows(t * QT, QT)

    def copy_to(src, dst, ss, rs, dev):
        return pltpu.make_async_remote_copy(src_ref=src, dst_ref=dst, send_sem=ss, recv_sem=rs, device_id=dev, device_id_type=MESH)

    if direct:
        slot = d * nz + z

        def w_ref(p, k):
            if p == 6:
                return SG.at[d * nz + k]
            return W.at[p, rows((d * nz + k) * rw, rw), :]

        def w_own(p):
            src = sm if p == 6 else wl.at[p]
            dst = w_ref(p, z)
            out = []
            for i, step in enumerate((1, 2, -1, -2)):
                ok = z + step < nz if step > 0 else z + step >= 0
                out.append((ok, copy_to(src, dst, wg_s.at[p, i], wg_r.at[p, z], (d, z + step, t))))
            return out

        def w_over(p, k):
            return copy_to(w_ref(p, k), w_ref(p, k), wg_s.at[p, 5 + k], wg_r.at[p, nz + k], dx_dev)

        def w_hop(p):
            return copy_to(w_ref(p, ck[3]), w_ref(p, ck[3]), wg_s.at[p, 4], wg_r.at[p, ck[3]], (d, nz - 1 - ck[3], t))

        def w_wait(p, k):
            copy_to(w_ref(p, k), w_ref(p, k), wg_s.at[p, 4], wg_r.at[p, k], dx_dev).wait_recv()

        def w_a(p):
            if p == 6:
                SG[slot] = sm[...]
            else:
                W[p, rows(slot * rw, rw), :] = wl[p]
            for ok, cp in w_own(p):
                pl.when(ok)(cp.start)

        def w_o(p):
            src = sm if p == 6 else wl.at[p]
            copy_to(src, w_ref(p, z), wg_s.at[p, 5 + z], wg_r.at[p, nz + z], dx_dev).start()

        def w_b(p):
            @pl.when(inner == 1)
            def _():
                w_wait(p, ck[3])
                w_hop(p).start()

        def w_c(p):
            for k in ck[1:3]:
                w_wait(p, k)
                w_over(p, k).start()

        def w_d(p):
            @pl.when(edge == 1)
            def _():
                w_wait(p, ck[3])

            w_over(p, ck[3]).start()

        def w_fin(p):
            for k in range(nz):
                w_over(p, k).wait_recv()

        def w_sent(p):
            for ok, cp in w_own(p):
                pl.when(ok)(cp.wait_send)

            @pl.when(inner == 1)
            def _():
                w_hop(p).wait_send()

            for k in ck:
                w_over(p, k).wait_send()
    else:

        def w_a(p):
            if p == 6:
                SV[...] = sm[...]
            else:
                W[p] = wl[p]

        def w_b(p):
            pass

        w_o = w_c = w_d = w_fin = w_sent = w_b

    ST = QT // 2

    def own_part(b):
        return rows(t * QT + b * ST, ST)

    def ag4(i, ref):
        st = {}

        def put(b):
            r = ref.at[own_part(b), :]
            st["c", b] = send(r, r, a4_s.at[i, b], a4_r.at[i, b], dsib)
            st["y", b] = send(r, r, a4_s.at[i, 2 + b], a4_r.at[i, 2 + b], dyp)

        def fin():
            for b in range(2):
                st["y", b].wait_recv()
                r = ref.at[rows(yp * QT + b * ST, ST), :]
                st["o", b] = send(r, r, a4_s.at[i, 4 + b], a4_r.at[i, 4 + b], dsib)
            for b in range(2):
                st["c", b].wait_recv()
                st["o", b].wait_recv()

        def sent():
            for cp in st.values():
                cp.wait_send()

        return put, fin, sent

    def rs4(i, part, consume, filler=None):
        r0 = [(1 - y) * HALF, y * HALF]
        st = {}
        for k in range(2):
            PB[rows(r0[k], HALF), :] = part(rows(r0[k], HALF)).astype(BF)
            for b in range(2):
                st["c", k, b] = send(
                    PB.at[rows(r0[k] + (1 - c) * QT + b * ST, ST), :], rsib.at[k, b], r4_s.at[i, 2 * k + b], r4_r.at[i, 2 * k + b], dsib
                )
            if k == 0:
                for b in range(2):
                    st["c", 0, b].wait_recv()
                    mine = rows(r0[0] + c * QT + b * ST, ST)
                    PB[mine, :] = (PB[mine, :].astype(F32) + rsib[0, b].astype(F32)).astype(BF)
                    st["y", b] = send(PB.at[mine, :], ry.at[b], r4_s.at[i, 4 + b], r4_r.at[i, 4 + b], dyp)
        if filler is not None:
            filler()
        for b in range(2):
            st["c", 1, b].wait_recv()
            st["y", b].wait_recv()
            consume(b, PB[own_part(b), :].astype(F32) + rsib[1, b].astype(F32) + ry[b].astype(F32))
        for cp in st.values():
            cp.wait_send()

    def xgather(l):
        st = {}

        def src_rows(k, q):
            return XA.at[l, rows(k * TL + q * QT, QT), :]

        def along(k, to, kind):
            r = src_rows(k, t)
            return copy_to(r, r, ax_s.at[l, kind * nz + k], ax_r.at[l, k], (d, to, t))

        def hop(j):
            right = (z - ck[j] + nz) // nz
            to = z - 1 + 2 * right
            return (to >= 0) & (to < nz), along(ck[j], to, 0)

        ends = [(z < nz - 1, along(z, z + 1, 0)), (z > 0, along(z, z - 1, 1))]

        def local(j):
            r = src_rows(ck[j], t)
            st["y", j] = send(r, r, ax_s.at[l, 2 * nz + ck[j]], ax_r.at[l, nz + ck[j]], dyp)
            st["c", j] = send(r, r, ax_s.at[l, 3 * nz + ck[j]], ax_r.at[l, 2 * nz + ck[j]], dsib)

        def start():
            for ok, cp in ends:
                pl.when(ok)(cp.start)
            if l > 0:
                local(0)

        def arrive(j):
            along(ck[j], z, 0).wait_recv()
            ok, cp = hop(j)
            pl.when(ok)(cp.start)
            local(j)

        def fwd(j):
            st["y", j].wait_recv()
            r = src_rows(ck[j], yp)
            st["c2", j] = send(r, r, ax_s.at[l, 4 * nz + ck[j]], ax_r.at[l, 3 * nz + ck[j]], dsib)

        def fin(j):
            st["c", j].wait_recv()
            st["c2", j].wait_recv()

        def sent():
            for ok, cp in ends + [hop(j) for j in range(1, nz)]:
                pl.when(ok)(cp.wait_send)
            for cp in st.values():
                cp.wait_send()

        return start, arrive, fwd, fin, sent

    def small(l, r):
        return SV[l, r : r + 1, :]

    def kv_proj(l, j):
        r = rows(ck[j] * TL, TL)
        bias = SV[l, 8:9, 0:384]
        KV[l, r, :] = (nn(XA[l, r, :], W[3 * l, :, 0:384]) + bias).astype(BF)

    def q_proj(l):
        bias = SV[l, 7:8, 0:256]
        q = (nn(XA[l, rows(z * TL, TL), :], W[3 * l, :, 384:640]) + bias).astype(BF).astype(F32) * 0.125
        a, b = q[:, 0:128], q[:, 128:256]
        lo = low_lanes(a.shape)
        QP[l, :, 0:128] = jnp.where(lo, a, 0.0).astype(BF)
        QP[l, :, 128:256] = jnp.where(lo, 0.0, a).astype(BF)
        QP[l, :, 256:384] = jnp.where(lo, b, 0.0).astype(BF)

    nb = TL // BLK

    def masked_scores(l, h, hl, r, j):
        kv = KV[l, r, pl.ds(hl, 128)]
        s = nt(kv, QP[l, :, pl.ds(hl, 128)])
        sq = segqm[h, pl.ds(pl.multiple_of(ck[j] * nb, nb), nb), :]
        sk = segk[r, :]
        parts = []
        for b in range(nb):
            skb = jnp.concatenate([sk[b * BLK : (b + 1) * BLK]] * (TL // 128), axis=1)
            parts.append(jnp.where(skb == sq[b : b + 1], s[b * BLK : (b + 1) * BLK], NEG))
        return kv, jnp.concatenate(parts, axis=0)

    def attend(l, j):
        r = rows(ck[j] * TL, TL)

        def head(h, carry):
            hl = pl.multiple_of(h * 128, 128)
            kv, s = masked_scores(l, h, hl, r, j)
            top = jnp.max(s, axis=0, keepdims=True)
            if j > 0:
                before = MX[h]
                top = jnp.maximum(before, top)
            e = jnp.exp(s - top)
            total = jnp.sum(e, axis=0, keepdims=True)
            o = tn(kv, e.astype(BF))
            if j > 0:
                a = jnp.exp(before - top)
                total = total + LS[h] * a
                o = o + ACC[h] * a
            MX[h] = top
            LS[h] = total
            ACC[h] = o
            return carry

        lax.fori_loop(0, 3, head, 0)

    def attend_end(l):
        o = []
        for h in range(3):
            LSE[3 * l + h] = MX[h] + jnp.log(LS[h])
            o.append((ACC[h] / LS[h]).T)
        lo = low_lanes(o[0].shape)
        OO[l, :, 0:128] = jnp.where(lo, 0.0, o[2]).astype(BF)
        OO[l, :, 128:256] = jnp.where(lo, o[1], o[0]).astype(BF)

    def gelu_parts(u):
        k = 0.7978845608028654
        th = jnp.tanh(k * (u + 0.044715 * u * u * u))
        g = 0.5 * u * (1.0 + th)
        dg = 0.5 * (1.0 + th) + 0.5 * u * (1.0 - th * th) * (k * (1.0 + 3 * 0.044715 * u * u))
        return g, dg

    seen = []

    def forward(l, bg, then):
        start, arrive, fwd, fin, sent = xg[l]
        if l > 0:
            start()
            arrive(1)
            fwd(0)
            fin(0)
            w_fin(3)
        q_proj(l)
        kv_proj(l, 0)
        arrive(2)
        fwd(1)
        attend(l, 0)
        arrive(3)
        fwd(2)
        bg[0]()
        for j in range(1, nz):
            fin(j)
            kv_proj(l, j)
            attend(l, j)
            if j == 1:
                fwd(3)
            bg[j]()
        attend_end(l)
        sent()
        wo = W[3 * l, :, 512:768]
        put, done, gone = ag4(4 * l, H1.at[l])

        def first(b, r):
            part = pl.ds(b * ST, ST)
            z1 = XR[part, :] + r + small(l, 0)
            n1, rs1 = normalise(z1)
            N1[l, part, :] = n1
            RS1[l, part, :] = rs1
            h1 = n1 * small(l, 4) + small(l, 1)
            H1[l, own_part(b), :] = h1.astype(BF)
            XR[part, :] = h1
            put(b)

        rs4(3 * l, lambda rr: nt(OO[l, rr, :], wo), first, bg[4])
        bg[5]()
        done()
        w_fin(3 * l + 1)

        def ffn(rr):
            u = nn(H1[l, rr, :], W[3 * l + 1]) + small(l, 6)
            g, dg = gelu_parts(u)
            DG[l, rr, :] = dg.astype(BF)
            gb = g.astype(BF)
            G[l, rr, :] = gb
            if l not in seen:
                seen.append(l)
                w_fin(3 * l + 2)
            return nt(gb, W[3 * l + 2])

        def fill():
            gone()
            bg[6]()

        def second(b, r):
            part = pl.ds(b * ST, ST)
            z2 = XR[part, :] + r + small(l, 2)
            n2, rs2 = normalise(z2)
            N2[l, part, :] = n2
            RS2[l, part, :] = rs2
            out = n2 * small(l, 5) + small(l, 3)
            XR[part, :] = out
            then(b, out)

        rs4(3 * l + 1, ffn, second, fill)
        bg[7]()

    gx = {}

    if direct:

        def g_start(p):
            for k in ck[::-1]:
                gx[p, len(gx)] = send(
                    W.at[p, rows(((1 - d) * nz + k) * rw, rw), :], XRV.at[p, rows(k * rw, rw), :], g_s.at[p, k], g_r.at[p, k], dx_dev
                )

        def g_slot(p, k):
            return W.at[p, rows((d * nz + k) * rw, rw), :]

        def g_to(p, part, to, slot_there):
            return copy_to(g_slot(p, part), ZRV.at[p, slot_there], g_s.at[p, nz + part], g_r.at[p, nz + slot_there], (d, to, t))

        def g_landed(p, k):
            x = ZRV.at[p, k]
            copy_to(x, x, g_s.at[p, nz + k], g_r.at[p, nz + k], dx_dev).wait_recv()

        def g_far(p):
            return lambda: g_to(p, ck[3], ck[1], ck[1]), lambda: g_to(p, ck[3], ck[3], z)

        def g_mid(p):
            for k in ck[::-1]:
                r = g_slot(p, k)
                x = XRV.at[p, rows(k * rw, rw), :]
                copy_to(x, x, g_s.at[p, k], g_r.at[p, k], dx_dev).wait_recv()
                r[...] = (r[...].astype(F32) + x[...].astype(F32)).astype(BF)
                if k is ck[3]:
                    pl.when(edge == 1)(g_far(p)[0]().start)
                elif k is not z:
                    g_to(p, k, k, z).start()

        def g_add(p):
            @pl.when(inner == 1)
            def _():
                g_landed(p, z)
                r = g_slot(p, ck[3])
                r[...] = (r[...].astype(F32) + ZRV[p, z].astype(F32)).astype(BF)
                g_far(p)[1]().start()

        def g_fin(p):
            l = p // 3
            goal = (SA, g1_out.at[l], g2_out.at[l])[p % 3]
            tot = g_slot(p, z)[...].astype(F32)
            for k in ck[1:3]:
                g_landed(p, k)
                tot = tot + ZRV[p, k].astype(F32)
            goal[...] = tot

            @pl.when(inner == 1)
            def _():
                g_landed(p, ck[3])
                goal[...] = goal[...] + ZRV[p, ck[3]].astype(F32)
                g_far(p)[1]().wait_send()

            pl.when(edge == 1)(g_far(p)[0]().wait_send)
            for k in ck[1:3]:
                g_to(p, k, k, z).wait_send()
            if p % 3 == 0:
                tile = [SA[:, 128 * i : 128 * (i + 1)] for i in range(6)]
                lo = low_lanes(tile[0].shape)
                gq_out[l, 0, :, 0:128] = tile[3]
                gq_out[l, 0, :, 128:192] = tile[4][:, 0:64]
                gq_out[l, 1, :, 0:128] = jnp.where(lo, tile[0], tile[1])
                gq_out[l, 1, :, 128:192] = tile[2][:, 0:64]
                gq_out[l, 2, :, 0:128] = pltpu.roll(jnp.where(lo, tile[1], tile[0]), 64, 1)
                gq_out[l, 2, :, 128:192] = pltpu.roll(tile[2], 64, 1)[:, 0:64]
                go_out[l, :, 0:128] = pltpu.roll(tile[5], 64, 1)
                go_out[l, :, 128:192] = pltpu.roll(tile[4], 64, 1)[:, 0:64]
    else:

        def g_start(p):
            gout[p] = W[p]

        def g_mid(p):
            pass

        g_add = g_fin = g_mid

    def accumulate(l, row, b, v):
        v = jnp.sum(v, axis=0, keepdims=True)
        SL[l, row : row + 1, :] = v if b == 0 else SL[l, row : row + 1, :] + v

    def second_back(l):
        put, done, gone = ag4(4 * l + 2, EB.at[2 * l + 1])

        def one(b, dy):
            part = pl.ds(b * ST, ST)
            n2 = N2[l, part, :]
            accumulate(l, 3, b, dy)
            accumulate(l, 5, b, dy * n2)
            dz2 = norm_back(dy * small(l, 5), n2, RS2[l, part, :])
            accumulate(l, 2, b, dz2)
            DZ[part, :] = dz2
            EB[2 * l + 1, own_part(b), :] = dz2.astype(BF)
            put(b)

        return one, done, gone

    def backward(l, bg, done, gone, then):
        bg.get(0, nop)()
        done()

        def ffn_back(rr):
            dgm = nn(EB[2 * l + 1, rr, :], W[3 * l + 2])
            du = (dgm * DG[l, rr, :].astype(F32)).astype(BF)
            DU[rr, :] = du
            return nt(du, W[3 * l + 1])

        def fill():
            gone()
            w_sent(3 * l + 2)
            w_sent(3 * l + 1)
            W[3 * l + 2] = tn(EB[2 * l + 1], G[l]).astype(BF)
            g_start(3 * l + 2)
            W[3 * l + 1] = tn(H1[l], DU[...]).astype(BF)
            g_start(3 * l + 1)
            SL[l, 6:7, :] = jnp.sum(DU[...].astype(F32), axis=0, keepdims=True)
            bg.get(1, nop)()

        put, done1, gone1 = ag4(4 * l + 3, EB.at[2 * l])

        def first_back(b, r):
            part = pl.ds(b * ST, ST)
            dh1 = DZ[part, :] + r
            n1 = N1[l, part, :]
            dz1 = norm_back(dh1 * small(l, 4), n1, RS1[l, part, :])
            DZ[part, :] = dz1
            EB[2 * l, own_part(b), :] = dz1.astype(BF)
            put(b)
            accumulate(l, 1, b, dh1)
            accumulate(l, 4, b, dh1 * n1)
            accumulate(l, 0, b, dz1)

        rs4(3 * l + 2, ffn_back, first_back, fill)
        bg.get(2, nop)()
        done1()
        doo = nn(EB[2 * l], W[3 * l, :, 512:768]).astype(BF).astype(F32)
        lo = low_lanes((TL, 128))
        da, db = doo[:, 0:128], doo[:, 128:256]
        DO[:, 0:128] = jnp.where(lo, 0.0, db).astype(BF)
        DO[:, 128:256] = jnp.where(lo, db, 0.0).astype(BF)
        DO[:, 256:384] = jnp.where(lo, 0.0, da).astype(BF)
        prod = (doo * OO[l].astype(F32)).T
        DEL[0] = jnp.sum(prod[192:256], axis=0, keepdims=True)
        DEL[1] = jnp.sum(prod[128:192], axis=0, keepdims=True)
        DEL[2] = jnp.sum(prod[64:128], axis=0, keepdims=True)

        xs = {}
        order = list(range(nz - 1, 0, -1)) + [0]

        def attend_back(j, first):
            r = rows(ck[j] * TL, TL)

            def head(h, carry):
                hl = pl.multiple_of(h * 128, 128)
                kv, s = masked_scores(l, h, hl, r, j)
                q = QP[l, :, pl.ds(hl, 128)]
                do = DO[:, pl.ds(hl, 128)]
                p = jnp.exp(s - LSE[3 * l + h])
                dp = nt(kv, do)
                ds = (p * (dp - DEL[h])).astype(BF)
                DKV[r, pl.ds(hl, 128)] = (nn(ds, q) + nn(p.astype(BF), do)).astype(BF)
                dq = tn(kv, ds)
                if first:
                    ACC[h] = dq
                else:
                    ACC[h] = ACC[h] + dq
                return carry

            lax.fori_loop(0, 3, head, 0)

        def dx_parts(j):
            for k in range(2):
                r0 = [(1 - y) * HALF, y * HALF][k]
                v = nt(DKV[rows(ck[j] * TL + r0, HALF), :], W[3 * l, :, 0:384])
                if j == 0:
                    v = v + nt(DQ[rows(r0, HALF), :], W[3 * l, :, 384:640])
                DXP[j, rows(r0, HALF), :] = v.astype(BF)
                xs["c", j, k] = send(DXP.at[j, rows(r0 + (1 - c) * QT, QT), :], xsib.at[j, k], r16_s.at[l, 3 * j + k], r16_r.at[l, 3 * j + k], dsib)

        def dx_y(j):
            xs["c", j, 0].wait_recv()
            mine = rows(yp * QT, QT)
            DXP[j, mine, :] = (DXP[j, mine, :].astype(F32) + xsib[j, 0].astype(F32)).astype(BF)
            xs["y", j] = send(DXP.at[j, mine, :], xy.at[j], r16_s.at[l, 3 * j + 2], r16_r.at[l, 3 * j + 2], dyp)

        def dx_z(j):
            xs["c", j, 1].wait_recv()
            xs["y", j].wait_recv()
            tot = DXP[j, own, :].astype(F32) + xsib[j, 1].astype(F32) + xy[j].astype(F32)
            if j == 0:
                return tot
            DXP[j, own, :] = tot.astype(BF)
            if j == nz - 1:
                pl.when(edge == 1)(dx_far()[0]().start)
            else:
                dx_to(j, ck[j], z).start()

        def dx_to(j, to, there):
            return copy_to(DXP.at[j, own, :], xz.at[l, there], r16_s.at[l, 3 * nz + ck[j]], r16_r.at[l, 3 * nz + there], (d, to, t))

        def dx_far():
            return lambda: dx_to(nz - 1, ck[1], ck[1]), lambda: dx_to(nz - 1, ck[nz - 1], z)

        def dx_landed(k):
            x = xz.at[l, k]
            copy_to(x, x, r16_s.at[l, 3 * nz + k], r16_r.at[l, 3 * nz + k], dsib).wait_recv()

        def dx_add():
            @pl.when(inner == 1)
            def _():
                dx_landed(z)
                j = nz - 1
                DXP[j, own, :] = (DXP[j, own, :].astype(F32) + xz[l, z].astype(F32)).astype(BF)
                dx_far()[1]().start()

        for i, j in enumerate(order):
            attend_back(j, i == 0)
            if i >= 2:
                dx_z(order[i - 2])
            if i < 2:
                bg.get(3 + i, nop)()
            if j == 0:
                a01 = ACC[0]
                hi = lax.broadcasted_iota(jnp.int32, a01.shape, 0) < 64
                DQ[:, 0:128] = (jnp.where(hi, a01, ACC[1]).T * 0.125).astype(BF)
                DQ[:, 128:256] = (jnp.where(hi, ACC[2], 0.0).T * 0.125).astype(BF)
            dx_parts(j)
            dx_y(j)
        gone1()
        w_sent(3 * l)
        xown = XA[l, rows(z * TL, TL), :]
        gq = tn(xown, DQ[...])
        go = tn(EB[2 * l], OO[l])
        gkv = tn(XA[l], DKV[...])
        SL[l, 7:8, 0:384] = jnp.sum(DKV[...].astype(F32), axis=0, keepdims=True)
        SL[l, 7:8, 384:640] = jnp.sum(DQ[...].astype(F32), axis=0, keepdims=True)
        SL[l, 7:8, 640:768] = jnp.zeros((1, 128), F32)
        W[3 * l, :, 0:384] = gkv.astype(BF)
        W[3 * l, :, 384:512] = gq[:, 0:128].astype(BF)
        W[3 * l, :, 512:640] = (gq[:, 128:256] + go[:, 0:128]).astype(BF)
        W[3 * l, :, 640:768] = go[:, 128:256].astype(BF)
        g_start(3 * l)
        dx_z(order[nz - 2])
        dx_add()
        bg.get(5, nop)()
        DZ[...] = DZ[...] + dx_z(0)
        for k in ck[1:3]:
            dx_landed(k)
            DZ[...] = DZ[...] + xz[l, k].astype(F32)

        @pl.when(inner == 1)
        def _():
            dx_landed(ck[3])
            DZ[...] = DZ[...] + xz[l, ck[3]].astype(F32)
            dx_far()[1]().wait_send()

        then(DZ[...])
        pl.when(edge == 1)(dx_far()[0]().wait_send)
        for j in (1, 2):
            dx_to(j, ck[j], z).wait_send()
        for cp in xs.values():
            cp.wait_send()

    xg = [xgather(0), xgather(1)]

    def pack(p):
        l = p // 3
        if p % 3:
            WL[p] = (w1_in, w2_in)[p % 3 - 1][l].astype(BF)
            return
        eye = lax.broadcasted_iota(jnp.int32, (rw, rw), 0) == lax.broadcasted_iota(jnp.int32, (rw, rw), 1)
        ot = nt(jnp.where(eye, 1.0, 0.0).astype(BF), o_in[l].astype(BF))

        def split(v):
            last = v[:, 128:192]
            return v[:, 0:128], jnp.concatenate([last, last], axis=1)

        (qa, qb), (ka, kb), (va, vb) = [split(q_in[l, i]) for i in range(3)]
        oa, ob = split(ot)
        lo = low_lanes(qa.shape)
        va = pltpu.roll(va, 64, 1)
        tiles = (
            jnp.where(lo, ka, va), jnp.where(lo, va, ka), jnp.where(lo, kb, vb), qa, jnp.where(lo, qb, ob), pltpu.roll(oa, 64, 1),
        )
        for i, v in enumerate(tiles):
            WL[p, :, 128 * i : 128 * (i + 1)] = v.astype(BF)

    def masks():
        length = seg.shape[1]
        nblk = length // BLK
        for i in range(length // 128):
            row = seg[:, 128 * i : 128 * (i + 1)].astype(F32)
            segk[128 * i : 128 * (i + 1), :] = jnp.broadcast_to(row, (128, 128)).T
        segq = seg[:, pl.ds(pl.multiple_of(z * TL, TL), TL)].astype(F32)
        block = lax.broadcasted_iota(jnp.int32, (1, TL), 1) // BLK
        key = lax.broadcasted_iota(jnp.int32, (nblk, TL), 0)
        away = key - (z * nb + lax.broadcasted_iota(jnp.int32, (nblk, TL), 1) // BLK)
        near = (away >= -1) & (away <= 1) | (key == 0) | (key == nblk - 1)
        for h in range(3):
            ok = near
            for r in range(rnd.shape[2]):
                pick = jnp.zeros((1, TL), jnp.int32)
                for b in range(nb):
                    pick = jnp.where(block == b, rnd[h, z * nb + b, r], pick)
                ok = ok | (key == pick)
            segqm[h] = jnp.where(ok, segq, -1.0)

    def run(*steps):
        def go():
            for fn, *a in steps:
                fn(*a)

        return go

    nop = run()
    if direct:
        SMS[...] = jnp.zeros_like(SMS)
        for l in range(LAYERS):
            SMS[l, 0:4, 0:rw] = sh_in[l].astype(BF).astype(F32)
            SMS[l, 4:6, 0:rw] = ga_in[l].astype(BF).astype(F32)
            SMS[l, 6:7, 0:rw] = mb_in[l].astype(BF).astype(F32)
            SMS[l, 8:10, 0 : rw // 4] = qv_in[l].astype(BF).astype(F32)
    if direct:
        pack(0)
    w_o(6)
    w_o(0)
    w_a(6)
    w_a(0)
    XA[0, rows(z * TL, TL), :] = xin[...]
    XR[...] = xin[own, :].astype(F32)
    if direct:
        for p in range(1, 3 * LAYERS):
            pack(p)
    w_o(1)
    w_o(2)
    w_b(6)
    w_b(0)
    w_c(6)
    w_c(0)
    xg[0][0]()
    masks()
    w_d(6)
    w_d(0)
    for p in (3, 4, 5):
        w_o(p)
    w_fin(6)
    if direct:
        wide = DM - 128
        nslot = SG.shape[0]
        for l in range(LAYERS):
            acc = jnp.zeros((16, DM), F32)
            cmp_ = jnp.zeros((8, DM), F32)
            for s_ in range(nslot):
                piece = jnp.concatenate([SG[s_, l], jnp.zeros((16, wide), F32)], axis=1)
                acc = acc + (pltpu.roll(piece, s_ * rw, 1) if s_ else piece)
                cmp_ = cmp_ + (pltpu.roll(piece[8:16], s_ * (rw // 4), 1) if s_ else piece[8:16])
            bq, bv = cmp_[0:1], cmp_[1:2]
            lane = lax.broadcasted_iota(jnp.int32, (1, DM), 1)
            kvb = jnp.where((lane >= 64) & (lane < 192), pltpu.roll(bv, 64, 1), 0.0) + jnp.where(
                (lane >= 320) & (lane < 384), pltpu.roll(bv, 192, 1), 0.0
            )
            SV[l, 0:8, :] = acc[0:8]
            SV[l, 7:8, :] = bq
            SV[l, 8:9, :] = kvb
    xg[0][1](1)
    w_fin(0)
    def next_input(b, v):
        XA[1, rows(z * TL + t * QT + b * ST, ST), :] = v.astype(BF)

    forward(0, [
        run((w_a, 1)),
        run(),
        run((w_b, 1)),
        run((w_a, 2), (w_c, 1)),
        run((w_d, 1), (w_b, 2), (w_a, 3)),
        run((w_c, 2), (w_d, 2)),
        run((w_b, 3), (w_a, 4), (w_c, 3)),
        run((w_d, 3)),
    ], next_input)
    start_back, done, gone = second_back(1)

    def last_output(b, v):
        start_back(b, cot[own_part(b), :].astype(F32))
        EB[0, own_part(b), :] = v.astype(BF)

    forward(1, [
        run((w_b, 4)),
        run((w_c, 4)),
        run((w_d, 4)),
        run((w_a, 5)),
        run((w_b, 5)),
        run((w_c, 5), (w_d, 5)),
        run(),
        run(),
    ], last_output)
    act_put, act_done, act_sent = ag4(1, EB.at[0])

    def act_start():
        act_put(0)
        act_put(1)

    def act_end():
        act_done()
        act[...] = EB[0]
        act_sent()

    lower = second_back(0)

    def to_lower(dy):
        for b in range(2):
            lower[0](b, dy[b * ST : (b + 1) * ST])

    backward(1, {0: run((act_start,)), 1: run((act_end,)), 3: run((g_mid, 5)), 4: run((g_add, 5)), 5: nop}, done, gone, to_lower)

    keep = lax.broadcasted_iota(jnp.int32, SL.shape, 1) < 6

    def s1():
        cp = send(SL, St1, s_s.at[0], s_r.at[0], dsib)
        cp.wait_recv()
        cp.wait_send()
        SL[...] = SL[...] + jnp.where(keep, St1[...], 0.0)
        sc.append(send(SL, St2, s_s.at[1], s_r.at[1], dyp))

    sc = []
    dx_put, dx_done, dx_sent = ag4(5, EB.at[3])

    def to_output(dx):
        EB[3, own, :] = dx.astype(BF)
        dx_put(0)
        dx_put(1)

    backward(
        0, {0: run((g_mid, 4)), 1: run((g_add, 4), (g_mid, 3), (g_fin, 5)), 3: run((g_add, 3), (g_mid, 2), (g_fin, 4)), 4: run((g_add, 2)), 5: run((s1,), (g_mid, 1), (g_fin, 3))}, lower[1], lower[2], to_output
    )

    sc[0].wait_recv()
    sc[0].wait_send()
    SL[...] = SL[...] + jnp.where(keep, St2[...], 0.0)
    zc = [send(SL, Sz.at[k - 1], s_s.at[1 + k], s_r.at[1 + k], (d, zk[k], t)) for k in range(1, nz)]
    g_add(1)
    g_mid(0)
    for cp in zc:
        cp.wait_recv()
    for cp in zc:
        cp.wait_send()
    tot = SL[...]
    for k in range(nz - 1):
        tot = tot + Sz[k]
    if direct:
        SL[...] = tot
        xc = send(SL, Sx, s_s.at[1 + nz], s_r.at[1 + nz], dx_dev)
    g_add(0)
    dx_done()
    dxo[...] = EB[3].astype(F32)
    dx_sent()
    g_fin(2)
    g_fin(1)
    if direct:
        xc.wait_recv()
        xc.wait_send()
        tot = tot + Sx[...]
    if direct:
        lane = lax.broadcasted_iota(jnp.int32, (8, DM), 1)
        for l in range(LAYERS):
            x = tot[l]
            gsm[l, 0:8, :] = pltpu.roll(x, lax.rem(DM - slot * rw, DM), 1)[:, 0:128]
            gq = pltpu.roll(x, DM - 384, 1)
            gv = jnp.where(lane < 128, pltpu.roll(x, DM - 64, 1), pltpu.roll(x, DM - 192, 1))
            back = lax.rem(DM - slot * (rw // 4), DM)
            gsm[l, 8:16, :] = pltpu.roll(gq, back, 1)[:, 0:128]
            gsm[l, 16:24, :] = pltpu.roll(gv, back, 1)[:, 0:128]
    else:
        gsm[...] = tot
    g_fin(0)
    w_sent(6)
    for cp in list(gx.values()):
        cp.wait_send()


def shards(dp, nz, nt_, x_in, cotangent, segment_ids, random_blocks, wqkv, wo, w1, w2, qv_bias, mid_bias, shifts, gains):
    rw = wqkv.shape[1]
    direct = dp == 2 and rw % 16 == 0
    TL, DM = x_in.shape[1], x_in.shape[2]
    length = segment_ids.shape[1]
    z = lax.axis_index("seq")
    slot = lax.axis_index("dp") * nz + z
    axes = ("dp", "seq")


    if direct:
        first_in = wqkv.transpose(0, 2, 1, 3)
        small_in = (wo, w1, w2.transpose(0, 2, 1), shifts, gains, mid_bias, qv_bias[:, :, 0])
    else:
        qw, kw, vw = [wqkv[:, :, i, :].reshape(LAYERS, rw, 3, 64) for i in range(3)]
        ot = wo.transpose(0, 2, 1).reshape(LAYERS, rw, 3, 64)
        attn = jnp.concatenate(
            [kw[:, :, 0], vw[:, :, 0], vw[:, :, 1], kw[:, :, 1], kw[:, :, 2], vw[:, :, 2],
             qw[:, :, 0], qw[:, :, 1], qw[:, :, 2], ot[:, :, 2], ot[:, :, 1], ot[:, :, 0]], axis=2)
        wl = jnp.stack([attn, w1, w2.transpose(0, 2, 1)], axis=1).astype(BF).reshape(3 * LAYERS, rw, DM)
        first_in = lax.all_gather(wl, axes, axis=1, tiled=True)
        sh = lax.all_gather(shifts.astype(BF), axes, axis=2, tiled=True).astype(F32)
        ga = lax.all_gather(gains.astype(BF), axes, axis=2, tiled=True).astype(F32)
        mb = lax.all_gather(mid_bias.astype(BF), axes, axis=2, tiled=True).astype(F32)
        qv = lax.all_gather(qv_bias[:, :, 0].astype(BF), axes, axis=2, tiled=True).astype(F32)
        bq, bv = qv[:, 0:1], qv[:, 1:2]
        gap = jnp.zeros((LAYERS, 1, 64), F32)
        kvb = jnp.concatenate([gap, bv[..., 0:128], gap, gap, bv[..., 128:192]], axis=2)
        fit = lambda v: jnp.pad(v, ((0, 0), (0, 0), (0, DM - v.shape[2])))
        sm = jnp.concatenate([sh, ga, mb, fit(bq), fit(kvb), jnp.zeros((LAYERS, 7, DM), F32)], axis=1)
        small_in = (sm,)

    QT = TL // 4
    L = LAYERS
    nslot = dp * nz if direct else 1
    vm = pl.BlockSpec(memory_space=pltpu.VMEM)
    dma = pltpu.SemaphoreType.DMA
    xr = nz * rw if direct else 16
    scratch = [
        pltpu.VMEM((3 * L, DM, DM), BF),
        pltpu.VMEM((nslot, L, 16, 128), F32),
        pltpu.VMEM((L, 16, DM), F32),
        pltpu.VMEM((L, length, DM), BF),
        pltpu.VMEM((L, length, 384), BF),
        pltpu.VMEM((L, TL, 384), BF),
        pltpu.VMEM((L, TL, 256), BF),
        pltpu.VMEM((3 * L, 1, TL), F32),
        pltpu.VMEM((L, TL, DM), BF),
        pltpu.VMEM((L, TL, DM), BF),
        pltpu.VMEM((L, TL, DM), BF),
        pltpu.VMEM((L, QT, DM), F32),
        pltpu.VMEM((L, QT, DM), F32),
        pltpu.VMEM((L, QT, 1), F32),
        pltpu.VMEM((L, QT, 1), F32),
        pltpu.VMEM((QT, DM), F32),
        pltpu.VMEM((QT, DM), F32),
        pltpu.VMEM((2 * L, TL, DM), BF),
        pltpu.VMEM((TL, DM), BF),
        pltpu.VMEM((2, 2, QT // 2, DM), BF),
        pltpu.VMEM((2, QT // 2, DM), BF),
        pltpu.VMEM((nz, TL, DM), BF),
        pltpu.VMEM((nz, 2, QT, DM), BF),
        pltpu.VMEM((nz, QT, DM), BF),
        pltpu.VMEM((L, nz, QT, DM), BF),
        pltpu.VMEM((3, 128, TL), F32),
        pltpu.VMEM((3, 1, TL), F32),
        pltpu.VMEM((3, 1, TL), F32),
        pltpu.VMEM((length, 384), BF),
        pltpu.VMEM((TL, DM), BF),
        pltpu.VMEM((TL, 256), BF),
        pltpu.VMEM((TL, 384), BF),
        pltpu.VMEM((3, 1, TL), F32),
        pltpu.VMEM((3 * L, xr, DM) if direct else (1, 16, 128), BF),
        pltpu.VMEM((3 * L, nz, rw, DM) if direct else (1, 1, 16, 128), BF),
        pltpu.VMEM((L, 8, DM), F32),
        pltpu.VMEM((L, 8, DM), F32),
        pltpu.VMEM((L, 8, DM), F32),
        pltpu.VMEM((nz - 1, L, 8, DM), F32),
        pltpu.VMEM((L, 8, DM), F32),
        pltpu.VMEM((L, 16, 128), F32),
        pltpu.VMEM((length, 128), F32),
        pltpu.VMEM((3, length // BLK, TL), F32),
        pltpu.VMEM((rw, DM) if direct else (8, 128), F32),
        pltpu.VMEM((3 * L, rw, DM) if direct else (1, 16, 128), BF),
        dma((7, 5 + nz)), dma((7, 2 * nz)),
        dma((L, 5 * nz)), dma((L, 4 * nz)),
        dma((8, 6)), dma((8, 6)),
        dma((6, 6)), dma((6, 6)),
        dma((L, 4 * nz)), dma((L, 4 * nz)),
        dma((6, 2 * nz)), dma((6, 2 * nz)),
        dma((2 + nz,)), dma((2 + nz,)),
    ]
    tokens = (jax.ShapeDtypeStruct((TL, DM), BF), jax.ShapeDtypeStruct((TL, DM), F32))
    if direct:
        grads = [(L, 3, rw, 192), (L, rw, 192), (L, rw, DM), (L, rw, DM), (L, 24, 128)]
        out_shape = tokens + tuple(jax.ShapeDtypeStruct(g, F32) for g in grads)
    else:
        out_shape = tokens + (jax.ShapeDtypeStruct((3 * L, DM, DM), BF), jax.ShapeDtypeStruct((L, 8, DM), F32))
    args = (first_in, x_in[0], cotangent[0], segment_ids, random_blocks[0]) + small_in
    results = pl.pallas_call(
        functools.partial(body, direct, nz, rw, len(args)),
        out_shape=out_shape,
        in_specs=[vm] * 4 + [pl.BlockSpec(memory_space=pltpu.SMEM)] + [vm] * len(small_in),
        out_specs=(vm,) * len(out_shape),
        scratch_shapes=scratch,
        compiler_params=pltpu.CompilerParams(collective_id=0, has_side_effects=True, vmem_limit_bytes=60 * 2**20),
        name="encoder",
    )(*args)
    act, dx = results[:2]
    if direct:
        gq, go, g1, g2, gsm = results[2:]
        return (
            act[None],
            dx[None],
            gq.transpose(0, 2, 1, 3),
            go.transpose(0, 2, 1),
            g1,
            g2.transpose(0, 2, 1),
            gsm[:, 15:24:8, None, : rw // 4],
            gsm[:, 6:7, :rw],
            gsm[:, 0:4, :rw],
            gsm[:, 4:6, :rw],
        )
    gout, gsm = results[2:]
    gout = lax.psum_scatter(gout.astype(F32), axes, scatter_dimension=1, tiled=True).reshape(L, 3, rw, DM)
    gsm = lax.psum(gsm, "dp")
    ga, g1, g2 = gout[:, 0], gout[:, 1], gout[:, 2]
    pc = [ga[:, :, i * 64 : (i + 1) * 64] for i in range(12)]
    gq = jnp.concatenate([pc[6], pc[7], pc[8]], axis=2)
    gk = jnp.concatenate([pc[0], pc[3], pc[4]], axis=2)
    gv = jnp.concatenate([pc[1], pc[2], pc[5]], axis=2)
    go = jnp.concatenate([pc[11], pc[10], pc[9]], axis=2).transpose(0, 2, 1)
    sl = lax.dynamic_slice_in_dim(gsm[:, 0:7], slot * rw, rw, axis=2)
    dbq = gsm[:, 7, 384:576]
    dbv = jnp.concatenate([gsm[:, 7, 64:192], gsm[:, 7, 320:384]], axis=1)
    qv = lax.dynamic_slice_in_dim(jnp.stack([dbq, dbv], axis=1), slot * (rw // 4), rw // 4, axis=2)
    return (
        act[None],
        dx[None],
        jnp.stack([gq, gk, gv], axis=2),
        go,
        g1,
        g2.transpose(0, 2, 1),
        qv[:, :, None, :],
        sl[:, 6:7],
        sl[:, 0:4],
        sl[:, 4:6],
    )


def solution(mesh):
    both = ("dp", "seq")
    weights = (
        P(None, both, None, "tensor"),
        P(None, "tensor", both),
        P(None, both, "tensor"),
        P(None, "tensor", both),
        P(None, None, "tensor", both),
        P(None, "tensor", both),
        P(None, None, both),
        P(None, None, both),
    )
    tokens = P("dp", "seq", None)
    in_specs = (tokens, tokens, P("dp", None), P("dp", "tensor", None, None)) + weights
    out_specs = (tokens, tokens) + weights
    fn = functools.partial(shards, mesh.shape["dp"], mesh.shape["seq"], mesh.shape["tensor"])
    return jax.shard_map(fn, mesh=mesh, in_specs=in_specs, out_specs=out_specs, check_vma=False)
```

```python
import functools

import jax
import jax.numpy as jnp
from jax import lax
from jax.experimental import pallas as pl
from jax.experimental.pallas import tpu as pltpu
from jax.sharding import PartitionSpec as P

BLK = 64
LAYERS = 2
EPS = 1e-06
NEG = -1e30
BF = jnp.bfloat16
F32 = jnp.float32
MESH = pl.DeviceIdType.MESH


def nn(a, b):
    return lax.dot_general(a, b, (((1,), (0,)), ((), ())), preferred_element_type=F32)


def nt(a, b):
    return lax.dot_general(a, b, (((1,), (1,)), ((), ())), preferred_element_type=F32)


def tn(a, b):
    return lax.dot_general(a, b, (((0,), (0,)), ((), ())), preferred_element_type=F32)


def normalise(z):
    mu = jnp.mean(z, axis=-1, keepdims=True)
    c = z - mu
    rs = lax.rsqrt(jnp.mean(c * c, axis=-1, keepdims=True) + EPS)
    return c * rs, rs


def norm_back(dn, n, rs):
    return (dn - jnp.mean(dn, axis=-1, keepdims=True) - n * jnp.mean(dn * n, axis=-1, keepdims=True)) * rs


def low_lanes(shape):
    return lax.broadcasted_iota(jnp.int32, shape, len(shape) - 1) % 128 < 64


def body(
    direct, nz, rw, n_in, *refs
):
    ins, refs = refs[:n_in], refs[n_in:]
    if direct:
        wl, xin, cot, seg, rnd, sh_in, ga_in, mb_in, qv_in = ins
        act, dxo, gq_out, go_out, g1_out, g2_out, qv_out, mb_out, sh_out, ga_out = refs[:10]
        refs = refs[10:]
    else:
        wl, xin, cot, seg, rnd, sm = ins
        act, dxo, gout, gsm = refs[:4]
        refs = refs[4:]
    (
    W, SG, SV, XA, KV, QP, OO, LSE, H1, DG, G, N1, N2, RS1, RS2, XR, DZ, EB,
    PB, rsib, ry, DXP, xsib, xy, xz, ACC, MX, LS, DKV, DU, DQ, DO, DEL, XRV, ZRV, SL, St1, St2, Sz, Sx,
        SMS, segk, segqm, SA,
        wg_s, wg_r, ax_s, ax_r, a4_s, a4_r, r4_s, r4_r, r16_s, r16_r, g_s, g_r, s_s, s_r,
    ) = refs
    if direct:
        sm = SMS
    d, z, t = lax.axis_index("dp"), lax.axis_index("seq"), lax.axis_index("tensor")
    c = t % 2
    y = t // 2
    sib, yp = 2 * y + (1 - c), 2 * (1 - y) + c
    DM = XA.shape[2]
    TL = xin.shape[0]
    QT = TL // 4
    HALF = TL // 2
    dsib, dyp = (d, z, sib), (d, z, yp)
    zk = [lax.rem(z + k, nz) for k in range(nz)]
    upper = z // 2
    edge = (1 - z) * (1 - upper) + (z - 2) * upper
    inner = 1 - edge
    ck = [z] + [o + upper * (nz - 1 - 2 * o) for o in (edge, 2, 3)]

    bar = pltpu.get_barrier_semaphore()
    peers = [dsib, dyp] + [(d, zk[k], t) for k in range(1, nz)]
    if direct:
        dx_dev = (1 - d, z, t)
        peers.append(dx_dev)
    for p in peers:
        pl.semaphore_signal(bar, inc=1, device_id=p, device_id_type=MESH)
    pl.semaphore_wait(bar, len(peers))

    def send(src, dst, ss, rs, dev):
        cp = pltpu.make_async_remote_copy(src_ref=src, dst_ref=dst, send_sem=ss, recv_sem=rs, device_id=dev, device_id_type=MESH)
        cp.start()
        return cp

    def rows(start, n):
        return pl.ds(pl.multiple_of(start, n if n % 16 == 0 else 16), n)

    own = rows(t * QT, QT)

    def copy_to(src, dst, ss, rs, dev):
        return pltpu.make_async_remote_copy(src_ref=src, dst_ref=dst, send_sem=ss, recv_sem=rs, device_id=dev, device_id_type=MESH)

    if direct:
        slot = d * nz + z

        def w_ref(p, k):
            if p == 6:
                return SG.at[d * nz + k]
            return W.at[p, rows((d * nz + k) * rw, rw), :]

        def w_own(p):
            src = sm if p == 6 else wl.at[p]
            dst = w_ref(p, z)
            out = []
            for i, step in enumerate((1, 2, -1, -2)):
                ok = z + step < nz if step > 0 else z + step >= 0
                out.append((ok, copy_to(src, dst, wg_s.at[p, i], wg_r.at[p, z], (d, z + step, t))))
            return out

        def w_over(p, k):
            return copy_to(w_ref(p, k), w_ref(p, k), wg_s.at[p, 5 + k], wg_r.at[p, nz + k], dx_dev)

        def w_hop(p):
            return copy_to(w_ref(p, ck[3]), w_ref(p, ck[3]), wg_s.at[p, 4], wg_r.at[p, ck[3]], (d, nz - 1 - ck[3], t))

        def w_wait(p, k):
            copy_to(w_ref(p, k), w_ref(p, k), wg_s.at[p, 4], wg_r.at[p, k], dx_dev).wait_recv()

        def w_a(p):
            if p == 6:
                SG[slot] = sm[...]
            else:
                W[p, rows(slot * rw, rw), :] = wl[p]
            for ok, cp in w_own(p):
                pl.when(ok)(cp.start)

        def w_o(p):
            src = sm if p == 6 else wl.at[p]
            copy_to(src, w_ref(p, z), wg_s.at[p, 5 + z], wg_r.at[p, nz + z], dx_dev).start()

        def w_b(p):
            @pl.when(inner == 1)
            def _():
                w_wait(p, ck[3])
                w_hop(p).start()

        def w_c(p):
            for k in ck[1:3]:
                w_wait(p, k)
                w_over(p, k).start()

        def w_d(p):
            @pl.when(edge == 1)
            def _():
                w_wait(p, ck[3])

            w_over(p, ck[3]).start()

        def w_fin(p):
            for k in range(nz):
                w_over(p, k).wait_recv()

        def w_sent(p):
            for ok, cp in w_own(p):
                pl.when(ok)(cp.wait_send)

            @pl.when(inner == 1)
            def _():
                w_hop(p).wait_send()

            for k in ck:
                w_over(p, k).wait_send()
    else:

        def w_a(p):
            if p == 6:
                SV[...] = sm[...]
            else:
                W[p] = wl[p]

        def w_b(p):
            pass

        w_o = w_c = w_d = w_fin = w_sent = w_b

    ST = QT // 2

    def own_part(b):
        return rows(t * QT + b * ST, ST)

    def ag4(i, ref):
        st = {}

        def put(b):
            r = ref.at[own_part(b), :]
            st["c", b] = send(r, r, a4_s.at[i, b], a4_r.at[i, b], dsib)
            st["y", b] = send(r, r, a4_s.at[i, 2 + b], a4_r.at[i, 2 + b], dyp)

        def fin():
            for b in range(2):
                st["y", b].wait_recv()
                r = ref.at[rows(yp * QT + b * ST, ST), :]
                st["o", b] = send(r, r, a4_s.at[i, 4 + b], a4_r.at[i, 4 + b], dsib)
            for b in range(2):
                st["c", b].wait_recv()
                st["o", b].wait_recv()

        def sent():
            for cp in st.values():
                cp.wait_send()

        return put, fin, sent

    def rs4(i, part, consume, filler=None):
        r0 = [(1 - y) * HALF, y * HALF]
        st = {}
        for k in range(2):
            PB[rows(r0[k], HALF), :] = part(rows(r0[k], HALF)).astype(BF)
            for b in range(2):
                st["c", k, b] = send(
                    PB.at[rows(r0[k] + (1 - c) * QT + b * ST, ST), :], rsib.at[k, b], r4_s.at[i, 2 * k + b], r4_r.at[i, 2 * k + b], dsib
                )
            if k == 0:
                for b in range(2):
                    st["c", 0, b].wait_recv()
                    mine = rows(r0[0] + c * QT + b * ST, ST)
                    PB[mine, :] = (PB[mine, :].astype(F32) + rsib[0, b].astype(F32)).astype(BF)
                    st["y", b] = send(PB.at[mine, :], ry.at[b], r4_s.at[i, 4 + b], r4_r.at[i, 4 + b], dyp)
        if filler is not None:
            filler()
        for b in range(2):
            st["c", 1, b].wait_recv()
            st["y", b].wait_recv()
            consume(b, PB[own_part(b), :].astype(F32) + rsib[1, b].astype(F32) + ry[b].astype(F32))
        for cp in st.values():
            cp.wait_send()

    def xgather(l):
        st = {}

        def src_rows(k, q):
            return XA.at[l, rows(k * TL + q * QT, QT), :]

        def along(k, to, kind):
            r = src_rows(k, t)
            return copy_to(r, r, ax_s.at[l, kind * nz + k], ax_r.at[l, k], (d, to, t))

        def hop(j):
            right = (z - ck[j] + nz) // nz
            to = z - 1 + 2 * right
            return (to >= 0) & (to < nz), along(ck[j], to, 0)

        ends = [(z < nz - 1, along(z, z + 1, 0)), (z > 0, along(z, z - 1, 1))]

        def local(j):
            r = src_rows(ck[j], t)
            st["y", j] = send(r, r, ax_s.at[l, 2 * nz + ck[j]], ax_r.at[l, nz + ck[j]], dyp)
            st["c", j] = send(r, r, ax_s.at[l, 3 * nz + ck[j]], ax_r.at[l, 2 * nz + ck[j]], dsib)

        def start():
            for ok, cp in ends:
                pl.when(ok)(cp.start)
            if l > 0:
                local(0)

        def arrive(j):
            along(ck[j], z, 0).wait_recv()
            ok, cp = hop(j)
            pl.when(ok)(cp.start)
            local(j)

        def fwd(j):
            st["y", j].wait_recv()
            r = src_rows(ck[j], yp)
            st["c2", j] = send(r, r, ax_s.at[l, 4 * nz + ck[j]], ax_r.at[l, 3 * nz + ck[j]], dsib)

        def fin(j):
            st["c", j].wait_recv()
            st["c2", j].wait_recv()

        def sent():
            for ok, cp in ends + [hop(j) for j in range(1, nz)]:
                pl.when(ok)(cp.wait_send)
            for cp in st.values():
                cp.wait_send()

        return start, arrive, fwd, fin, sent

    def small(l, r):
        return SV[l, r : r + 1, :]

    def kv_proj(l, j):
        r = rows(ck[j] * TL, TL)
        bias = SV[l, 8:9, 0:384]
        KV[l, r, :] = (nn(XA[l, r, :], W[3 * l, :, 0:384]) + bias).astype(BF)

    def q_proj(l):
        bias = SV[l, 7:8, 0:256]
        q = (nn(XA[l, rows(z * TL, TL), :], W[3 * l, :, 384:640]) + bias).astype(BF).astype(F32) * 0.125
        a, b = q[:, 0:128], q[:, 128:256]
        lo = low_lanes(a.shape)
        QP[l, :, 0:128] = jnp.where(lo, a, 0.0).astype(BF)
        QP[l, :, 128:256] = jnp.where(lo, 0.0, a).astype(BF)
        QP[l, :, 256:384] = jnp.where(lo, b, 0.0).astype(BF)

    nb = TL // BLK

    def masked_scores(l, h, hl, r, j):
        kv = KV[l, r, pl.ds(hl, 128)]
        s = nt(kv, QP[l, :, pl.ds(hl, 128)])
        sq = segqm[h, pl.ds(pl.multiple_of(ck[j] * nb, nb), nb), :]
        sk = segk[r, :]
        parts = []
        for b in range(nb):
            skb = jnp.concatenate([sk[b * BLK : (b + 1) * BLK]] * (TL // 128), axis=1)
            parts.append(jnp.where(skb == sq[b : b + 1], s[b * BLK : (b + 1) * BLK], NEG))
        return kv, jnp.concatenate(parts, axis=0)

    def attend(l, j):
        r = rows(ck[j] * TL, TL)

        def head(h, carry):
            hl = pl.multiple_of(h * 128, 128)
            kv, s = masked_scores(l, h, hl, r, j)
            top = jnp.max(s, axis=0, keepdims=True)
            if j > 0:
                before = MX[h]
                top = jnp.maximum(before, top)
            e = jnp.exp(s - top)
            total = jnp.sum(e, axis=0, keepdims=True)
            o = tn(kv, e.astype(BF))
            if j > 0:
                a = jnp.exp(before - top)
                total = total + LS[h] * a
                o = o + ACC[h] * a
            MX[h] = top
            LS[h] = total
            ACC[h] = o
            return carry

        lax.fori_loop(0, 3, head, 0)

    def attend_end(l):
        o = []
        for h in range(3):
            LSE[3 * l + h] = MX[h] + jnp.log(LS[h])
            o.append((ACC[h] / LS[h]).T)
        lo = low_lanes(o[0].shape)
        OO[l, :, 0:128] = jnp.where(lo, 0.0, o[2]).astype(BF)
        OO[l, :, 128:256] = jnp.where(lo, o[1], o[0]).astype(BF)

    def gelu_parts(u):
        k = 0.7978845608028654
        th = jnp.tanh(k * (u + 0.044715 * u * u * u))
        g = 0.5 * u * (1.0 + th)
        dg = 0.5 * (1.0 + th) + 0.5 * u * (1.0 - th * th) * (k * (1.0 + 3 * 0.044715 * u * u))
        return g, dg

    seen = []

    def forward(l, bg, then):
        start, arrive, fwd, fin, sent = xg[l]
        if l > 0:
            start()
            arrive(1)
            fwd(0)
            fin(0)
            w_fin(3)
        q_proj(l)
        kv_proj(l, 0)
        arrive(2)
        fwd(1)
        attend(l, 0)
        arrive(3)
        fwd(2)
        bg[0]()
        for j in range(1, nz):
            fin(j)
            kv_proj(l, j)
            attend(l, j)
            if j == 1:
                fwd(3)
            bg[j]()
        attend_end(l)
        sent()
        wo = W[3 * l, :, 512:768]
        put, done, gone = ag4(4 * l, H1.at[l])

        def first(b, r):
            part = pl.ds(b * ST, ST)
            z1 = XR[part, :] + r + small(l, 0)
            n1, rs1 = normalise(z1)
            N1[l, part, :] = n1
            RS1[l, part, :] = rs1
            h1 = n1 * small(l, 4) + small(l, 1)
            H1[l, own_part(b), :] = h1.astype(BF)
            XR[part, :] = h1
            put(b)

        rs4(3 * l, lambda rr: nt(OO[l, rr, :], wo), first, bg[4])
        bg[5]()
        done()
        w_fin(3 * l + 1)

        def ffn(rr):
            u = nn(H1[l, rr, :], W[3 * l + 1]) + small(l, 6)
            g, dg = gelu_parts(u)
            DG[l, rr, :] = dg.astype(BF)
            gb = g.astype(BF)
            G[l, rr, :] = gb
            if l not in seen:
                seen.append(l)
                w_fin(3 * l + 2)
            return nt(gb, W[3 * l + 2])

        def fill():
            gone()
            bg[6]()

        def second(b, r):
            part = pl.ds(b * ST, ST)
            z2 = XR[part, :] + r + small(l, 2)
            n2, rs2 = normalise(z2)
            N2[l, part, :] = n2
            RS2[l, part, :] = rs2
            out = n2 * small(l, 5) + small(l, 3)
            XR[part, :] = out
            then(b, out)

        rs4(3 * l + 1, ffn, second, fill)
        bg[7]()

    gx = {}

    if direct:

        def g_start(p):
            for k in ck[::-1]:
                gx[p, len(gx)] = send(
                    W.at[p, rows(((1 - d) * nz + k) * rw, rw), :], XRV.at[p, rows(k * rw, rw), :], g_s.at[p, k], g_r.at[p, k], dx_dev
                )

        def g_slot(p, k):
            return W.at[p, rows((d * nz + k) * rw, rw), :]

        def g_to(p, part, to, slot_there):
            return copy_to(g_slot(p, part), ZRV.at[p, slot_there], g_s.at[p, nz + part], g_r.at[p, nz + slot_there], (d, to, t))

        def g_landed(p, k):
            x = ZRV.at[p, k]
            copy_to(x, x, g_s.at[p, nz + k], g_r.at[p, nz + k], dx_dev).wait_recv()

        def g_far(p):
            return lambda: g_to(p, ck[3], ck[1], ck[1]), lambda: g_to(p, ck[3], ck[3], z)

        def g_mid(p):
            for k in ck[::-1]:
                r = g_slot(p, k)
                x = XRV.at[p, rows(k * rw, rw), :]
                copy_to(x, x, g_s.at[p, k], g_r.at[p, k], dx_dev).wait_recv()
                r[...] = (r[...].astype(F32) + x[...].astype(F32)).astype(BF)
                if k is ck[3]:
                    pl.when(edge == 1)(g_far(p)[0]().start)
                elif k is not z:
                    g_to(p, k, k, z).start()

        def g_add(p):
            @pl.when(inner == 1)
            def _():
                g_landed(p, z)
                r = g_slot(p, ck[3])
                r[...] = (r[...].astype(F32) + ZRV[p, z].astype(F32)).astype(BF)
                g_far(p)[1]().start()

        def g_fin(p):
            l = p // 3
            goal = (SA, g1_out.at[l], g2_out.at[l])[p % 3]
            tot = g_slot(p, z)[...].astype(F32)
            for k in ck[1:3]:
                g_landed(p, k)
                tot = tot + ZRV[p, k].astype(F32)
            goal[...] = tot

            @pl.when(inner == 1)
            def _():
                g_landed(p, ck[3])
                goal[...] = goal[...] + ZRV[p, ck[3]].astype(F32)
                g_far(p)[1]().wait_send()

            pl.when(edge == 1)(g_far(p)[0]().wait_send)
            for k in ck[1:3]:
                g_to(p, k, k, z).wait_send()
            if p % 3 == 0:
                tile = [SA[:, 128 * i : 128 * (i + 1)] for i in range(6)]
                lo = low_lanes(tile[0].shape)
                gq_out[l, 0, :, 0:128] = tile[3]
                gq_out[l, 0, :, 128:192] = tile[4][:, 0:64]
                gq_out[l, 1, :, 0:128] = jnp.where(lo, tile[0], tile[1])
                gq_out[l, 1, :, 128:192] = tile[2][:, 0:64]
                gq_out[l, 2, :, 0:128] = pltpu.roll(jnp.where(lo, tile[1], tile[0]), 64, 1)
                gq_out[l, 2, :, 128:192] = pltpu.roll(tile[2], 64, 1)[:, 0:64]
                go_out[l, :, 0:128] = pltpu.roll(tile[5], 64, 1)
                go_out[l, :, 128:192] = pltpu.roll(tile[4], 64, 1)[:, 0:64]
    else:

        def g_start(p):
            gout[p] = W[p]

        def g_mid(p):
            pass

        g_add = g_fin = g_mid

    def accumulate(l, row, b, v):
        v = jnp.sum(v, axis=0, keepdims=True)
        SL[l, row : row + 1, :] = v if b == 0 else SL[l, row : row + 1, :] + v

    def second_back(l):
        put, done, gone = ag4(4 * l + 2, EB.at[2 * l + 1])

        def one(b, dy):
            part = pl.ds(b * ST, ST)
            n2 = N2[l, part, :]
            accumulate(l, 3, b, dy)
            accumulate(l, 5, b, dy * n2)
            dz2 = norm_back(dy * small(l, 5), n2, RS2[l, part, :])
            accumulate(l, 2, b, dz2)
            DZ[part, :] = dz2
            EB[2 * l + 1, own_part(b), :] = dz2.astype(BF)
            put(b)

        return one, done, gone

    def backward(l, bg, done, gone, then):
        bg.get(0, nop)()
        done()

        def ffn_back(rr):
            dgm = nn(EB[2 * l + 1, rr, :], W[3 * l + 2])
            du = (dgm * DG[l, rr, :].astype(F32)).astype(BF)
            DU[rr, :] = du
            return nt(du, W[3 * l + 1])

        def fill():
            gone()
            w_sent(3 * l + 2)
            w_sent(3 * l + 1)
            W[3 * l + 2] = tn(EB[2 * l + 1], G[l]).astype(BF)
            g_start(3 * l + 2)
            W[3 * l + 1] = tn(H1[l], DU[...]).astype(BF)
            g_start(3 * l + 1)
            SL[l, 6:7, :] = jnp.sum(DU[...].astype(F32), axis=0, keepdims=True)
            bg.get(1, nop)()

        put, done1, gone1 = ag4(4 * l + 3, EB.at[2 * l])

        def first_back(b, r):
            part = pl.ds(b * ST, ST)
            dh1 = DZ[part, :] + r
            n1 = N1[l, part, :]
            dz1 = norm_back(dh1 * small(l, 4), n1, RS1[l, part, :])
            DZ[part, :] = dz1
            EB[2 * l, own_part(b), :] = dz1.astype(BF)
            put(b)
            accumulate(l, 1, b, dh1)
            accumulate(l, 4, b, dh1 * n1)
            accumulate(l, 0, b, dz1)

        rs4(3 * l + 2, ffn_back, first_back, fill)
        bg.get(2, nop)()
        done1()
        doo = nn(EB[2 * l], W[3 * l, :, 512:768]).astype(BF).astype(F32)
        lo = low_lanes((TL, 128))
        da, db = doo[:, 0:128], doo[:, 128:256]
        DO[:, 0:128] = jnp.where(lo, 0.0, db).astype(BF)
        DO[:, 128:256] = jnp.where(lo, db, 0.0).astype(BF)
        DO[:, 256:384] = jnp.where(lo, 0.0, da).astype(BF)
        prod = (doo * OO[l].astype(F32)).T
        DEL[0] = jnp.sum(prod[192:256], axis=0, keepdims=True)
        DEL[1] = jnp.sum(prod[128:192], axis=0, keepdims=True)
        DEL[2] = jnp.sum(prod[64:128], axis=0, keepdims=True)

        xs = {}
        order = list(range(nz - 1, 0, -1)) + [0]

        def attend_back(j, first):
            r = rows(ck[j] * TL, TL)

            def head(h, carry):
                hl = pl.multiple_of(h * 128, 128)
                kv, s = masked_scores(l, h, hl, r, j)
                q = QP[l, :, pl.ds(hl, 128)]
                do = DO[:, pl.ds(hl, 128)]
                p = jnp.exp(s - LSE[3 * l + h])
                dp = nt(kv, do)
                ds = (p * (dp - DEL[h])).astype(BF)
                DKV[r, pl.ds(hl, 128)] = (nn(ds, q) + nn(p.astype(BF), do)).astype(BF)
                dq = tn(kv, ds)
                if first:
                    ACC[h] = dq
                else:
                    ACC[h] = ACC[h] + dq
                return carry

            lax.fori_loop(0, 3, head, 0)

        def dx_parts(j):
            for k in range(2):
                r0 = [(1 - y) * HALF, y * HALF][k]
                v = nt(DKV[rows(ck[j] * TL + r0, HALF), :], W[3 * l, :, 0:384])
                if j == 0:
                    v = v + nt(DQ[rows(r0, HALF), :], W[3 * l, :, 384:640])
                DXP[j, rows(r0, HALF), :] = v.astype(BF)
                xs["c", j, k] = send(DXP.at[j, rows(r0 + (1 - c) * QT, QT), :], xsib.at[j, k], r16_s.at[l, 3 * j + k], r16_r.at[l, 3 * j + k], dsib)

        def dx_y(j):
            xs["c", j, 0].wait_recv()
            mine = rows(yp * QT, QT)
            DXP[j, mine, :] = (DXP[j, mine, :].astype(F32) + xsib[j, 0].astype(F32)).astype(BF)
            xs["y", j] = send(DXP.at[j, mine, :], xy.at[j], r16_s.at[l, 3 * j + 2], r16_r.at[l, 3 * j + 2], dyp)

        def dx_z(j):
            xs["c", j, 1].wait_recv()
            xs["y", j].wait_recv()
            tot = DXP[j, own, :].astype(F32) + xsib[j, 1].astype(F32) + xy[j].astype(F32)
            if j == 0:
                return tot
            DXP[j, own, :] = tot.astype(BF)
            if j == nz - 1:
                pl.when(edge == 1)(dx_far()[0]().start)
            else:
                dx_to(j, ck[j], z).start()

        def dx_to(j, to, there):
            return copy_to(DXP.at[j, own, :], xz.at[l, there], r16_s.at[l, 3 * nz + ck[j]], r16_r.at[l, 3 * nz + there], (d, to, t))

        def dx_far():
            return lambda: dx_to(nz - 1, ck[1], ck[1]), lambda: dx_to(nz - 1, ck[nz - 1], z)

        def dx_landed(k):
            x = xz.at[l, k]
            copy_to(x, x, r16_s.at[l, 3 * nz + k], r16_r.at[l, 3 * nz + k], dsib).wait_recv()

        def dx_add():
            @pl.when(inner == 1)
            def _():
                dx_landed(z)
                j = nz - 1
                DXP[j, own, :] = (DXP[j, own, :].astype(F32) + xz[l, z].astype(F32)).astype(BF)
                dx_far()[1]().start()

        for i, j in enumerate(order):
            attend_back(j, i == 0)
            if i >= 2:
                dx_z(order[i - 2])
            if i < 2:
                bg.get(3 + i, nop)()
            if j == 0:
                a01 = ACC[0]
                hi = lax.broadcasted_iota(jnp.int32, a01.shape, 0) < 64
                DQ[:, 0:128] = (jnp.where(hi, a01, ACC[1]).T * 0.125).astype(BF)
                DQ[:, 128:256] = (jnp.where(hi, ACC[2], 0.0).T * 0.125).astype(BF)
            dx_parts(j)
            dx_y(j)
        gone1()
        w_sent(3 * l)
        xown = XA[l, rows(z * TL, TL), :]
        gq = tn(xown, DQ[...])
        go = tn(EB[2 * l], OO[l])
        gkv = tn(XA[l], DKV[...])
        SL[l, 7:8, 0:384] = jnp.sum(DKV[...].astype(F32), axis=0, keepdims=True)
        SL[l, 7:8, 384:640] = jnp.sum(DQ[...].astype(F32), axis=0, keepdims=True)
        SL[l, 7:8, 640:768] = jnp.zeros((1, 128), F32)
        W[3 * l, :, 0:384] = gkv.astype(BF)
        W[3 * l, :, 384:512] = gq[:, 0:128].astype(BF)
        W[3 * l, :, 512:640] = (gq[:, 128:256] + go[:, 0:128]).astype(BF)
        W[3 * l, :, 640:768] = go[:, 128:256].astype(BF)
        g_start(3 * l)
        dx_z(order[nz - 2])
        dx_add()
        bg.get(5, nop)()
        DZ[...] = DZ[...] + dx_z(0)
        for k in ck[1:3]:
            dx_landed(k)
            DZ[...] = DZ[...] + xz[l, k].astype(F32)

        @pl.when(inner == 1)
        def _():
            dx_landed(ck[3])
            DZ[...] = DZ[...] + xz[l, ck[3]].astype(F32)
            dx_far()[1]().wait_send()

        then(DZ[...])
        pl.when(edge == 1)(dx_far()[0]().wait_send)
        for j in (1, 2):
            dx_to(j, ck[j], z).wait_send()
        for cp in xs.values():
            cp.wait_send()

    xg = [xgather(0), xgather(1)]

    def masks():
        length = seg.shape[1]
        nblk = length // BLK
        for i in range(length // 128):
            row = seg[:, 128 * i : 128 * (i + 1)].astype(F32)
            segk[128 * i : 128 * (i + 1), :] = jnp.broadcast_to(row, (128, 128)).T
        segq = seg[:, pl.ds(pl.multiple_of(z * TL, TL), TL)].astype(F32)
        block = lax.broadcasted_iota(jnp.int32, (1, TL), 1) // BLK
        key = lax.broadcasted_iota(jnp.int32, (nblk, TL), 0)
        away = key - (z * nb + lax.broadcasted_iota(jnp.int32, (nblk, TL), 1) // BLK)
        near = (away >= -1) & (away <= 1) | (key == 0) | (key == nblk - 1)
        for h in range(3):
            ok = near
            for r in range(rnd.shape[2]):
                pick = jnp.zeros((1, TL), jnp.int32)
                for b in range(nb):
                    pick = jnp.where(block == b, rnd[h, z * nb + b, r], pick)
                ok = ok | (key == pick)
            segqm[h] = jnp.where(ok, segq, -1.0)

    def run(*steps):
        def go():
            for fn, *a in steps:
                fn(*a)

        return go

    nop = run()
    if direct:
        SMS[...] = jnp.zeros_like(SMS)
        for l in range(LAYERS):
            SMS[l, 0:4, 0:rw] = sh_in[l].astype(BF).astype(F32)
            SMS[l, 4:6, 0:rw] = ga_in[l].astype(BF).astype(F32)
            SMS[l, 6:7, 0:rw] = mb_in[l].astype(BF).astype(F32)
            SMS[l, 8:10, 0 : rw // 4] = qv_in[l].astype(BF).astype(F32)
    for p in (6, 0, 1, 2):
        w_o(p)
    w_a(6)
    w_a(0)
    XA[0, rows(z * TL, TL), :] = xin[...]
    XR[...] = xin[own, :].astype(F32)
    w_b(6)
    w_b(0)
    w_c(6)
    w_c(0)
    xg[0][0]()
    masks()
    w_d(6)
    w_d(0)
    for p in (3, 4, 5):
        w_o(p)
    w_fin(6)
    if direct:
        wide = DM - 128
        nslot = SG.shape[0]
        for l in range(LAYERS):
            acc = jnp.zeros((16, DM), F32)
            cmp_ = jnp.zeros((8, DM), F32)
            for s_ in range(nslot):
                piece = jnp.concatenate([SG[s_, l], jnp.zeros((16, wide), F32)], axis=1)
                acc = acc + (pltpu.roll(piece, s_ * rw, 1) if s_ else piece)
                cmp_ = cmp_ + (pltpu.roll(piece[8:16], s_ * (rw // 4), 1) if s_ else piece[8:16])
            bq, bv = cmp_[0:1], cmp_[1:2]
            lane = lax.broadcasted_iota(jnp.int32, (1, DM), 1)
            kvb = jnp.where((lane >= 64) & (lane < 192), pltpu.roll(bv, 64, 1), 0.0) + jnp.where(
                (lane >= 320) & (lane < 384), pltpu.roll(bv, 192, 1), 0.0
            )
            SV[l, 0:8, :] = acc[0:8]
            SV[l, 7:8, :] = bq
            SV[l, 8:9, :] = kvb
    xg[0][1](1)
    w_fin(0)
    def next_input(b, v):
        XA[1, rows(z * TL + t * QT + b * ST, ST), :] = v.astype(BF)

    forward(0, [
        run((w_a, 1)),
        run(),
        run((w_b, 1)),
        run((w_a, 2), (w_c, 1)),
        run((w_d, 1), (w_b, 2), (w_a, 3)),
        run((w_c, 2), (w_d, 2)),
        run((w_b, 3), (w_a, 4), (w_c, 3)),
        run((w_d, 3)),
    ], next_input)
    start_back, done, gone = second_back(1)

    def last_output(b, v):
        start_back(b, cot[own_part(b), :].astype(F32))
        EB[0, own_part(b), :] = v.astype(BF)

    forward(1, [
        run((w_b, 4)),
        run((w_c, 4)),
        run((w_d, 4)),
        run((w_a, 5)),
        run((w_b, 5)),
        run((w_c, 5), (w_d, 5)),
        run(),
        run(),
    ], last_output)
    act_put, act_done, act_sent = ag4(1, EB.at[0])

    def act_start():
        act_put(0)
        act_put(1)

    def act_end():
        act_done()
        act[...] = EB[0]
        act_sent()

    lower = second_back(0)

    def to_lower(dy):
        for b in range(2):
            lower[0](b, dy[b * ST : (b + 1) * ST])

    backward(1, {0: run((act_start,)), 1: run((act_end,)), 3: run((g_mid, 5)), 4: run((g_add, 5)), 5: nop}, done, gone, to_lower)

    keep = lax.broadcasted_iota(jnp.int32, SL.shape, 1) < 6

    def s1():
        cp = send(SL, St1, s_s.at[0], s_r.at[0], dsib)
        cp.wait_recv()
        cp.wait_send()
        SL[...] = SL[...] + jnp.where(keep, St1[...], 0.0)
        sc.append(send(SL, St2, s_s.at[1], s_r.at[1], dyp))

    sc = []
    dx_put, dx_done, dx_sent = ag4(5, EB.at[3])

    def to_output(dx):
        EB[3, own, :] = dx.astype(BF)
        dx_put(0)
        dx_put(1)

    backward(
        0, {0: run((g_mid, 4)), 1: run((g_add, 4), (g_mid, 3), (g_fin, 5)), 3: run((g_add, 3), (g_mid, 2), (g_fin, 4)), 4: run((g_add, 2)), 5: run((s1,), (g_mid, 1), (g_fin, 3))}, lower[1], lower[2], to_output
    )

    sc[0].wait_recv()
    sc[0].wait_send()
    SL[...] = SL[...] + jnp.where(keep, St2[...], 0.0)
    zc = [send(SL, Sz.at[k - 1], s_s.at[1 + k], s_r.at[1 + k], (d, zk[k], t)) for k in range(1, nz)]
    g_add(1)
    g_mid(0)
    for cp in zc:
        cp.wait_recv()
    for cp in zc:
        cp.wait_send()
    tot = SL[...]
    for k in range(nz - 1):
        tot = tot + Sz[k]
    if direct:
        SL[...] = tot
        xc = send(SL, Sx, s_s.at[1 + nz], s_r.at[1 + nz], dx_dev)
    g_add(0)
    dx_done()
    dxo[...] = EB[3].astype(F32)
    dx_sent()
    g_fin(2)
    g_fin(1)
    if direct:
        xc.wait_recv()
        xc.wait_send()
        tot = tot + Sx[...]
    if direct:
        lane = lax.broadcasted_iota(jnp.int32, (8, DM), 1)
        for l in range(LAYERS):
            x = tot[l]
            own_cols = pltpu.roll(x, lax.rem(DM - slot * rw, DM), 1)
            sh_out[l] = own_cols[0:4, 0:rw]
            ga_out[l] = own_cols[4:6, 0:rw]
            mb_out[l] = own_cols[6:7, 0:rw]
            gq = pltpu.roll(x, DM - 384, 1)
            gv = jnp.where(lane < 128, pltpu.roll(x, DM - 64, 1), pltpu.roll(x, DM - 192, 1))
            back = lax.rem(DM - slot * (rw // 4), DM)
            qv_out[l, 0:1, :] = pltpu.roll(gq, back, 1)[7:8, 0 : rw // 4]
            qv_out[l, 1:2, :] = pltpu.roll(gv, back, 1)[7:8, 0 : rw // 4]
    else:
        gsm[...] = tot
    g_fin(0)
    w_sent(6)
    for cp in list(gx.values()):
        cp.wait_send()


def shards(dp, nz, nt_, x_in, cotangent, segment_ids, random_blocks, wqkv, wo, w1, w2, qv_bias, mid_bias, shifts, gains):
    rw = wqkv.shape[1]
    direct = dp == 2 and rw % 16 == 0
    TL, DM = x_in.shape[1], x_in.shape[2]
    length = segment_ids.shape[1]
    z = lax.axis_index("seq")
    slot = lax.axis_index("dp") * nz + z
    axes = ("dp", "seq")

    qw, kw, vw = [wqkv[:, :, i, :].reshape(LAYERS, rw, 3, 64) for i in range(3)]
    ot = wo.transpose(0, 2, 1).reshape(LAYERS, rw, 3, 64)
    attn = jnp.concatenate(
        [kw[:, :, 0], vw[:, :, 0], vw[:, :, 1], kw[:, :, 1], kw[:, :, 2], vw[:, :, 2],
         qw[:, :, 0], qw[:, :, 1], qw[:, :, 2], ot[:, :, 2], ot[:, :, 1], ot[:, :, 0]], axis=2)
    wl = jnp.stack([attn, w1, w2.transpose(0, 2, 1)], axis=1).astype(BF).reshape(3 * LAYERS, rw, DM)

    def low(v):
        return v.astype(BF).astype(F32)

    if direct:
        small_in = (shifts, gains, mid_bias, qv_bias[:, :, 0])
    else:
        wl = lax.all_gather(wl, axes, axis=1, tiled=True)
        sh = lax.all_gather(shifts.astype(BF), axes, axis=2, tiled=True).astype(F32)
        ga = lax.all_gather(gains.astype(BF), axes, axis=2, tiled=True).astype(F32)
        mb = lax.all_gather(mid_bias.astype(BF), axes, axis=2, tiled=True).astype(F32)
        qv = lax.all_gather(qv_bias[:, :, 0].astype(BF), axes, axis=2, tiled=True).astype(F32)
        bq, bv = qv[:, 0:1], qv[:, 1:2]
        gap = jnp.zeros((LAYERS, 1, 64), F32)
        kvb = jnp.concatenate([gap, bv[..., 0:128], gap, gap, bv[..., 128:192]], axis=2)
        fit = lambda v: jnp.pad(v, ((0, 0), (0, 0), (0, DM - v.shape[2])))
        sm = jnp.concatenate([sh, ga, mb, fit(bq), fit(kvb), jnp.zeros((LAYERS, 7, DM), F32)], axis=1)
        small_in = (sm,)

    QT = TL // 4
    L = LAYERS
    nslot = dp * nz if direct else 1
    vm = pl.BlockSpec(memory_space=pltpu.VMEM)
    dma = pltpu.SemaphoreType.DMA
    xr = nz * rw if direct else 16
    scratch = [
        pltpu.VMEM((3 * L, DM, DM), BF),
        pltpu.VMEM((nslot, L, 16, 128), F32),
        pltpu.VMEM((L, 16, DM), F32),
        pltpu.VMEM((L, length, DM), BF),
        pltpu.VMEM((L, length, 384), BF),
        pltpu.VMEM((L, TL, 384), BF),
        pltpu.VMEM((L, TL, 256), BF),
        pltpu.VMEM((3 * L, 1, TL), F32),
        pltpu.VMEM((L, TL, DM), BF),
        pltpu.VMEM((L, TL, DM), BF),
        pltpu.VMEM((L, TL, DM), BF),
        pltpu.VMEM((L, QT, DM), F32),
        pltpu.VMEM((L, QT, DM), F32),
        pltpu.VMEM((L, QT, 1), F32),
        pltpu.VMEM((L, QT, 1), F32),
        pltpu.VMEM((QT, DM), F32),
        pltpu.VMEM((QT, DM), F32),
        pltpu.VMEM((2 * L, TL, DM), BF),
        pltpu.VMEM((TL, DM), BF),
        pltpu.VMEM((2, 2, QT // 2, DM), BF),
        pltpu.VMEM((2, QT // 2, DM), BF),
        pltpu.VMEM((nz, TL, DM), BF),
        pltpu.VMEM((nz, 2, QT, DM), BF),
        pltpu.VMEM((nz, QT, DM), BF),
        pltpu.VMEM((L, nz, QT, DM), BF),
        pltpu.VMEM((3, 128, TL), F32),
        pltpu.VMEM((3, 1, TL), F32),
        pltpu.VMEM((3, 1, TL), F32),
        pltpu.VMEM((length, 384), BF),
        pltpu.VMEM((TL, DM), BF),
        pltpu.VMEM((TL, 256), BF),
        pltpu.VMEM((TL, 384), BF),
        pltpu.VMEM((3, 1, TL), F32),
        pltpu.VMEM((3 * L, xr, DM) if direct else (1, 16, 128), BF),
        pltpu.VMEM((3 * L, nz, rw, DM) if direct else (1, 1, 16, 128), BF),
        pltpu.VMEM((L, 8, DM), F32),
        pltpu.VMEM((L, 8, DM), F32),
        pltpu.VMEM((L, 8, DM), F32),
        pltpu.VMEM((nz - 1, L, 8, DM), F32),
        pltpu.VMEM((L, 8, DM), F32),
        pltpu.VMEM((L, 16, 128), F32),
        pltpu.VMEM((length, 128), F32),
        pltpu.VMEM((3, length // BLK, TL), F32),
        pltpu.VMEM((rw, DM) if direct else (8, 128), F32),
        dma((7, 5 + nz)), dma((7, 2 * nz)),
        dma((L, 5 * nz)), dma((L, 4 * nz)),
        dma((8, 6)), dma((8, 6)),
        dma((6, 6)), dma((6, 6)),
        dma((L, 4 * nz)), dma((L, 4 * nz)),
        dma((6, 2 * nz)), dma((6, 2 * nz)),
        dma((2 + nz,)), dma((2 + nz,)),
    ]
    tokens = (jax.ShapeDtypeStruct((TL, DM), BF), jax.ShapeDtypeStruct((TL, DM), F32))
    if direct:
        grads = [(L, 3, rw, 192), (L, rw, 192), (L, rw, DM), (L, rw, DM), (L, 2, rw // 4), (L, 1, rw), (L, 4, rw), (L, 2, rw)]
        out_shape = tokens + tuple(jax.ShapeDtypeStruct(g, F32) for g in grads)
    else:
        out_shape = tokens + (jax.ShapeDtypeStruct((3 * L, DM, DM), BF), jax.ShapeDtypeStruct((L, 8, DM), F32))
    args = (wl, x_in[0], cotangent[0], segment_ids, random_blocks[0]) + small_in
    results = pl.pallas_call(
        functools.partial(body, direct, nz, rw, len(args)),
        out_shape=out_shape,
        in_specs=[vm] * 4 + [pl.BlockSpec(memory_space=pltpu.SMEM)] + [vm] * len(small_in),
        out_specs=(vm,) * len(out_shape),
        scratch_shapes=scratch,
        compiler_params=pltpu.CompilerParams(collective_id=0, has_side_effects=True, vmem_limit_bytes=60 * 2**20),
        name="encoder",
    )(*args)
    act, dx = results[:2]
    if direct:
        gq, go, g1, g2, gqv, gmid, gsh, gga = results[2:]
        return (
            act[None],
            dx[None],
            gq.transpose(0, 2, 1, 3),
            go.transpose(0, 2, 1),
            g1,
            g2.transpose(0, 2, 1),
            gqv[:, :, None, :],
            gmid,
            gsh,
            gga,
        )
    gout, gsm = results[2:]
    gout = lax.psum_scatter(gout.astype(F32), axes, scatter_dimension=1, tiled=True).reshape(L, 3, rw, DM)
    gsm = lax.psum(gsm, "dp")
    ga, g1, g2 = gout[:, 0], gout[:, 1], gout[:, 2]
    pc = [ga[:, :, i * 64 : (i + 1) * 64] for i in range(12)]
    gq = jnp.concatenate([pc[6], pc[7], pc[8]], axis=2)
    gk = jnp.concatenate([pc[0], pc[3], pc[4]], axis=2)
    gv = jnp.concatenate([pc[1], pc[2], pc[5]], axis=2)
    go = jnp.concatenate([pc[11], pc[10], pc[9]], axis=2).transpose(0, 2, 1)
    sl = lax.dynamic_slice_in_dim(gsm[:, 0:7], slot * rw, rw, axis=2)
    dbq = gsm[:, 7, 384:576]
    dbv = jnp.concatenate([gsm[:, 7, 64:192], gsm[:, 7, 320:384]], axis=1)
    qv = lax.dynamic_slice_in_dim(jnp.stack([dbq, dbv], axis=1), slot * (rw // 4), rw // 4, axis=2)
    return (
        act[None],
        dx[None],
        jnp.stack([gq, gk, gv], axis=2),
        go,
        g1,
        g2.transpose(0, 2, 1),
        qv[:, :, None, :],
        sl[:, 6:7],
        sl[:, 0:4],
        sl[:, 4:6],
    )


def solution(mesh):
    both = ("dp", "seq")
    weights = (
        P(None, both, None, "tensor"),
        P(None, "tensor", both),
        P(None, both, "tensor"),
        P(None, "tensor", both),
        P(None, None, "tensor", both),
        P(None, "tensor", both),
        P(None, None, both),
        P(None, None, both),
    )
    tokens = P("dp", "seq", None)
    in_specs = (tokens, tokens, P("dp", None), P("dp", "tensor", None, None)) + weights
    out_specs = (tokens, tokens) + weights
    fn = functools.partial(shards, mesh.shape["dp"], mesh.shape["seq"], mesh.shape["tensor"])
    return jax.shard_map(fn, mesh=mesh, in_specs=in_specs, out_specs=out_specs, check_vma=False)
```
